32 devices in a mesh: row: 8 (over z, x), col: 4 (over y, core).
Axes of the slice: x: 2, y: 2, z: 4, core: 2. Of those that a mesh axis runs over, the one named last changes fastest.
Arguments:
- features: bfloat16 [512, 512, 128], P('row', 'col'), may hold values from -6 to 6
- kernels: bfloat16 [2, 3, 3, 128, 128], replicated, may hold values from -0.1875 to 0.1875
- length: int32 [1], replicated, may hold values from 256 to 512
- cotangent: bfloat16 [512, 512, 128], P('row', 'col'), may hold values from -6 to 6
Outputs:
- output_map: bfloat16 [512, 512, 128], P('row', 'col')
- feature_grad: bfloat16 [512, 512, 128], P('row', 'col')
- kernel_gradient: float32 [2, 3, 3, 128, 128], replicated
The draws below stay inside these ranges and needn't reach their ends.
Inputs may be any that keep to these rules, and one draw needn't show every extreme that they name: The protein occupies the first length rows and columns of the pair map.
All inputs are finite; a program needn't handle non-finite values.
Results may differ from the reference program's by a relative error of at most 0.0039.
Values may be sent and summed in bfloat16 or wider, within the bound.
No kernel may reach another device: no remote copies, remote signals or barrier semaphores. Data moves between devices by JAX's collectives and lax.ppermute only.
A program may use at most 192 MiB of HBM per device.

```python
import jax
import jax.numpy as jnp
from jax import lax

C = 128
FIRST_SPACING = 4
SECOND_SPACING = 8
N = 512


def block_levels(key, dims, cuts, low, largest):
    def one(position, blocks):
        heights = jax.random.uniform(jax.random.fold_in(jax.random.fold_in(key, 6), position), (blocks,), jnp.float32, low / len(cuts), largest / len(cuts))
        return jnp.repeat(jnp.exp(heights), dims[position] // blocks).reshape((-1,) + (1,) * (len(dims) - position - 1))

    gain = one(*cuts[0])
    for cut in cuts[1:]:
        gain = gain * one(*cut)
    return gain


def scatter_about(key, extent, scale, most, shards=(), kind=jnp.bfloat16):
    level = block_levels(key, extent, shards, -0.22, 0.18) if shards else 1.0
    drawn = jax.random.normal(key, extent, jnp.float32) * scale * level
    return jnp.minimum(jnp.maximum(drawn, -most), most).astype(kind)


def setup_inputs(seed: int = 0) -> dict:
    key_of = jax.random.split(jax.random.key(seed), 5)
    return {
        "features": scatter_about(key_of[0], (N, N, C), 1.0, 6.0, ((0, 8), (1, 4))),
        "kernels": scatter_about(key_of[1], (2, 3, 3, C, C), (9 * C) ** -0.5, 0.1875),
        "length": jax.random.randint(key_of[2], (1,), N // 2, N + 1).astype(jnp.int32),
        "cotangent": scatter_about(key_of[3], (N, N, C), 1.0, 6.0, ((0, 8), (1, 4))),
    }


def elu_value(values):
    return jnp.where(values > 0, values, jnp.expm1(jnp.minimum(values, 0.0)))


def elu_slope(values):
    return jnp.where(values > 0, 1.0, jnp.exp(jnp.minimum(values, 0.0)))


def spaced_kernel(inputs, kernel, dilation):
    result = lax.conv_general_dilated(inputs.astype(jnp.float32)[None], kernel.astype(jnp.float32), (1, 1), ((dilation, dilation), (dilation, dilation)), rhs_dilation=(dilation, dilation), dimension_numbers=("NHWC", "HWIO", "NHWC"), precision=lax.Precision.HIGHEST)
    return result[0]


def reversed_kernel(kernel):
    return kernel[::-1, ::-1].transpose(0, 1, 3, 2)


def kernel_contributions(acts, grads, dilation):
    padded = jnp.pad(acts.astype(jnp.float32), ((dilation, dilation), (dilation, dilation), (0, 0)))
    flat_grads = grads.astype(jnp.float32).reshape(-1, C)
    pieces = []
    for p in range(3):
        for q in range(3):
            window = padded[p * dilation:p * dilation + N, q * dilation:q * dilation + N].reshape(-1, C)
            pieces.append(lax.dot_general(window, flat_grads, (((0,), (0,)), ((), ())), precision=lax.Precision.HIGHEST, preferred_element_type=jnp.float32))
    return jnp.stack(pieces).reshape(3, 3, C, C)


def reference(features, kernels, length, cotangent):
    limit = length[0]
    inside = jnp.arange(N) < limit
    live = (inside[:, None] & inside[None, :]).astype(jnp.float32)[:, :, None]
    initial_state = features.astype(jnp.float32)
    first_activation = (live * elu_value(initial_state)).astype(jnp.bfloat16)
    first_state = initial_state + spaced_kernel(first_activation, kernels[0], FIRST_SPACING)
    second_activation = (live * elu_value(first_state)).astype(jnp.bfloat16)
    second_state = first_state + spaced_kernel(second_activation, kernels[1], SECOND_SPACING)
    output_map = (live * second_state).astype(jnp.bfloat16)
    second_gradient = (live * cotangent.astype(jnp.float32)).astype(jnp.bfloat16)
    second_backward = spaced_kernel(second_gradient, reversed_kernel(kernels[1]), SECOND_SPACING)
    grad_full = second_gradient.astype(jnp.float32) + live * elu_slope(first_state) * second_backward
    first_gradient = grad_full.astype(jnp.bfloat16)
    first_backward = spaced_kernel(first_gradient, reversed_kernel(kernels[0]), FIRST_SPACING)
    feature_grad = (grad_full + live * elu_slope(initial_state) * first_backward).astype(jnp.bfloat16)
    kernel_gradient = jnp.stack([kernel_contributions(first_activation, first_gradient, FIRST_SPACING), kernel_contributions(second_activation, second_gradient, SECOND_SPACING)])
    kernel_gradient = kernel_gradient / limit.astype(jnp.float32)
    return output_map, feature_grad, kernel_gradient
```

```python
import functools

import jax
import jax.numpy as jnp
from jax import lax
from jax.experimental import pallas as pl
from jax.experimental.pallas import tpu as pltpu
from jax.sharding import PartitionSpec as P

H = 3
C = 128
F32 = jnp.float32
BF16 = jnp.bfloat16
VMEM_LIMIT = 56 * 1024 * 1024
ANY = pl.BlockSpec(memory_space=pl.ANY)
VMEM = pl.BlockSpec(memory_space=pltpu.VMEM)
SMEM = pl.BlockSpec(memory_space=pltpu.SMEM)


def params():
    return pltpu.CompilerParams(vmem_limit_bytes=VMEM_LIMIT)


def cost(flops, nbytes):
    return pl.CostEstimate(flops=int(flops), bytes_accessed=int(nbytes), transcendentals=0)


def to_blocks(rows):
    cols = rows[0].shape[0]
    v = [r.reshape(cols // 8, 8, C) for r in rows]
    low = lax.broadcasted_iota(jnp.int32, v[0].shape, 1) < 4

    def swap(a, b):
        return jnp.where(low, a, pltpu.roll(b, 4, 1)), jnp.where(low, pltpu.roll(a, 4, 1), b)

    a, b = swap(v[0], v[1])
    c, d = swap(v[2], v[3])
    y = jnp.stack([jnp.concatenate([a, c], axis=1), jnp.concatenate([b, d], axis=1)], axis=1)
    return y.reshape(4 * cols, C)


def from_blocks(y):
    cols = y.shape[0] // 4
    y = y.reshape(cols // 8, 2, 2, 8, C)
    a, b, c, d = y[:, 0, 0], y[:, 1, 0], y[:, 0, 1], y[:, 1, 1]
    low = lax.broadcasted_iota(jnp.int32, a.shape, 1) < 4

    def swap(a, b):
        return jnp.where(low, a, pltpu.roll(b, 4, 1)), jnp.where(low, pltpu.roll(a, 4, 1), b)

    r0, r1 = swap(a, b)
    r2, r3 = swap(c, d)
    return [r.reshape(cols, C) for r in (r0, r1, r2, r3)]


def column_mask(meta, nj):
    shape = (nj + 2 * H, 16, C)
    j = lax.broadcasted_iota(jnp.int32, shape, 0)
    s = lax.broadcasted_iota(jnp.int32, shape, 1)
    col = meta[1] + 4 * (j - H) + (s & 3)
    return ((col >= 0) & (col < meta[2])).astype(F32).reshape(-1, C)


def live(meta, cm, a, start, size):
    s = lax.broadcasted_iota(jnp.int32, (1, 16, C), 1)
    row = meta[0] + 4 * a + (s >> 2)
    row_mask = ((row >= 0) & (row < meta[2])).astype(F32)
    return (cm[start : start + size, :].reshape(size // 16, 16, C) * row_mask).reshape(size, C)


def elu_parts(v):
    e = jnp.exp(jnp.minimum(v, 0.0))
    return jnp.maximum(v, 0.0) + (e - 1.0), e


def conv_pairs(read, pairs, d, weights):
    parts = []
    for a in pairs:
        cells = []
        for q in range(3):
            cells += [read(a, q), read(a + d, q), read(a - d, q), read(a + 2 * d, q)]
        parts.append(jnp.concatenate(cells, axis=1))
    left = jnp.concatenate(parts, axis=0) if len(parts) > 1 else parts[0]
    return jnp.dot(left, weights, preferred_element_type=F32)


def outer(left, right):
    return lax.dot_general(left, right, (((0,), (0,)), ((), ())), preferred_element_type=F32)


def pack_kernel(k_ref, w_ref):
    zero = jnp.zeros((C, C), BF16)
    for layer in range(2):
        for back in range(2):
            def tap(p, q):
                if back:
                    return k_ref[layer, 2 - p, 2 - q].T
                return k_ref[layer, p, q]

            n = 2 * layer + back
            for q in range(3):
                t0, t1, t2 = tap(0, q), tap(1, q), tap(2, q)
                o = 4 * C * q
                blocks = ((t1, t0), (t2, t1), (t0, zero), (zero, t2))
                for i, (x, y) in enumerate(blocks):
                    w_ref[n, o + C * i : o + C * (i + 1), :C] = x
                    w_ref[n, o + C * i : o + C * (i + 1), C:] = y


def layout_kernel(meta, f_ref, g_ref, fx_ref, gx_ref, left_ref, right_ref, *, step, nj):
    m0 = 16 * nj
    base = pl.program_id(0) * step
    s = lax.broadcasted_iota(jnp.int32, (nj, 16, C), 1)
    j = lax.broadcasted_iota(jnp.int32, (nj, 16, C), 0)
    cm = (meta[1] + 4 * j + (s & 3) < meta[2]).astype(F32)
    s1 = lax.broadcasted_iota(jnp.int32, (1, 16, C), 1)
    for k in range(step):
        fb = to_blocks([f_ref[4 * k + i].astype(F32) for i in range(4)]).astype(BF16)
        gb = to_blocks([g_ref[4 * k + i].astype(F32) for i in range(4)])
        rm = (meta[0] + 4 * (base + k) + (s1 >> 2) < meta[2]).astype(F32)
        gb = (gb.reshape(nj, 16, C) * (cm * rm)).reshape(m0, C).astype(BF16)
        for n, (v, x_ref) in enumerate(((fb, fx_ref), (gb, gx_ref))):
            x_ref[k, 16 * H : 16 * H + m0] = v
            left_ref[n, k] = v[: 16 * H]
            right_ref[n, k] = v[m0 - 16 * H :]


def assemble_kernel(fx_in, gx_in, lh, rh, fx, gx, ua, ub, da, db, sem, *, na, nj):
    del fx_in, gx_in
    m0 = 16 * nj
    jobs = []

    def go(src, dst):
        c = pltpu.make_async_copy(src, dst, sem.at[len(jobs)])
        c.start()
        jobs.append(c)

    for n, x in enumerate((fx, gx)):
        go(lh.at[n], x.at[:, pl.ds(0, 16 * H)])
        go(rh.at[n], x.at[:, pl.ds(16 * H + m0, 16 * H)])
    for c in jobs:
        c.wait()
    first = len(jobs)
    go(fx.at[pl.ds(0, 1)], ua.at[pl.ds(0, 1)])
    go(gx.at[pl.ds(0, 2)], ua.at[pl.ds(1, 2)])
    go(fx.at[pl.ds(1, 2)], ub.at[pl.ds(0, 2)])
    go(gx.at[pl.ds(2, 1)], ub.at[pl.ds(2, 1)])
    go(fx.at[pl.ds(na - 1, 1)], da.at[pl.ds(0, 1)])
    go(gx.at[pl.ds(na - 2, 2)], da.at[pl.ds(1, 2)])
    go(fx.at[pl.ds(na - 3, 2)], db.at[pl.ds(0, 2)])
    go(gx.at[pl.ds(na - 3, 1)], db.at[pl.ds(2, 1)])
    for c in jobs[first:]:
        c.wait()


def inner_kernel(meta, fx, gx, wp, a1o, a2o, so, g1o, gfo, acc_o, a1, a2, st, es, g1, gf, cm, sem, *, na, nj):
    m0, m1, m2, w = 16 * nj, 16 * (nj + 2), 16 * (nj + 4), 16 * (nj + 6)
    ni = na - 4
    cm[...] = column_mask(meta, nj)

    def activate(a, _):
        v, _e = elu_parts(fx[a].astype(F32))
        a1[a] = (v * live(meta, cm, a, 0, w)).astype(BF16)
        return 0

    lax.fori_loop(0, na, activate, 0)
    out_a1 = pltpu.make_async_copy(a1, a1o, sem.at[0])
    out_a1.start()

    def quad(t, _):
        r = 2 + 4 * t
        acc = conv_pairs(lambda row, q: a1[row, pl.ds(16 * q, m2), :], [r, r + 2], 1, wp[0])
        for k in range(2):
            for b in range(2):
                row = r + 2 * k + b
                v = fx[row, pl.ds(16, m2), :].astype(F32) + acc[k * m2 : (k + 1) * m2, b * C : (b + 1) * C]
                act, e = elu_parts(v)
                a2[row + 2] = (act * live(meta, cm, row, 16, m2)).astype(BF16)
                es[row - 2] = e[16 : 16 + m1]
                st[row - 2] = v[32 : 32 + m0]
        acc = conv_pairs(lambda row, q: gx[row, pl.ds(32 * q, m1), :], [r, r + 1], 2, wp[3])
        for k in range(2):
            for b in range(2):
                row = r + k + 2 * b
                back = acc[k * m1 : (k + 1) * m1, b * C : (b + 1) * C]
                full = gx[row, pl.ds(32, m1), :].astype(F32) + live(meta, cm, row, 32, m1) * es[row - 2] * back
                g1[row + 1] = full.astype(BF16)
                gf[row - 2] = full[16 : 16 + m0]
        return 0

    lax.fori_loop(0, ni // 4, quad, 0)
    copies = [
        pltpu.make_async_copy(a2.at[pl.ds(4, ni)], a2o.at[pl.ds(4, ni)], sem.at[1]),
        pltpu.make_async_copy(st, so.at[pl.ds(2, ni)], sem.at[2]),
        pltpu.make_async_copy(g1.at[pl.ds(3, ni)], g1o.at[pl.ds(3, ni)], sem.at[3]),
        pltpu.make_async_copy(gf, gfo.at[pl.ds(2, ni)], sem.at[4]),
    ]
    for c in copies:
        c.start()
    for i in (0, 1, 2, 3):
        a2[i] = jnp.zeros((m2, C), BF16)
        a2[na + i] = jnp.zeros((m2, C), BF16)
    for i in (0, 1, 2):
        g1[i] = jnp.zeros((m1, C), BF16)
        g1[na - 1 + i] = jnp.zeros((m1, C), BF16)

    def second(rows):
        left = [jnp.concatenate([a2[b + 2 + s, 32 : 32 + m0] for s in (2, 0, -2)], axis=1) for b in rows]
        right = [jnp.concatenate([gx[b, 16 + 32 * q : 16 + 32 * q + m0] for q in range(3)], axis=1) for b in rows]
        return outer(jnp.concatenate(left, axis=0), jnp.concatenate(right, axis=0))

    def first(rows):
        left = [jnp.concatenate([g1[b + 1 + s, 16 : 16 + m0] for s in (1, 0, -1)], axis=1) for b in rows]
        right = [jnp.concatenate([a1[b, 32 + 16 * q : 32 + 16 * q + m0] for q in range(3)], axis=1) for b in rows]
        return outer(jnp.concatenate(left, axis=0), jnp.concatenate(right, axis=0))

    half = na // 2
    acc_o[1] = second(range(half))
    acc_o[1] += second(range(half, na))
    acc_o[0] = first(range(1, half))
    acc_o[0] += first(range(half, na - 1))
    out_a1.wait()
    for c in copies:
        c.wait()


def edge_kernel(
    meta, fx, gx, a1i, up, dn, wp, acc_i, _a2, _s, _g1, _gf, a2o, so, g1o, gfo, kg,
    a1, g, f, fh, a2, st, es, g1, gf, cm, sem, *, na, nj,
):
    m0, m1, m2, w = 16 * nj, 16 * (nj + 2), 16 * (nj + 4), 16 * (nj + 6)
    jobs = []

    def go(src, dst):
        c = pltpu.make_async_copy(src, dst, sem.at[len(jobs)])
        c.start()
        jobs.append(c)

    go(up.at[pl.ds(0, 1)], fh.at[0])
    go(dn.at[pl.ds(0, 1)], fh.at[1])
    go(up.at[pl.ds(1, 2)], g.at[0, pl.ds(0, 2)])
    go(gx.at[pl.ds(0, 6)], g.at[0, pl.ds(2, 6)])
    go(gx.at[pl.ds(na - 6, 6)], g.at[1, pl.ds(0, 6)])
    go(dn.at[pl.ds(1, 2)], g.at[1, pl.ds(6, 2)])
    go(a1i.at[pl.ds(0, 3)], a1.at[0, pl.ds(1, 3)])
    go(a1i.at[pl.ds(na - 3, 3)], a1.at[1, pl.ds(0, 3)])
    go(fx.at[pl.ds(0, 2)], f.at[0])
    go(fx.at[pl.ds(na - 2, 2)], f.at[1])
    cm[...] = column_mask(meta, nj)
    for c in jobs:
        c.wait()
    for s, row, slot in ((0, -1, 0), (1, na, 3)):
        v, _e = elu_parts(fh[s, 0].astype(F32))
        a1[s, slot] = (v * live(meta, cm, row, 0, w)).astype(BF16)

    acc = conv_pairs(lambda i, q: a1[i // 8, i % 8, 16 * q : 16 * q + m2], [1, 9], 1, wp[0])
    for s in range(2):
        for b in range(2):
            row = (na - 2) * s + b
            v = f[s, b, 16 : 16 + m2].astype(F32) + acc[s * m2 : (s + 1) * m2, b * C : (b + 1) * C]
            act, e = elu_parts(v)
            a2[s, b] = (act * live(meta, cm, row, 16, m2)).astype(BF16)
            es[s, b] = e[16 : 16 + m1]
            st[s, b] = v[32 : 32 + m0]
    acc = conv_pairs(lambda i, q: g[i // 16, i % 16, 32 * q : 32 * q + m1], [2, 3, 18, 19], 2, wp[3])
    for s in range(2):
        for b in range(2):
            row = (na - 2) * s + b
            k = 2 * s + b
            back = acc[k * m1 : (k + 1) * m1, s * C : (s + 1) * C]
            full = g[s, 2 + 2 * s + b, 32 : 32 + m1].astype(F32) + live(meta, cm, row, 32, m1) * es[s, b] * back
            g1[s, b] = full.astype(BF16)
            gf[s, b] = full[16 : 16 + m0]
    outs = len(jobs)
    for s in range(2):
        go(a2.at[s], a2o.at[pl.ds(2 + (na - 2) * s, 2)])
        go(st.at[s], so.at[pl.ds((na - 2) * s, 2)])
        go(g1.at[s], g1o.at[pl.ds(1 + (na - 2) * s, 2)])
        go(gf.at[s], gfo.at[pl.ds((na - 2) * s, 2)])

    rows = [(s, b) for s in range(2) for b in range(2)]
    left = jnp.concatenate([a2[s, b, 32 : 32 + m0] for s, b in rows], axis=0)
    for p in range(3):
        right = [
            jnp.concatenate([g[s, 2 * s + b + 2 * p, 16 + 32 * q : 16 + 32 * q + m0] for q in range(3)], axis=1)
            for s, b in rows
        ]
        total = acc_i[1, C * p : C * (p + 1)] + outer(left, jnp.concatenate(right, axis=0))
        for q in range(3):
            kg[1, 2 - p, 2 - q] = total[:, C * q : C * (q + 1)].astype(BF16)
    left = jnp.concatenate([g1[s, b, 16 : 16 + m0] for s, b in rows], axis=0)
    for p in range(3):
        right = [
            jnp.concatenate([a1[s, b + p, 32 + 16 * q : 32 + 16 * q + m0] for q in range(3)], axis=1) for s, b in rows
        ]
        total = acc_i[0, C * p : C * (p + 1)] + outer(left, jnp.concatenate(right, axis=0))
        for q in range(3):
            kg[0, p, q] = total[:, C * q : C * (q + 1)].T.astype(BF16)
    for c in jobs[outs:]:
        c.wait()


def last_kernel(
    meta, fx, gx, a1i, upa, dna, upb, dnb, wp, a2i, si, g1i, gfi, out, fg,
    a1, g, f, fm, a2, st, es, g1, gf, cm, ot, ft, sem, osem, *, na, nj,
):
    m0, m1, m2, w = 16 * nj, 16 * (nj + 2), 16 * (nj + 4), 16 * (nj + 6)
    jobs = []

    def go(src, dst):
        c = pltpu.make_async_copy(src, dst, sem.at[len(jobs)])
        c.start()
        jobs.append(c)

    go(upb.at[pl.ds(0, 2)], f.at[0, pl.ds(0, 2)])
    go(upa.at[pl.ds(0, 1)], f.at[0, pl.ds(2, 1)])
    go(dna.at[pl.ds(0, 1)], f.at[1, pl.ds(0, 1)])
    go(dnb.at[pl.ds(0, 2)], f.at[1, pl.ds(1, 2)])
    go(upb.at[pl.ds(2, 1)], g.at[0, pl.ds(0, 1)])
    go(upa.at[pl.ds(2, 1)], g.at[0, pl.ds(1, 1)])
    go(gx.at[pl.ds(1, 1)], g.at[0, pl.ds(2, 1)])
    go(gx.at[pl.ds(3, 1)], g.at[0, pl.ds(3, 1)])
    go(gx.at[pl.ds(na - 4, 1)], g.at[1, pl.ds(0, 1)])
    go(gx.at[pl.ds(na - 2, 1)], g.at[1, pl.ds(1, 1)])
    go(dna.at[pl.ds(1, 1)], g.at[1, pl.ds(2, 1)])
    go(dnb.at[pl.ds(2, 1)], g.at[1, pl.ds(3, 1)])
    go(a1i.at[pl.ds(0, 1)], a1.at[0, pl.ds(3, 1)])
    go(a1i.at[pl.ds(na - 1, 1)], a1.at[1, pl.ds(0, 1)])
    early = len(jobs)
    go(a2i.at[pl.ds(2, na)], a2.at[pl.ds(2, na)])
    go(si, st)
    go(g1i.at[pl.ds(1, na)], g1.at[pl.ds(1, na)])
    go(fx.at[:, pl.ds(16 * H, m0)], fm)
    go(gfi, gf)
    cm[...] = column_mask(meta, nj)
    for c in jobs[:early]:
        c.wait()
    for s in range(2):
        for i in range(3):
            row = i - 3 if s == 0 else na + i
            v, _e = elu_parts(f[s, i].astype(F32))
            a1[s, i + s] = (v * live(meta, cm, row, 0, w)).astype(BF16)
    acc = conv_pairs(lambda i, q: a1[i // 8, i % 8, 16 * q : 16 * q + m2], [1, 9], 1, wp[0])
    for s in range(2):
        for b in range(2):
            row = b - 2 if s == 0 else na + b
            v = f[s, 1 - s + b, 16 : 16 + m2].astype(F32) + acc[s * m2 : (s + 1) * m2, b * C : (b + 1) * C]
            act, e = elu_parts(v)
            a2[row + 2] = (act * live(meta, cm, row, 16, m2)).astype(BF16)
            if b != s:
                es[s] = e[16 : 16 + m1]
    acc = conv_pairs(lambda i, q: g[i // 8, i % 8, 32 * q : 32 * q + m1], [1, 9], 1, wp[3])
    for s in range(2):
        row = -1 if s == 0 else na
        back = acc[s * m1 : (s + 1) * m1, s * C : (s + 1) * C]
        full = g[s, 1 + s, 32 : 32 + m1].astype(F32) + live(meta, cm, row, 32, m1) * es[s] * back
        g1[row + 1] = full.astype(BF16)
    for c in jobs[early:]:
        c.wait()

    def quad(t, _):
        r = 4 * t
        acc = conv_pairs(lambda row, q: a2[row + 2, pl.ds(32 * q, m0), :], [r, r + 1], 2, wp[2])
        for k in range(2):
            for b in range(2):
                row = r + k + 2 * b
                v = (st[row] + acc[k * m0 : (k + 1) * m0, b * C : (b + 1) * C]) * live(meta, cm, row, 16 * H, m0)
                for i, x in enumerate(from_blocks(v)):
                    ot[4 * row + i] = x.astype(BF16)
        acc = conv_pairs(lambda row, q: g1[row + 1, pl.ds(16 * q, m0), :], [r, r + 2], 1, wp[1])
        for k in range(2):
            for b in range(2):
                row = r + 2 * k + b
                slope = jnp.exp(jnp.minimum(fm[row].astype(F32), 0.0))
                back = acc[k * m0 : (k + 1) * m0, b * C : (b + 1) * C]
                v = gf[row] + live(meta, cm, row, 16 * H, m0) * slope * back
                for i, x in enumerate(from_blocks(v)):
                    ft[4 * row + i] = x.astype(BF16)
        pltpu.make_async_copy(ot.at[pl.ds(16 * t, 16)], out.at[pl.ds(16 * t, 16)], osem.at[0]).start()
        pltpu.make_async_copy(ft.at[pl.ds(16 * t, 16)], fg.at[pl.ds(16 * t, 16)], osem.at[1]).start()
        return 0

    lax.fori_loop(0, na // 4, quad, 0)
    pltpu.make_async_copy(ot, out, osem.at[0]).wait()
    pltpu.make_async_copy(ft, fg, osem.at[1]).wait()


def sum_kernel(meta, x_ref, o_ref):
    total = jnp.sum(x_ref[...].astype(F32), axis=0) / meta[2].astype(F32)
    o_ref[...] = jnp.broadcast_to(total.astype(BF16)[None], o_ref.shape)


def shift(x, axis, step):
    n = lax.axis_size(axis)
    return lax.ppermute(x, axis, [(i, i + step) for i in range(n) if 0 <= i + step < n])


def body(features, kernels, length, cotangent):
    rows, cols, _ = features.shape
    na, nj = rows // 4, cols // 4
    m0, m1, m2, w = 16 * nj, 16 * (nj + 2), 16 * (nj + 4), 16 * (nj + 6)
    ni = na - 4
    meta = jnp.stack([lax.axis_index("row") * rows, lax.axis_index("col") * cols, length[0]]).astype(jnp.int32)
    sds = jax.ShapeDtypeStruct

    step = 4
    fx, gx, to_left, to_right = pl.pallas_call(
        functools.partial(layout_kernel, step=step, nj=nj),
        grid=(na // step,),
        in_specs=[SMEM] + [pl.BlockSpec((4 * step, cols, C), lambda i: (i, 0, 0))] * 2,
        out_specs=[pl.BlockSpec((step, w, C), lambda i: (i, 0, 0))] * 2
        + [pl.BlockSpec((2, step, 16 * H, C), lambda i: (0, i, 0, 0))] * 2,
        out_shape=[sds((na, w, C), BF16)] * 2 + [sds((2, na, 16 * H, C), BF16)] * 2,
        compiler_params=params(),
        cost_estimate=cost(0, 16 << 20),
    )(meta, features, cotangent)
    rh = shift(to_left, "col", -1)
    lh = shift(to_right, "col", 1)
    wp = pl.pallas_call(
        pack_kernel,
        in_specs=[VMEM],
        out_specs=VMEM,
        out_shape=sds((4, 12 * C, 2 * C), BF16),
        compiler_params=params(),
        cost_estimate=cost(0, 8 << 20),
    )(kernels)
    fx, gx, ua, ub, da, db = pl.pallas_call(
        functools.partial(assemble_kernel, na=na, nj=nj),
        in_specs=[ANY] * 4,
        out_specs=[ANY] * 6,
        out_shape=[sds((na, w, C), BF16)] * 2 + [sds((3, w, C), BF16)] * 4,
        scratch_shapes=[pltpu.SemaphoreType.DMA((12,))],
        input_output_aliases={0: 0, 1: 1},
        compiler_params=params(),
        cost_estimate=cost(0, 4 << 20),
    )(fx, gx, lh, rh)
    dna = shift(ua, "row", -1)
    upa = shift(da, "row", 1)
    dnb = shift(ub, "row", -1)
    upb = shift(db, "row", 1)

    conv_flops = 2 * rows * cols * 9 * C * C
    a1, a2, st, g1, gf, acc = pl.pallas_call(
        functools.partial(inner_kernel, na=na, nj=nj),
        in_specs=[SMEM] + [VMEM] * 3,
        out_specs=[ANY] * 5 + [VMEM],
        out_shape=[
            sds((na, w, C), BF16),
            sds((na + 4, m2, C), BF16),
            sds((na, m0, C), F32),
            sds((na + 2, m1, C), BF16),
            sds((na, m0, C), F32),
            sds((2, 3 * C, 3 * C), F32),
        ],
        scratch_shapes=[
            pltpu.VMEM((na, w, C), BF16),
            pltpu.VMEM((na + 4, m2, C), BF16),
            pltpu.VMEM((ni, m0, C), F32),
            pltpu.VMEM((ni, m1, C), F32),
            pltpu.VMEM((na + 2, m1, C), BF16),
            pltpu.VMEM((ni, m0, C), F32),
            pltpu.VMEM((w, C), F32),
            pltpu.SemaphoreType.DMA((5,)),
        ],
        compiler_params=params(),
        cost_estimate=cost(4 * conv_flops, 24 << 20),
    )(meta, fx, gx, wp)

    a2, st, g1, gf, kg = pl.pallas_call(
        functools.partial(edge_kernel, na=na, nj=nj),
        in_specs=[SMEM] + [ANY] * 5 + [VMEM] * 2 + [ANY] * 4,
        out_specs=[ANY] * 4 + [VMEM],
        out_shape=[
            sds((na + 4, m2, C), BF16),
            sds((na, m0, C), F32),
            sds((na + 2, m1, C), BF16),
            sds((na, m0, C), F32),
            sds((2, 3, 3, C, C), BF16),
        ],
        scratch_shapes=[
            pltpu.VMEM((2, 4, w, C), BF16),
            pltpu.VMEM((2, 8, w, C), BF16),
            pltpu.VMEM((2, 2, w, C), BF16),
            pltpu.VMEM((2, 1, w, C), BF16),
            pltpu.VMEM((2, 2, m2, C), BF16),
            pltpu.VMEM((2, 2, m0, C), F32),
            pltpu.VMEM((2, 2, m1, C), F32),
            pltpu.VMEM((2, 2, m1, C), BF16),
            pltpu.VMEM((2, 2, m0, C), F32),
            pltpu.VMEM((w, C), F32),
            pltpu.SemaphoreType.DMA((18,)),
        ],
        input_output_aliases={8: 0, 9: 1, 10: 2, 11: 3},
        compiler_params=params(),
        cost_estimate=cost(conv_flops, 12 << 20),
    )(meta, fx, gx, a1, upa, dna, wp, acc, a2, st, g1, gf)

    axes = ("row", "col")
    parts = lax.axis_size(axes)
    shares = lax.all_to_all(kg.reshape(parts, -1, C), axes, 0, 0, tiled=True)
    spread = pl.pallas_call(
        sum_kernel,
        in_specs=[SMEM, VMEM],
        out_specs=VMEM,
        out_shape=sds(shares.shape, BF16),
        compiler_params=params(),
        cost_estimate=cost(0, 2 << 20),
    )(meta, shares)
    whole = lax.all_to_all(spread, axes, 0, 0, tiled=True)
    kernel_gradient = whole.reshape(kernels.shape).astype(F32)

    out, fg = pl.pallas_call(
        functools.partial(last_kernel, na=na, nj=nj),
        in_specs=[SMEM] + [ANY] * 7 + [VMEM] + [ANY] * 4,
        out_specs=[ANY] * 2,
        out_shape=[sds(features.shape, BF16)] * 2,
        scratch_shapes=[
            pltpu.VMEM((2, 4, w, C), BF16),
            pltpu.VMEM((2, 4, w, C), BF16),
            pltpu.VMEM((2, 3, w, C), BF16),
            pltpu.VMEM((na, m0, C), BF16),
            pltpu.VMEM((na + 4, m2, C), BF16),
            pltpu.VMEM((na, m0, C), F32),
            pltpu.VMEM((2, m1, C), F32),
            pltpu.VMEM((na + 2, m1, C), BF16),
            pltpu.VMEM((na, m0, C), F32),
            pltpu.VMEM((w, C), F32),
            pltpu.VMEM(features.shape, BF16),
            pltpu.VMEM(features.shape, BF16),
            pltpu.SemaphoreType.DMA((19,)),
            pltpu.SemaphoreType.DMA((2,)),
        ],
        compiler_params=params(),
        cost_estimate=cost(2 * conv_flops, 24 << 20),
    )(meta, fx, gx, a1, upa, dna, upb, dnb, wp, a2, st, g1, gf)
    return out, fg, kernel_gradient


def solution(mesh):
    spec = P("row", "col", None)
    return jax.shard_map(
        body, mesh=mesh, in_specs=(spec, P(), P(), spec), out_specs=(spec, spec, P()), check_vma=False
    )
```

```python
import functools

import jax
import jax.numpy as jnp
from jax import lax
from jax.experimental import pallas as pl
from jax.experimental.pallas import tpu as pltpu
from jax.sharding import PartitionSpec as P

H = 3
C = 128
F32 = jnp.float32
BF16 = jnp.bfloat16
VMEM_LIMIT = 56 * 1024 * 1024
ANY = pl.BlockSpec(memory_space=pl.ANY)
VMEM = pl.BlockSpec(memory_space=pltpu.VMEM)
SMEM = pl.BlockSpec(memory_space=pltpu.SMEM)


def params():
    return pltpu.CompilerParams(vmem_limit_bytes=VMEM_LIMIT)


def cost(flops, nbytes):
    return pl.CostEstimate(flops=int(flops), bytes_accessed=int(nbytes), transcendentals=0)


def to_blocks(rows):
    cols = rows[0].shape[0]
    v = [r.reshape(cols // 8, 8, C) for r in rows]
    low = lax.broadcasted_iota(jnp.int32, v[0].shape, 1) < 4

    def swap(a, b):
        return jnp.where(low, a, pltpu.roll(b, 4, 1)), jnp.where(low, pltpu.roll(a, 4, 1), b)

    a, b = swap(v[0], v[1])
    c, d = swap(v[2], v[3])
    y = jnp.stack([jnp.concatenate([a, c], axis=1), jnp.concatenate([b, d], axis=1)], axis=1)
    return y.reshape(4 * cols, C)


def from_blocks(y):
    cols = y.shape[0] // 4
    y = y.reshape(cols // 8, 2, 2, 8, C)
    a, b, c, d = y[:, 0, 0], y[:, 1, 0], y[:, 0, 1], y[:, 1, 1]
    low = lax.broadcasted_iota(jnp.int32, a.shape, 1) < 4

    def swap(a, b):
        return jnp.where(low, a, pltpu.roll(b, 4, 1)), jnp.where(low, pltpu.roll(a, 4, 1), b)

    r0, r1 = swap(a, b)
    r2, r3 = swap(c, d)
    return [r.reshape(cols, C) for r in (r0, r1, r2, r3)]


def column_mask(meta, nj):
    shape = (nj + 2 * H, 16, C)
    j = lax.broadcasted_iota(jnp.int32, shape, 0)
    s = lax.broadcasted_iota(jnp.int32, shape, 1)
    col = meta[1] + 4 * (j - H) + (s & 3)
    return ((col >= 0) & (col < meta[2])).astype(F32).reshape(-1, C)


def live(meta, cm, a, start, size):
    s = lax.broadcasted_iota(jnp.int32, (1, 16, C), 1)
    row = meta[0] + 4 * a + (s >> 2)
    row_mask = ((row >= 0) & (row < meta[2])).astype(F32)
    return (cm[start : start + size, :].reshape(size // 16, 16, C) * row_mask).reshape(size, C)


def elu_parts(v):
    e = jnp.exp(jnp.minimum(v, 0.0))
    return jnp.maximum(v, 0.0) + (e - 1.0), e


def conv_pairs(read, pairs, d, weights):
    parts = []
    for a in pairs:
        cells = []
        for q in range(3):
            cells += [read(a, q), read(a + d, q), read(a - d, q), read(a + 2 * d, q)]
        parts.append(jnp.concatenate(cells, axis=1))
    left = jnp.concatenate(parts, axis=0) if len(parts) > 1 else parts[0]
    return jnp.dot(left, weights, preferred_element_type=F32)


def outer(left, right):
    return lax.dot_general(left, right, (((0,), (0,)), ((), ())), preferred_element_type=F32)


def pack_kernel(k_ref, w_ref):
    zero = jnp.zeros((C, C), BF16)
    for layer in range(2):
        for back in range(2):
            def tap(p, q):
                if back:
                    return k_ref[layer, 2 - p, 2 - q].T
                return k_ref[layer, p, q]

            n = 2 * layer + back
            for q in range(3):
                t0, t1, t2 = tap(0, q), tap(1, q), tap(2, q)
                o = 4 * C * q
                blocks = ((t1, t0), (t2, t1), (t0, zero), (zero, t2))
                for i, (x, y) in enumerate(blocks):
                    w_ref[n, o + C * i : o + C * (i + 1), :C] = x
                    w_ref[n, o + C * i : o + C * (i + 1), C:] = y


def layout_kernel(meta, f_ref, g_ref, fx_ref, gx_ref, left_ref, right_ref, *, step, nj):
    m0 = 16 * nj
    base = pl.program_id(0) * step
    s = lax.broadcasted_iota(jnp.int32, (nj, 16, C), 1)
    j = lax.broadcasted_iota(jnp.int32, (nj, 16, C), 0)
    cm = (meta[1] + 4 * j + (s & 3) < meta[2]).astype(F32)
    s1 = lax.broadcasted_iota(jnp.int32, (1, 16, C), 1)
    for k in range(step):
        fb = to_blocks([f_ref[4 * k + i].astype(F32) for i in range(4)]).astype(BF16)
        gb = to_blocks([g_ref[4 * k + i].astype(F32) for i in range(4)])
        rm = (meta[0] + 4 * (base + k) + (s1 >> 2) < meta[2]).astype(F32)
        gb = (gb.reshape(nj, 16, C) * (cm * rm)).reshape(m0, C).astype(BF16)
        for n, (v, x_ref) in enumerate(((fb, fx_ref), (gb, gx_ref))):
            x_ref[k] = v
            left_ref[n, k] = v[: 16 * H]
            right_ref[n, k] = v[m0 - 16 * H :]


def gather_rows(go, own, lh, rh, n, row, count, dst, m0):
    go(own.at[pl.ds(row, count)], dst.at[:, pl.ds(16 * H, m0)])
    go(lh.at[n, pl.ds(row, count)], dst.at[:, pl.ds(0, 16 * H)])
    go(rh.at[n, pl.ds(row, count)], dst.at[:, pl.ds(16 * H + m0, 16 * H)])


def copier(sem, jobs):
    def go(src, dst):
        c = pltpu.make_async_copy(src, dst, sem.at[len(jobs)])
        c.start()
        jobs.append(c)

    return go


def assemble_kernel(fo, xo, lh, rh, ua, ub, da, db, buf, sem, *, na, nj):
    m0 = 16 * nj
    jobs = []
    go = copier(sem, jobs)
    gather_rows(go, fo, lh, rh, 0, 0, 1, buf.at[0, pl.ds(0, 1)], m0)
    gather_rows(go, xo, lh, rh, 1, 0, 2, buf.at[0, pl.ds(1, 2)], m0)
    gather_rows(go, fo, lh, rh, 0, na - 1, 1, buf.at[1, pl.ds(0, 1)], m0)
    gather_rows(go, xo, lh, rh, 1, na - 2, 2, buf.at[1, pl.ds(1, 2)], m0)
    gather_rows(go, fo, lh, rh, 0, 1, 2, buf.at[2, pl.ds(0, 2)], m0)
    gather_rows(go, xo, lh, rh, 1, 2, 1, buf.at[2, pl.ds(2, 1)], m0)
    gather_rows(go, fo, lh, rh, 0, na - 3, 2, buf.at[3, pl.ds(0, 2)], m0)
    gather_rows(go, xo, lh, rh, 1, na - 3, 1, buf.at[3, pl.ds(2, 1)], m0)
    first = len(jobs)
    for i, out in enumerate((ua, da, ub, db)):
        for c in jobs[6 * i : 6 * i + 6]:
            c.wait()
        go(buf.at[i], out)
    for c in jobs[first:]:
        c.wait()


def inner_kernel(
    meta, fo, xo, lh, rh, wp, a1o, a2o, so, g1o, gfo, acc_o,
    fx, gx, a1, a2, st, es, g1, gf, cm, sem, insem, *, na, nj,
):
    m0, m1, m2, w = 16 * nj, 16 * (nj + 2), 16 * (nj + 4), 16 * (nj + 6)
    ni = na - 4
    jobs = []
    go = copier(insem, jobs)
    gather_rows(go, fo, lh, rh, 0, 0, na, fx, m0)
    gather_rows(go, xo, lh, rh, 1, 0, na, gx, m0)
    cm[...] = column_mask(meta, nj)
    for c in jobs[:3]:
        c.wait()

    def activate(a, _):
        v, _e = elu_parts(fx[a].astype(F32))
        a1[a] = (v * live(meta, cm, a, 0, w)).astype(BF16)
        return 0

    lax.fori_loop(0, na, activate, 0)
    out_a1 = pltpu.make_async_copy(a1, a1o, sem.at[0])
    out_a1.start()
    for c in jobs[3:]:
        c.wait()

    def quad(t, _):
        r = 2 + 4 * t
        acc = conv_pairs(lambda row, q: a1[row, pl.ds(16 * q, m2), :], [r, r + 2], 1, wp[0])
        for k in range(2):
            for b in range(2):
                row = r + 2 * k + b
                v = fx[row, pl.ds(16, m2), :].astype(F32) + acc[k * m2 : (k + 1) * m2, b * C : (b + 1) * C]
                act, e = elu_parts(v)
                a2[row + 2] = (act * live(meta, cm, row, 16, m2)).astype(BF16)
                es[row - 2] = e[16 : 16 + m1]
                st[row - 2] = v[32 : 32 + m0]
        acc = conv_pairs(lambda row, q: gx[row, pl.ds(32 * q, m1), :], [r, r + 1], 2, wp[3])
        for k in range(2):
            for b in range(2):
                row = r + k + 2 * b
                back = acc[k * m1 : (k + 1) * m1, b * C : (b + 1) * C]
                full = gx[row, pl.ds(32, m1), :].astype(F32) + live(meta, cm, row, 32, m1) * es[row - 2] * back
                g1[row + 1] = full.astype(BF16)
                gf[row - 2] = full[16 : 16 + m0]
        return 0

    lax.fori_loop(0, ni // 4, quad, 0)
    copies = [
        pltpu.make_async_copy(a2.at[pl.ds(4, ni)], a2o.at[pl.ds(4, ni)], sem.at[1]),
        pltpu.make_async_copy(st, so.at[pl.ds(2, ni)], sem.at[2]),
        pltpu.make_async_copy(g1.at[pl.ds(3, ni)], g1o.at[pl.ds(3, ni)], sem.at[3]),
        pltpu.make_async_copy(gf, gfo.at[pl.ds(2, ni)], sem.at[4]),
    ]
    for c in copies:
        c.start()
    for i in (0, 1, 2, 3):
        a2[i] = jnp.zeros((m2, C), BF16)
        a2[na + i] = jnp.zeros((m2, C), BF16)
    for i in (0, 1, 2):
        g1[i] = jnp.zeros((m1, C), BF16)
        g1[na - 1 + i] = jnp.zeros((m1, C), BF16)

    def second(rows):
        left = [jnp.concatenate([a2[b + 2 + s, 32 : 32 + m0] for s in (2, 0, -2)], axis=1) for b in rows]
        right = [jnp.concatenate([gx[b, 16 + 32 * q : 16 + 32 * q + m0] for q in range(3)], axis=1) for b in rows]
        return outer(jnp.concatenate(left, axis=0), jnp.concatenate(right, axis=0))

    def first(rows):
        left = [jnp.concatenate([g1[b + 1 + s, 16 : 16 + m0] for s in (1, 0, -1)], axis=1) for b in rows]
        right = [jnp.concatenate([a1[b, 32 + 16 * q : 32 + 16 * q + m0] for q in range(3)], axis=1) for b in rows]
        return outer(jnp.concatenate(left, axis=0), jnp.concatenate(right, axis=0))

    half = na // 2
    acc_o[1] = second(range(half))
    acc_o[1] += second(range(half, na))
    acc_o[0] = first(range(1, half))
    acc_o[0] += first(range(half, na - 1))
    out_a1.wait()
    for c in copies:
        c.wait()


def edge_kernel(
    meta, fo, xo, lh, rh, a1i, up, dn, wp, acc_i, _a2, _s, _g1, _gf, a2o, so, g1o, gfo, kg,
    a1, g, f, fh, a2, st, es, g1, gf, cm, sem, *, na, nj,
):
    m0, m1, m2, w = 16 * nj, 16 * (nj + 2), 16 * (nj + 4), 16 * (nj + 6)
    jobs = []

    go = copier(sem, jobs)
    go(up.at[pl.ds(0, 1)], fh.at[0])
    go(dn.at[pl.ds(0, 1)], fh.at[1])
    go(up.at[pl.ds(1, 2)], g.at[0, pl.ds(0, 2)])
    gather_rows(go, xo, lh, rh, 1, 0, 6, g.at[0, pl.ds(2, 6)], m0)
    gather_rows(go, xo, lh, rh, 1, na - 6, 6, g.at[1, pl.ds(0, 6)], m0)
    go(dn.at[pl.ds(1, 2)], g.at[1, pl.ds(6, 2)])
    go(a1i.at[pl.ds(0, 3)], a1.at[0, pl.ds(1, 3)])
    go(a1i.at[pl.ds(na - 3, 3)], a1.at[1, pl.ds(0, 3)])
    gather_rows(go, fo, lh, rh, 0, 0, 2, f.at[0], m0)
    gather_rows(go, fo, lh, rh, 0, na - 2, 2, f.at[1], m0)
    cm[...] = column_mask(meta, nj)
    for c in jobs:
        c.wait()
    for s, row, slot in ((0, -1, 0), (1, na, 3)):
        v, _e = elu_parts(fh[s, 0].astype(F32))
        a1[s, slot] = (v * live(meta, cm, row, 0, w)).astype(BF16)

    acc = conv_pairs(lambda i, q: a1[i // 8, i % 8, 16 * q : 16 * q + m2], [1, 9], 1, wp[0])
    for s in range(2):
        for b in range(2):
            row = (na - 2) * s + b
            v = f[s, b, 16 : 16 + m2].astype(F32) + acc[s * m2 : (s + 1) * m2, b * C : (b + 1) * C]
            act, e = elu_parts(v)
            a2[s, b] = (act * live(meta, cm, row, 16, m2)).astype(BF16)
            es[s, b] = e[16 : 16 + m1]
            st[s, b] = v[32 : 32 + m0]
    acc = conv_pairs(lambda i, q: g[i // 16, i % 16, 32 * q : 32 * q + m1], [2, 3, 18, 19], 2, wp[3])
    for s in range(2):
        for b in range(2):
            row = (na - 2) * s + b
            k = 2 * s + b
            back = acc[k * m1 : (k + 1) * m1, s * C : (s + 1) * C]
            full = g[s, 2 + 2 * s + b, 32 : 32 + m1].astype(F32) + live(meta, cm, row, 32, m1) * es[s, b] * back
            g1[s, b] = full.astype(BF16)
            gf[s, b] = full[16 : 16 + m0]
    outs = len(jobs)
    for s in range(2):
        go(a2.at[s], a2o.at[pl.ds(2 + (na - 2) * s, 2)])
        go(st.at[s], so.at[pl.ds((na - 2) * s, 2)])
        go(g1.at[s], g1o.at[pl.ds(1 + (na - 2) * s, 2)])
        go(gf.at[s], gfo.at[pl.ds((na - 2) * s, 2)])

    rows = [(s, b) for s in range(2) for b in range(2)]
    left = jnp.concatenate([a2[s, b, 32 : 32 + m0] for s, b in rows], axis=0)
    for p in range(3):
        right = [
            jnp.concatenate([g[s, 2 * s + b + 2 * p, 16 + 32 * q : 16 + 32 * q + m0] for q in range(3)], axis=1)
            for s, b in rows
        ]
        total = acc_i[1, C * p : C * (p + 1)] + outer(left, jnp.concatenate(right, axis=0))
        for q in range(3):
            kg[1, 2 - p, 2 - q] = total[:, C * q : C * (q + 1)].astype(BF16)
    left = jnp.concatenate([g1[s, b, 16 : 16 + m0] for s, b in rows], axis=0)
    for p in range(3):
        right = [
            jnp.concatenate([a1[s, b + p, 32 + 16 * q : 32 + 16 * q + m0] for q in range(3)], axis=1) for s, b in rows
        ]
        total = acc_i[0, C * p : C * (p + 1)] + outer(left, jnp.concatenate(right, axis=0))
        for q in range(3):
            kg[0, p, q] = total[:, C * q : C * (q + 1)].T.astype(BF16)
    for c in jobs[outs:]:
        c.wait()


def last_kernel(
    meta, fo, xo, lh, rh, a1i, upa, dna, upb, dnb, wp, a2i, si, g1i, gfi, out, fg,
    a1, g, f, fm, a2, st, es, g1, gf, cm, ot, ft, sem, osem, *, na, nj,
):
    m0, m1, m2, w = 16 * nj, 16 * (nj + 2), 16 * (nj + 4), 16 * (nj + 6)
    jobs = []

    go = copier(sem, jobs)
    go(upb.at[pl.ds(0, 2)], f.at[0, pl.ds(0, 2)])
    go(upa.at[pl.ds(0, 1)], f.at[0, pl.ds(2, 1)])
    go(dna.at[pl.ds(0, 1)], f.at[1, pl.ds(0, 1)])
    go(dnb.at[pl.ds(0, 2)], f.at[1, pl.ds(1, 2)])
    go(upb.at[pl.ds(2, 1)], g.at[0, pl.ds(0, 1)])
    go(upa.at[pl.ds(2, 1)], g.at[0, pl.ds(1, 1)])
    gather_rows(go, xo, lh, rh, 1, 1, 1, g.at[0, pl.ds(2, 1)], m0)
    gather_rows(go, xo, lh, rh, 1, 3, 1, g.at[0, pl.ds(3, 1)], m0)
    gather_rows(go, xo, lh, rh, 1, na - 4, 1, g.at[1, pl.ds(0, 1)], m0)
    gather_rows(go, xo, lh, rh, 1, na - 2, 1, g.at[1, pl.ds(1, 1)], m0)
    go(dna.at[pl.ds(1, 1)], g.at[1, pl.ds(2, 1)])
    go(dnb.at[pl.ds(2, 1)], g.at[1, pl.ds(3, 1)])
    go(a1i.at[pl.ds(0, 1)], a1.at[0, pl.ds(3, 1)])
    go(a1i.at[pl.ds(na - 1, 1)], a1.at[1, pl.ds(0, 1)])
    early = len(jobs)
    go(a2i.at[pl.ds(2, na)], a2.at[pl.ds(2, na)])
    go(si, st)
    go(g1i.at[pl.ds(1, na)], g1.at[pl.ds(1, na)])
    go(fo, fm)
    go(gfi, gf)
    cm[...] = column_mask(meta, nj)
    for c in jobs[:early]:
        c.wait()
    for s in range(2):
        for i in range(3):
            row = i - 3 if s == 0 else na + i
            v, _e = elu_parts(f[s, i].astype(F32))
            a1[s, i + s] = (v * live(meta, cm, row, 0, w)).astype(BF16)
    acc = conv_pairs(lambda i, q: a1[i // 8, i % 8, 16 * q : 16 * q + m2], [1, 9], 1, wp[0])
    for s in range(2):
        for b in range(2):
            row = b - 2 if s == 0 else na + b
            v = f[s, 1 - s + b, 16 : 16 + m2].astype(F32) + acc[s * m2 : (s + 1) * m2, b * C : (b + 1) * C]
            act, e = elu_parts(v)
            a2[row + 2] = (act * live(meta, cm, row, 16, m2)).astype(BF16)
            if b != s:
                es[s] = e[16 : 16 + m1]
    acc = conv_pairs(lambda i, q: g[i // 8, i % 8, 32 * q : 32 * q + m1], [1, 9], 1, wp[3])
    for s in range(2):
        row = -1 if s == 0 else na
        back = acc[s * m1 : (s + 1) * m1, s * C : (s + 1) * C]
        full = g[s, 1 + s, 32 : 32 + m1].astype(F32) + live(meta, cm, row, 32, m1) * es[s] * back
        g1[row + 1] = full.astype(BF16)
    for c in jobs[early:]:
        c.wait()

    def quad(t, _):
        r = 4 * t
        acc = conv_pairs(lambda row, q: a2[row + 2, pl.ds(32 * q, m0), :], [r, r + 1], 2, wp[2])
        for k in range(2):
            for b in range(2):
                row = r + k + 2 * b
                v = (st[row] + acc[k * m0 : (k + 1) * m0, b * C : (b + 1) * C]) * live(meta, cm, row, 16 * H, m0)
                for i, x in enumerate(from_blocks(v)):
                    ot[4 * row + i] = x.astype(BF16)
        acc = conv_pairs(lambda row, q: g1[row + 1, pl.ds(16 * q, m0), :], [r, r + 2], 1, wp[1])
        for k in range(2):
            for b in range(2):
                row = r + 2 * k + b
                slope = jnp.exp(jnp.minimum(fm[row].astype(F32), 0.0))
                back = acc[k * m0 : (k + 1) * m0, b * C : (b + 1) * C]
                v = gf[row] + live(meta, cm, row, 16 * H, m0) * slope * back
                for i, x in enumerate(from_blocks(v)):
                    ft[4 * row + i] = x.astype(BF16)
        pltpu.make_async_copy(ot.at[pl.ds(16 * t, 16)], out.at[pl.ds(16 * t, 16)], osem.at[0]).start()
        pltpu.make_async_copy(ft.at[pl.ds(16 * t, 16)], fg.at[pl.ds(16 * t, 16)], osem.at[1]).start()
        return 0

    lax.fori_loop(0, na // 4, quad, 0)
    pltpu.make_async_copy(ot, out, osem.at[0]).wait()
    pltpu.make_async_copy(ft, fg, osem.at[1]).wait()


def sum_kernel(meta, x_ref, _up, _dn, o_ref):
    total = jnp.sum(x_ref[...].astype(F32), axis=0) / meta[2].astype(F32)
    o_ref[...] = jnp.broadcast_to(total.astype(BF16)[None], o_ref.shape)


def shift(x, axis, step):
    n = lax.axis_size(axis)
    return lax.ppermute(x, axis, [(i, i + step) for i in range(n) if 0 <= i + step < n])


def body(features, kernels, length, cotangent):
    rows, cols, _ = features.shape
    na, nj = rows // 4, cols // 4
    m0, m1, m2, w = 16 * nj, 16 * (nj + 2), 16 * (nj + 4), 16 * (nj + 6)
    ni = na - 4
    meta = jnp.stack([lax.axis_index("row") * rows, lax.axis_index("col") * cols, length[0]]).astype(jnp.int32)
    sds = jax.ShapeDtypeStruct

    step = 4
    fx, gx, to_left, to_right = pl.pallas_call(
        functools.partial(layout_kernel, step=step, nj=nj),
        grid=(na // step,),
        in_specs=[SMEM] + [pl.BlockSpec((4 * step, cols, C), lambda i: (i, 0, 0))] * 2,
        out_specs=[pl.BlockSpec((step, m0, C), lambda i: (i, 0, 0))] * 2
        + [pl.BlockSpec((2, step, 16 * H, C), lambda i: (0, i, 0, 0))] * 2,
        out_shape=[sds((na, m0, C), BF16)] * 2 + [sds((2, na, 16 * H, C), BF16)] * 2,
        compiler_params=params(),
        cost_estimate=cost(0, 16 << 20),
    )(meta, features, cotangent)
    rh = shift(to_left, "col", -1)
    lh = shift(to_right, "col", 1)
    wp = pl.pallas_call(
        pack_kernel,
        in_specs=[VMEM],
        out_specs=VMEM,
        out_shape=sds((4, 12 * C, 2 * C), BF16),
        compiler_params=params(),
        cost_estimate=cost(0, 8 << 20),
    )(kernels)
    ua, ub, da, db = pl.pallas_call(
        functools.partial(assemble_kernel, na=na, nj=nj),
        in_specs=[ANY] * 4,
        out_specs=[ANY] * 4,
        out_shape=[sds((3, w, C), BF16)] * 4,
        scratch_shapes=[pltpu.VMEM((4, 3, w, C), BF16), pltpu.SemaphoreType.DMA((28,))],
        compiler_params=params(),
        cost_estimate=cost(0, 4 << 20),
    )(fx, gx, lh, rh)
    dna = shift(ua, "row", -1)
    upa = shift(da, "row", 1)
    dnb = shift(ub, "row", -1)
    upb = shift(db, "row", 1)

    conv_flops = 2 * rows * cols * 9 * C * C
    a1, a2, st, g1, gf, acc = pl.pallas_call(
        functools.partial(inner_kernel, na=na, nj=nj),
        in_specs=[SMEM] + [ANY] * 4 + [VMEM],
        out_specs=[ANY] * 5 + [VMEM],
        out_shape=[
            sds((na, w, C), BF16),
            sds((na + 4, m2, C), BF16),
            sds((na, m0, C), F32),
            sds((na + 2, m1, C), BF16),
            sds((na, m0, C), F32),
            sds((2, 3 * C, 3 * C), F32),
        ],
        scratch_shapes=[
            pltpu.VMEM((na, w, C), BF16),
            pltpu.VMEM((na, w, C), BF16),
            pltpu.VMEM((na, w, C), BF16),
            pltpu.VMEM((na + 4, m2, C), BF16),
            pltpu.VMEM((ni, m0, C), F32),
            pltpu.VMEM((ni, m1, C), F32),
            pltpu.VMEM((na + 2, m1, C), BF16),
            pltpu.VMEM((ni, m0, C), F32),
            pltpu.VMEM((w, C), F32),
            pltpu.SemaphoreType.DMA((5,)),
            pltpu.SemaphoreType.DMA((6,)),
        ],
        compiler_params=params(),
        cost_estimate=cost(4 * conv_flops, 24 << 20),
    )(meta, fx, gx, lh, rh, wp)

    a2, st, g1, gf, kg = pl.pallas_call(
        functools.partial(edge_kernel, na=na, nj=nj),
        in_specs=[SMEM] + [ANY] * 7 + [VMEM] * 2 + [ANY] * 4,
        out_specs=[ANY] * 4 + [VMEM],
        out_shape=[
            sds((na + 4, m2, C), BF16),
            sds((na, m0, C), F32),
            sds((na + 2, m1, C), BF16),
            sds((na, m0, C), F32),
            sds((2, 3, 3, C, C), BF16),
        ],
        scratch_shapes=[
            pltpu.VMEM((2, 4, w, C), BF16),
            pltpu.VMEM((2, 8, w, C), BF16),
            pltpu.VMEM((2, 2, w, C), BF16),
            pltpu.VMEM((2, 1, w, C), BF16),
            pltpu.VMEM((2, 2, m2, C), BF16),
            pltpu.VMEM((2, 2, m0, C), F32),
            pltpu.VMEM((2, 2, m1, C), F32),
            pltpu.VMEM((2, 2, m1, C), BF16),
            pltpu.VMEM((2, 2, m0, C), F32),
            pltpu.VMEM((w, C), F32),
            pltpu.SemaphoreType.DMA((26,)),
        ],
        input_output_aliases={10: 0, 11: 1, 12: 2, 13: 3},
        compiler_params=params(),
        cost_estimate=cost(conv_flops, 12 << 20),
    )(meta, fx, gx, lh, rh, a1, upa, dna, wp, acc, a2, st, g1, gf)

    axes = ("row", "col")
    parts = lax.axis_size(axes)
    shares = lax.all_to_all(kg.reshape(parts, -1, C), axes, 0, 0, tiled=True)
    spread = pl.pallas_call(
        sum_kernel,
        in_specs=[SMEM, VMEM, ANY, ANY],
        out_specs=VMEM,
        out_shape=sds(shares.shape, BF16),
        compiler_params=params(),
        cost_estimate=cost(0, 2 << 20),
    )(meta, shares, upb, dnb)
    whole = lax.all_to_all(spread, axes, 0, 0, tiled=True)
    kernel_gradient = whole.reshape(kernels.shape).astype(F32)

    out, fg = pl.pallas_call(
        functools.partial(last_kernel, na=na, nj=nj),
        in_specs=[SMEM] + [ANY] * 9 + [VMEM] + [ANY] * 4,
        out_specs=[ANY] * 2,
        out_shape=[sds(features.shape, BF16)] * 2,
        scratch_shapes=[
            pltpu.VMEM((2, 4, w, C), BF16),
            pltpu.VMEM((2, 4, w, C), BF16),
            pltpu.VMEM((2, 3, w, C), BF16),
            pltpu.VMEM((na, m0, C), BF16),
            pltpu.VMEM((na + 4, m2, C), BF16),
            pltpu.VMEM((na, m0, C), F32),
            pltpu.VMEM((2, m1, C), F32),
            pltpu.VMEM((na + 2, m1, C), BF16),
            pltpu.VMEM((na, m0, C), F32),
            pltpu.VMEM((w, C), F32),
            pltpu.VMEM(features.shape, BF16),
            pltpu.VMEM(features.shape, BF16),
            pltpu.SemaphoreType.DMA((27,)),
            pltpu.SemaphoreType.DMA((2,)),
        ],
        compiler_params=params(),
        cost_estimate=cost(2 * conv_flops, 24 << 20),
    )(meta, fx, gx, lh, rh, a1, upa, dna, upb, dnb, wp, a2, st, g1, gf)
    return out, fg, kernel_gradient


def solution(mesh):
    spec = P("row", "col", None)
    return jax.shard_map(
        body, mesh=mesh, in_specs=(spec, P(), P(), spec), out_specs=(spec, spec, P()), check_vma=False
    )
```

```python
import functools

import jax
import jax.numpy as jnp
from jax import lax
from jax.experimental import pallas as pl
from jax.experimental.pallas import tpu as pltpu
from jax.sharding import PartitionSpec as P

H = 3
C = 128
F32 = jnp.float32
BF16 = jnp.bfloat16
ANY = pl.BlockSpec(memory_space=pl.ANY)
VMEM = pl.BlockSpec(memory_space=pltpu.VMEM)
SMEM = pl.BlockSpec(memory_space=pltpu.SMEM)


def params(mib):
    return pltpu.CompilerParams(vmem_limit_bytes=mib << 20)


def cost(flops, nbytes):
    return pl.CostEstimate(flops=int(flops), bytes_accessed=int(nbytes), transcendentals=0)


def to_blocks(rows):
    cols = rows[0].shape[0]
    v = [r.reshape(cols // 8, 8, C) for r in rows]
    low = lax.broadcasted_iota(jnp.int32, v[0].shape, 1) < 4

    def swap(a, b):
        return jnp.where(low, a, pltpu.roll(b, 4, 1)), jnp.where(low, pltpu.roll(a, 4, 1), b)

    a, b = swap(v[0], v[1])
    c, d = swap(v[2], v[3])
    y = jnp.stack([jnp.concatenate([a, c], axis=1), jnp.concatenate([b, d], axis=1)], axis=1)
    return y.reshape(4 * cols, C)


def from_blocks(y):
    cols = y.shape[0] // 4
    y = y.reshape(cols // 8, 2, 2, 8, C)
    a, b, c, d = y[:, 0, 0], y[:, 1, 0], y[:, 0, 1], y[:, 1, 1]
    low = lax.broadcasted_iota(jnp.int32, a.shape, 1) < 4

    def swap(a, b):
        return jnp.where(low, a, pltpu.roll(b, 4, 1)), jnp.where(low, pltpu.roll(a, 4, 1), b)

    r0, r1 = swap(a, b)
    r2, r3 = swap(c, d)
    return [r.reshape(cols, C) for r in (r0, r1, r2, r3)]


def column_mask(meta, nj):
    shape = (nj + 2 * H, 16, C)
    j = lax.broadcasted_iota(jnp.int32, shape, 0)
    s = lax.broadcasted_iota(jnp.int32, shape, 1)
    col = meta[1] + 4 * (j - H) + (s & 3)
    return ((col >= 0) & (col < meta[2])).astype(F32).reshape(-1, C)


def live(meta, cm, a, start, size):
    s = lax.broadcasted_iota(jnp.int32, (1, 16, C), 1)
    row = meta[0] + 4 * a + (s >> 2)
    row_mask = ((row >= 0) & (row < meta[2])).astype(F32)
    return (cm[start : start + size, :].reshape(size // 16, 16, C) * row_mask).reshape(size, C)


def elu_parts(v):
    e = jnp.exp(jnp.minimum(v, 0.0))
    return jnp.maximum(v, 0.0) + (e - 1.0), e


def conv_pairs(read, pairs, d, weights):
    parts = []
    for a in pairs:
        cells = []
        for q in range(3):
            cells += [read(a, q), read(a + d, q), read(a - d, q), read(a + 2 * d, q)]
        parts.append(jnp.concatenate(cells, axis=1))
    left = jnp.concatenate(parts, axis=0) if len(parts) > 1 else parts[0]
    return jnp.dot(left, weights, preferred_element_type=F32)


def outer(left, right):
    return lax.dot_general(left, right, (((0,), (0,)), ((), ())), preferred_element_type=F32)


def pack_kernel(k_ref, *w_refs):
    zero = jnp.zeros((C, C), BF16)
    for layer in range(2):
        for back in range(2):
            def tap(p, q):
                if back:
                    return k_ref[layer, 2 - p, 2 - q].T
                return k_ref[layer, p, q]

            w_ref = w_refs[2 * layer + back]
            for q in range(3):
                t0, t1, t2 = tap(0, q), tap(1, q), tap(2, q)
                o = 4 * C * q
                blocks = ((t1, t0), (t2, t1), (t0, zero), (zero, t2))
                for i, (x, y) in enumerate(blocks):
                    w_ref[o + C * i : o + C * (i + 1), :C] = x
                    w_ref[o + C * i : o + C * (i + 1), C:] = y


def layout_kernel(meta, f_ref, g_ref, fx, gx, ua, da, ub, db, *, step, nj, na):
    m0 = 16 * nj
    i = pl.program_id(0)
    base = i * step
    shape = (nj, 16, C)
    s = lax.broadcasted_iota(jnp.int32, shape, 1)
    j = lax.broadcasted_iota(jnp.int32, shape, 0)
    cm = (meta[1] + 4 * j + (s & 3) < meta[2]).astype(F32)
    s1 = lax.broadcasted_iota(jnp.int32, (1, 16, C), 1)
    own = pl.ds(16 * H, m0)

    def blocks(ref, k):
        return to_blocks([ref[4 * k + t].astype(F32) for t in range(4)])

    for k in range(step):
        fx[k, own] = blocks(f_ref, k).astype(BF16)
        rm = (meta[0] + 4 * (base + k) + (s1 >> 2) < meta[2]).astype(F32)
        g = blocks(g_ref, k).reshape(shape)
        gx[k, own] = (g * (cm * rm)).reshape(m0, C).astype(BF16)

    @pl.when(i == 0)
    def _():
        for out, rows in ((ua, (fx.at[0], gx.at[0], gx.at[1])), (ub, (fx.at[1], fx.at[2], gx.at[2]))):
            for t in range(3):
                out[t, own] = rows[t][own]

    @pl.when(i == na // step - 1)
    def _():
        for out, rows in (
            (da, (fx.at[step - 1], gx.at[step - 2], gx.at[step - 1])),
            (db, (fx.at[step - 3], fx.at[step - 2], gx.at[step - 3])),
        ):
            for t in range(3):
                out[t, own] = rows[t][own]


def halo_kernel(meta, ev_ref, od_ref, _w, *refs, nj, na):
    fx, gx, ua, da, ub, db, buf, sem = refs[6:]
    m0 = 16 * nj
    odd = meta[3] == 1
    shape = (2 * H, 16, C)
    s = lax.broadcasted_iota(jnp.int32, shape, 1)
    j = lax.broadcasted_iota(jnp.int32, shape, 0) - H
    col = meta[1] + 4 * jnp.where(j < 0, j, j + nj) + (s & 3)
    cm = ((col >= 0) & (col < meta[2])).astype(F32)
    s1 = lax.broadcasted_iota(jnp.int32, (1, 16, C), 1)

    def halos(n, k):
        def blocks(ref):
            return to_blocks([ref[n, 4 * k + t].astype(F32) for t in range(4)])

        ev, od = blocks(ev_ref), blocks(od_ref)
        low = jnp.where(odd, ev, od)[16 * (4 - H) :]
        high = jnp.where(odd, od, ev)[: 16 * H]
        return jnp.concatenate([low, high], axis=0)

    for k in range(na):
        f = halos(0, k).astype(BF16)
        rm = (meta[0] + 4 * k + (s1 >> 2) < meta[2]).astype(F32)
        g = (halos(1, k).reshape(shape) * (cm * rm)).reshape(2 * H * 16, C).astype(BF16)
        for n, v in enumerate((f, g)):
            buf[n, 0, k] = v[: 16 * H]
            buf[n, 1, k] = v[16 * H :]
    jobs = []
    go = copier(sem, jobs)
    for side, start in ((0, 0), (1, 16 * H + m0)):
        to = pl.ds(start, 16 * H)
        for out, f0, fn, g0, gn in ((ua, 0, 1, 0, 2), (da, na - 1, 1, na - 2, 2), (ub, 1, 2, 2, 1), (db, na - 3, 2, na - 3, 1)):
            go(buf.at[0, side, pl.ds(f0, fn)], out.at[pl.ds(0, fn), to])
            go(buf.at[1, side, pl.ds(g0, gn)], out.at[pl.ds(fn, gn), to])
        go(buf.at[0, side], fx.at[:, to])
        go(buf.at[1, side], gx.at[:, to])
    for c in jobs:
        c.wait()


def copier(sem, jobs):
    def go(src, dst):
        c = pltpu.make_async_copy(src, dst, sem.at[len(jobs)])
        c.start()
        jobs.append(c)

    return go


def inner_kernel(
    meta, fxi, gxi, wc, wb, a1o, a2o, so, g1o, gfo, acc_o,
    fx, gx, a1, a2, st, es, g1, gf, cm, sem, insem, *, na, nj,
):
    m0, m1, m2, w = 16 * nj, 16 * (nj + 2), 16 * (nj + 4), 16 * (nj + 6)
    ni = na - 4
    jobs = []
    go = copier(insem, jobs)
    go(fxi, fx)
    go(gxi, gx)
    cm[...] = column_mask(meta, nj)
    jobs[0].wait()

    def activate(a, _):
        v, _e = elu_parts(fx[a].astype(F32))
        a1[a] = (v * live(meta, cm, a, 0, w)).astype(BF16)
        return 0

    lax.fori_loop(0, na, activate, 0)
    out_a1 = pltpu.make_async_copy(a1, a1o, sem.at[0])
    out_a1.start()
    jobs[1].wait()

    def quad(t, _):
        r = 2 + 4 * t
        acc = conv_pairs(lambda row, q: a1[row, pl.ds(16 * q, m2), :], [r, r + 2], 1, wc[...])
        for k in range(2):
            for b in range(2):
                row = r + 2 * k + b
                v = fx[row, pl.ds(16, m2), :].astype(F32) + acc[k * m2 : (k + 1) * m2, b * C : (b + 1) * C]
                act, e = elu_parts(v)
                a2[row + 2] = (act * live(meta, cm, row, 16, m2)).astype(BF16)
                es[row - 2] = e[16 : 16 + m1]
                st[row - 2] = v[32 : 32 + m0]
        acc = conv_pairs(lambda row, q: gx[row, pl.ds(32 * q, m1), :], [r, r + 1], 2, wb[...])
        for k in range(2):
            for b in range(2):
                row = r + k + 2 * b
                back = acc[k * m1 : (k + 1) * m1, b * C : (b + 1) * C]
                full = gx[row, pl.ds(32, m1), :].astype(F32) + live(meta, cm, row, 32, m1) * es[row - 2] * back
                g1[row + 1] = full.astype(BF16)
                gf[row - 2] = full[16 : 16 + m0]
        return 0

    lax.fori_loop(0, ni // 4, quad, 0)
    copies = [
        pltpu.make_async_copy(a2.at[pl.ds(4, ni)], a2o.at[pl.ds(4, ni)], sem.at[1]),
        pltpu.make_async_copy(st, so.at[pl.ds(2, ni)], sem.at[2]),
        pltpu.make_async_copy(g1.at[pl.ds(3, ni)], g1o.at[pl.ds(3, ni)], sem.at[3]),
        pltpu.make_async_copy(gf, gfo.at[pl.ds(2, ni)], sem.at[4]),
    ]
    for c in copies:
        c.start()
    for i in (0, 1, 2, 3):
        a2[i] = jnp.zeros((m2, C), BF16)
        a2[na + i] = jnp.zeros((m2, C), BF16)
    for i in (0, 1, 2):
        g1[i] = jnp.zeros((m1, C), BF16)
        g1[na - 1 + i] = jnp.zeros((m1, C), BF16)

    def second(rows):
        left = [jnp.concatenate([a2[b + 2 + s, 32 : 32 + m0] for s in (2, 0, -2)], axis=1) for b in rows]
        right = [jnp.concatenate([gx[b, 16 + 32 * q : 16 + 32 * q + m0] for q in range(3)], axis=1) for b in rows]
        return outer(jnp.concatenate(left, axis=0), jnp.concatenate(right, axis=0))

    def first(rows):
        left = [jnp.concatenate([g1[b + 1 + s, 16 : 16 + m0] for s in (1, 0, -1)], axis=1) for b in rows]
        right = [jnp.concatenate([a1[b, 32 + 16 * q : 32 + 16 * q + m0] for q in range(3)], axis=1) for b in rows]
        return outer(jnp.concatenate(left, axis=0), jnp.concatenate(right, axis=0))

    half = na // 2
    acc_o[1] = second(range(half))
    acc_o[1] += second(range(half, na))
    acc_o[0] = first(range(1, half))
    acc_o[0] += first(range(half, na - 1))
    out_a1.wait()
    for c in copies:
        c.wait()


def edge_kernel(
    meta, fxi, gxi, a1i, up, dn, wc, wb, acc_i, _a2, _s, _g1, _gf, a2o, so, g1o, gfo, kg,
    a1, g, f, fh, a2, st, es, g1, gf, cm, sem, *, na, nj,
):
    m0, m1, m2, w = 16 * nj, 16 * (nj + 2), 16 * (nj + 4), 16 * (nj + 6)
    jobs = []

    go = copier(sem, jobs)
    go(up.at[pl.ds(0, 1)], fh.at[0])
    go(dn.at[pl.ds(0, 1)], fh.at[1])
    go(up.at[pl.ds(1, 2)], g.at[0, pl.ds(0, 2)])
    go(gxi.at[pl.ds(0, 6)], g.at[0, pl.ds(2, 6)])
    go(gxi.at[pl.ds(na - 6, 6)], g.at[1, pl.ds(0, 6)])
    go(dn.at[pl.ds(1, 2)], g.at[1, pl.ds(6, 2)])
    go(a1i.at[pl.ds(0, 3)], a1.at[0, pl.ds(1, 3)])
    go(a1i.at[pl.ds(na - 3, 3)], a1.at[1, pl.ds(0, 3)])
    go(fxi.at[pl.ds(0, 2)], f.at[0])
    go(fxi.at[pl.ds(na - 2, 2)], f.at[1])
    cm[...] = column_mask(meta, nj)
    for c in jobs:
        c.wait()
    for s, row, slot in ((0, -1, 0), (1, na, 3)):
        v, _e = elu_parts(fh[s, 0].astype(F32))
        a1[s, slot] = (v * live(meta, cm, row, 0, w)).astype(BF16)

    acc = conv_pairs(lambda i, q: a1[i // 8, i % 8, 16 * q : 16 * q + m2], [1, 9], 1, wc[...])
    for s in range(2):
        for b in range(2):
            row = (na - 2) * s + b
            v = f[s, b, 16 : 16 + m2].astype(F32) + acc[s * m2 : (s + 1) * m2, b * C : (b + 1) * C]
            act, e = elu_parts(v)
            a2[s, b] = (act * live(meta, cm, row, 16, m2)).astype(BF16)
            es[s, b] = e[16 : 16 + m1]
            st[s, b] = v[32 : 32 + m0]
    acc = conv_pairs(lambda i, q: g[i // 16, i % 16, 32 * q : 32 * q + m1], [2, 3, 18, 19], 2, wb[...])
    for s in range(2):
        for b in range(2):
            row = (na - 2) * s + b
            k = 2 * s + b
            back = acc[k * m1 : (k + 1) * m1, s * C : (s + 1) * C]
            full = g[s, 2 + 2 * s + b, 32 : 32 + m1].astype(F32) + live(meta, cm, row, 32, m1) * es[s, b] * back
            g1[s, b] = full.astype(BF16)
            gf[s, b] = full[16 : 16 + m0]
    outs = len(jobs)
    for s in range(2):
        go(a2.at[s], a2o.at[pl.ds(2 + (na - 2) * s, 2)])
        go(st.at[s], so.at[pl.ds((na - 2) * s, 2)])
        go(g1.at[s], g1o.at[pl.ds(1 + (na - 2) * s, 2)])
        go(gf.at[s], gfo.at[pl.ds((na - 2) * s, 2)])

    rows = [(s, b) for s in range(2) for b in range(2)]
    left = jnp.concatenate([a2[s, b, 32 : 32 + m0] for s, b in rows], axis=0)
    for p in range(3):
        right = [
            jnp.concatenate([g[s, 2 * s + b + 2 * p, 16 + 32 * q : 16 + 32 * q + m0] for q in range(3)], axis=1)
            for s, b in rows
        ]
        total = acc_i[1, C * p : C * (p + 1)] + outer(left, jnp.concatenate(right, axis=0))
        for q in range(3):
            kg[1, 2 - p, 2 - q] = total[:, C * q : C * (q + 1)].astype(BF16)
    left = jnp.concatenate([g1[s, b, 16 : 16 + m0] for s, b in rows], axis=0)
    for p in range(3):
        right = [
            jnp.concatenate([a1[s, b + p, 32 + 16 * q : 32 + 16 * q + m0] for q in range(3)], axis=1) for s, b in rows
        ]
        total = acc_i[0, C * p : C * (p + 1)] + outer(left, jnp.concatenate(right, axis=0))
        for q in range(3):
            kg[0, p, q] = total[:, C * q : C * (q + 1)].T.astype(BF16)
    for c in jobs[outs:]:
        c.wait()


def finish_rows(meta, cm, rows, acc2, acc1, state, grads, feats, put):
    m0 = feats(rows[0]).shape[0]
    for row in rows:
        mask = live(meta, cm, row, 16 * H, m0)
        put(0, row, from_blocks((state(row) + acc2(row)) * mask))
        slope = jnp.exp(jnp.minimum(feats(row).astype(F32), 0.0))
        put(1, row, from_blocks(grads(row) + mask * slope * acc1(row)))


def middle_kernel(meta, fxi, wc2, wb1, a2i, si, g1i, gfi, out, fg, fm, a2, st, g1, gf, cm, ot, ft, sem, osem, *, na, nj):
    m0 = 16 * nj
    ni = na - 4
    jobs = []
    go = copier(sem, jobs)
    go(a2i.at[pl.ds(2, na)], a2)
    go(g1i.at[pl.ds(2, na - 2)], g1)
    go(si.at[pl.ds(2, ni)], st)
    go(fxi.at[pl.ds(2, ni), pl.ds(16 * H, m0)], fm)
    go(gfi.at[pl.ds(2, ni)], gf)
    cm[...] = column_mask(meta, nj)
    for c in jobs:
        c.wait()

    def quad(t, _):
        r = 2 + 4 * t
        acc2 = conv_pairs(lambda row, q: a2[row, pl.ds(32 * q, m0), :], [r, r + 1], 2, wc2[...])
        acc1 = conv_pairs(lambda row, q: g1[row - 1, pl.ds(16 * q, m0), :], [r, r + 2], 1, wb1[...])

        def put(n, row, parts):
            for i, x in enumerate(parts):
                (ot, ft)[n][4 * (row - 2) + i] = x.astype(BF16)

        for k in range(4):
            i2, j2, i1, j1 = k % 2, k // 2, k // 2, k % 2
            finish_rows(
                meta, cm, [r + k],
                lambda _: acc2[i2 * m0 : (i2 + 1) * m0, j2 * C : (j2 + 1) * C],
                lambda _: acc1[i1 * m0 : (i1 + 1) * m0, j1 * C : (j1 + 1) * C],
                lambda row: st[row - 2], lambda row: gf[row - 2], lambda row: fm[row - 2], put,
            )
        here, there = pl.ds(16 * t, 16), pl.ds(16 * t + 8, 16)
        pltpu.make_async_copy(ot.at[here], out.at[there], osem.at[0]).start()
        pltpu.make_async_copy(ft.at[here], fg.at[there], osem.at[1]).start()
        return 0

    lax.fori_loop(0, ni // 4, quad, 0)
    pltpu.make_async_copy(ot, out.at[pl.ds(8, 4 * ni)], osem.at[0]).wait()
    pltpu.make_async_copy(ft, fg.at[pl.ds(8, 4 * ni)], osem.at[1]).wait()


def mask_kernel(meta, cm, *, nj):
    cm[...] = column_mask(meta, nj)


def last_kernel(
    meta, cm, fxi, gxi, a1i, upa, dna, upb, dnb, wc, wb, wc2, wb1, a2i, si, g1i, gfi, _out, _fg, out, fg,
    a1, g, f, fm, a2, st, es, g1, gf, ot, ft, sem, *, na, nj,
):
    m0, m1, m2, w = 16 * nj, 16 * (nj + 2), 16 * (nj + 4), 16 * (nj + 6)
    jobs = []
    go = copier(sem, jobs)
    go(upb.at[pl.ds(0, 2)], f.at[0, pl.ds(0, 2)])
    go(upa.at[pl.ds(0, 1)], f.at[0, pl.ds(2, 1)])
    go(dna.at[pl.ds(0, 1)], f.at[1, pl.ds(0, 1)])
    go(dnb.at[pl.ds(0, 2)], f.at[1, pl.ds(1, 2)])
    go(upb.at[pl.ds(2, 1)], g.at[0, pl.ds(0, 1)])
    go(upa.at[pl.ds(2, 1)], g.at[0, pl.ds(1, 1)])
    go(gxi.at[pl.ds(1, 1)], g.at[0, pl.ds(2, 1)])
    go(gxi.at[pl.ds(3, 1)], g.at[0, pl.ds(3, 1)])
    go(gxi.at[pl.ds(na - 4, 1)], g.at[1, pl.ds(0, 1)])
    go(gxi.at[pl.ds(na - 2, 1)], g.at[1, pl.ds(1, 1)])
    go(dna.at[pl.ds(1, 1)], g.at[1, pl.ds(2, 1)])
    go(dnb.at[pl.ds(2, 1)], g.at[1, pl.ds(3, 1)])
    go(a1i.at[pl.ds(0, 1)], a1.at[0, pl.ds(3, 1)])
    go(a1i.at[pl.ds(na - 1, 1)], a1.at[1, pl.ds(0, 1)])
    early = len(jobs)
    go(a2i.at[pl.ds(2, 6)], a2.at[0, pl.ds(2, 6)])
    go(a2i.at[pl.ds(na - 4, 6)], a2.at[1, pl.ds(0, 6)])
    go(g1i.at[pl.ds(1, 3)], g1.at[0, pl.ds(1, 3)])
    go(g1i.at[pl.ds(na - 2, 3)], g1.at[1, pl.ds(0, 3)])
    for s in range(2):
        two = pl.ds((na - 2) * s, 2)
        go(si.at[two], st.at[s])
        go(fxi.at[two, pl.ds(16 * H, m0)], fm.at[s])
        go(gfi.at[two], gf.at[s])
    for c in jobs[:early]:
        c.wait()
    for s in range(2):
        for i in range(3):
            row = i - 3 if s == 0 else na + i
            v, _e = elu_parts(f[s, i].astype(F32))
            a1[s, i + s] = (v * live(meta, cm, row, 0, w)).astype(BF16)
    acc = conv_pairs(lambda i, q: a1[i // 8, i % 8, 16 * q : 16 * q + m2], [1, 9], 1, wc[...])
    for s in range(2):
        for b in range(2):
            row = b - 2 if s == 0 else na + b
            v = f[s, 1 - s + b, 16 : 16 + m2].astype(F32) + acc[s * m2 : (s + 1) * m2, b * C : (b + 1) * C]
            act, e = elu_parts(v)
            a2[s, 6 * s + b] = (act * live(meta, cm, row, 16, m2)).astype(BF16)
            if b != s:
                es[s] = e[16 : 16 + m1]
    acc = conv_pairs(lambda i, q: g[i // 8, i % 8, 32 * q : 32 * q + m1], [1, 9], 1, wb[...])
    for s in range(2):
        row = -1 if s == 0 else na
        back = acc[s * m1 : (s + 1) * m1, s * C : (s + 1) * C]
        full = g[s, 1 + s, 32 : 32 + m1].astype(F32) + live(meta, cm, row, 32, m1) * es[s] * back
        g1[s, 3 * s] = full.astype(BF16)
    for c in jobs[early:]:
        c.wait()
    acc2 = conv_pairs(lambda i, q: a2[i // 16, i % 16, 32 * q : 32 * q + m0], [2, 3, 18, 19], 2, wc2[...])
    acc1 = conv_pairs(lambda i, q: g1[i // 8, i % 8, 16 * q : 16 * q + m0], [1, 9], 1, wb1[...])
    for s in range(2):
        for b in range(2):
            row = (na - 2) * s + b
            k = 2 * s + b

            def put(n, row, parts):
                for i, x in enumerate(parts):
                    (ot, ft)[n][s, 4 * b + i] = x.astype(BF16)

            finish_rows(
                meta, cm, [row],
                lambda _: acc2[k * m0 : (k + 1) * m0, s * C : (s + 1) * C],
                lambda _: acc1[s * m0 : (s + 1) * m0, b * C : (b + 1) * C],
                lambda _: st[s, b], lambda _: gf[s, b], lambda _: fm[s, b], put,
            )
    done = len(jobs)
    for s in range(2):
        go(ot.at[s], out.at[pl.ds(4 * (na - 2) * s, 8)])
        go(ft.at[s], fg.at[pl.ds(4 * (na - 2) * s, 8)])
    for c in jobs[done:]:
        c.wait()


def sum_kernel(meta, x_ref, _out, o_ref):
    total = jnp.sum(x_ref[...].astype(F32), axis=0) / meta[2].astype(F32)
    o_ref[...] = jnp.broadcast_to(total.astype(BF16)[None], o_ref.shape)


def shift(x, axis, step):
    n = lax.axis_size(axis)
    return lax.ppermute(x, axis, [(i, i + step) for i in range(n) if 0 <= i + step < n])


def body(features, kernels, length, cotangent):
    rows, cols, _ = features.shape
    na, nj = rows // 4, cols // 4
    m0, m1, m2, w = 16 * nj, 16 * (nj + 2), 16 * (nj + 4), 16 * (nj + 6)
    ni = na - 4
    odd = lax.rem(lax.axis_index("col"), 2)
    meta = jnp.stack([lax.axis_index("row") * rows, lax.axis_index("col") * cols, length[0], odd]).astype(jnp.int32)
    sds = jax.ShapeDtypeStruct

    near = jnp.where(odd == 1, 0, cols - 16)
    far = jnp.where(odd == 1, cols - 16, 0)

    def edges(start):
        return jnp.stack([lax.dynamic_slice_in_dim(x, start, 16, axis=1) for x in (features, cotangent)])

    n = lax.axis_size("col")
    inner = [(i, i ^ 1) for i in range(n)]
    outer_pairs = [(i, i + 1) for i in range(1, n - 1, 2)]
    od = lax.ppermute(edges(far), "col", outer_pairs + [(j, i) for i, j in outer_pairs])
    ev = lax.ppermute(edges(near), "col", inner)
    w_one, w_one_back, w_two, w_two_back = pl.pallas_call(
        pack_kernel,
        in_specs=[VMEM],
        out_specs=[VMEM] * 4,
        out_shape=[sds((12 * C, 2 * C), BF16)] * 4,
        compiler_params=params(56),
        cost_estimate=cost(0, 8 << 20),
    )(kernels)
    step = 4
    row_block = pl.BlockSpec((4 * step, cols, C), lambda i: (i, 0, 0))
    shapes = [sds((na, w, C), BF16)] * 2 + [sds((3, w, C), BF16)] * 4
    extended = pl.pallas_call(
        functools.partial(layout_kernel, step=step, nj=nj, na=na),
        grid=(na // step,),
        in_specs=[SMEM, row_block, row_block],
        out_specs=[pl.BlockSpec((step, w, C), lambda i: (i, 0, 0))] * 2
        + [pl.BlockSpec((3, w, C), lambda i: (0, 0, 0))] * 4,
        out_shape=shapes,
        compiler_params=params(56),
        cost_estimate=cost(0, 12 << 20),
    )(meta, features, cotangent)
    fx, gx, ua, da, ub, db = pl.pallas_call(
        functools.partial(halo_kernel, nj=nj, na=na),
        in_specs=[SMEM, VMEM, VMEM, ANY] + [ANY] * 6,
        out_specs=[ANY] * 6,
        out_shape=shapes,
        scratch_shapes=[pltpu.VMEM((2, 2, na, 16 * H, C), BF16), pltpu.SemaphoreType.DMA((20,))],
        input_output_aliases={4 + i: i for i in range(6)},
        compiler_params=params(56),
        cost_estimate=cost(0, 4 << 20),
    )(meta, ev, od, w_one, *extended)
    dna = shift(ua, "row", -1)
    upa = shift(da, "row", 1)
    dnb = shift(ub, "row", -1)
    upb = shift(db, "row", 1)

    conv_flops = 2 * rows * cols * 9 * C * C
    a1, a2, st, g1, gf, acc = pl.pallas_call(
        functools.partial(inner_kernel, na=na, nj=nj),
        in_specs=[SMEM] + [ANY] * 2 + [VMEM] * 2,
        out_specs=[ANY] * 5 + [VMEM],
        out_shape=[
            sds((na, w, C), BF16),
            sds((na + 4, m2, C), BF16),
            sds((na, m0, C), F32),
            sds((na + 2, m1, C), BF16),
            sds((na, m0, C), F32),
            sds((2, 3 * C, 3 * C), F32),
        ],
        scratch_shapes=[
            pltpu.VMEM((na, w, C), BF16),
            pltpu.VMEM((na, w, C), BF16),
            pltpu.VMEM((na, w, C), BF16),
            pltpu.VMEM((na + 4, m2, C), BF16),
            pltpu.VMEM((ni, m0, C), F32),
            pltpu.VMEM((ni, m1, C), F32),
            pltpu.VMEM((na + 2, m1, C), BF16),
            pltpu.VMEM((ni, m0, C), F32),
            pltpu.VMEM((w, C), F32),
            pltpu.SemaphoreType.DMA((5,)),
            pltpu.SemaphoreType.DMA((2,)),
        ],
        compiler_params=params(56),
        cost_estimate=cost(0, 1 << 20),
    )(meta, fx, gx, w_one, w_two_back)

    a2, st, g1, gf, kg = pl.pallas_call(
        functools.partial(edge_kernel, na=na, nj=nj),
        in_specs=[SMEM] + [ANY] * 2 + [ANY] + [ANY] * 2 + [VMEM] * 3 + [ANY] * 4,
        out_specs=[ANY] * 4 + [VMEM],
        out_shape=[
            sds((na + 4, m2, C), BF16),
            sds((na, m0, C), F32),
            sds((na + 2, m1, C), BF16),
            sds((na, m0, C), F32),
            sds((2, 3, 3, C, C), BF16),
        ],
        scratch_shapes=[
            pltpu.VMEM((2, 4, w, C), BF16),
            pltpu.VMEM((2, 8, w, C), BF16),
            pltpu.VMEM((2, 2, w, C), BF16),
            pltpu.VMEM((2, 1, w, C), BF16),
            pltpu.VMEM((2, 2, m2, C), BF16),
            pltpu.VMEM((2, 2, m0, C), F32),
            pltpu.VMEM((2, 2, m1, C), F32),
            pltpu.VMEM((2, 2, m1, C), BF16),
            pltpu.VMEM((2, 2, m0, C), F32),
            pltpu.VMEM((w, C), F32),
            pltpu.SemaphoreType.DMA((18,)),
        ],
        input_output_aliases={9: 0, 10: 1, 11: 2, 12: 3},
        compiler_params=params(56),
        cost_estimate=cost(0, 1 << 20),
    )(meta, fx, gx, a1, upa, dna, w_one, w_two_back, acc, a2, st, g1, gf)

    out, fg = pl.pallas_call(
        functools.partial(middle_kernel, na=na, nj=nj),
        in_specs=[SMEM, ANY] + [VMEM] * 2 + [ANY] * 4,
        out_specs=[ANY] * 2,
        out_shape=[sds(features.shape, BF16)] * 2,
        scratch_shapes=[
            pltpu.VMEM((ni, m0, C), BF16),
            pltpu.VMEM((na, m2, C), BF16),
            pltpu.VMEM((ni, m0, C), F32),
            pltpu.VMEM((na - 2, m1, C), BF16),
            pltpu.VMEM((ni, m0, C), F32),
            pltpu.VMEM((w, C), F32),
            pltpu.VMEM((4 * ni, cols, C), BF16),
            pltpu.VMEM((4 * ni, cols, C), BF16),
            pltpu.SemaphoreType.DMA((5,)),
            pltpu.SemaphoreType.DMA((2,)),
        ],
        compiler_params=params(56),
        cost_estimate=cost(0, 1 << 20),
    )(meta, fx, w_two, w_one_back, a2, st, g1, gf)
    axes = ("row", "col")
    parts = lax.axis_size(axes)
    shares = lax.all_to_all(kg.reshape(parts, -1, C), axes, 0, 0, tiled=True)
    spread = pl.pallas_call(
        sum_kernel,
        in_specs=[SMEM, VMEM, ANY],
        out_specs=VMEM,
        out_shape=sds(shares.shape, BF16),
        compiler_params=params(56),
        cost_estimate=cost(0, 2 << 20),
    )(meta, shares, out)
    whole = lax.all_to_all(spread, axes, 0, 0, tiled=True)
    kernel_gradient = whole.reshape(kernels.shape).astype(F32)

    cm = pl.pallas_call(
        functools.partial(mask_kernel, nj=nj),
        in_specs=[SMEM],
        out_specs=VMEM,
        out_shape=sds((w, C), F32),
        compiler_params=params(56),
        cost_estimate=cost(20 * conv_flops, 1 << 20),
    )(meta)
    out, fg = pl.pallas_call(
        functools.partial(last_kernel, na=na, nj=nj),
        in_specs=[SMEM, VMEM] + [ANY] * 7 + [VMEM] * 4 + [ANY] * 6,
        out_specs=[ANY] * 2,
        out_shape=[sds(features.shape, BF16)] * 2,
        scratch_shapes=[
            pltpu.VMEM((2, 4, w, C), BF16),
            pltpu.VMEM((2, 4, w, C), BF16),
            pltpu.VMEM((2, 3, w, C), BF16),
            pltpu.VMEM((2, 2, m0, C), BF16),
            pltpu.VMEM((2, 8, m2, C), BF16),
            pltpu.VMEM((2, 2, m0, C), F32),
            pltpu.VMEM((2, m1, C), F32),
            pltpu.VMEM((2, 4, m1, C), BF16),
            pltpu.VMEM((2, 2, m0, C), F32),
            pltpu.VMEM((2, 8, cols, C), BF16),
            pltpu.VMEM((2, 8, cols, C), BF16),
            pltpu.SemaphoreType.DMA((28,)),
        ],
        input_output_aliases={17: 0, 18: 1},
        compiler_params=params(56),
        cost_estimate=cost(conv_flops, 12 << 20),
    )(meta, cm, fx, gx, a1, upa, dna, upb, dnb, w_one, w_two_back, w_two, w_one_back, a2, st, g1, gf, out, fg)
    return out, fg, kernel_gradient


def solution(mesh):
    spec = P("row", "col", None)
    return jax.shard_map(
        body, mesh=mesh, in_specs=(spec, P(), P(), spec), out_specs=(spec, spec, P()), check_vma=False
    )
```

```python
import functools

import jax
import jax.numpy as jnp
from jax import lax
from jax.experimental import pallas as pl
from jax.experimental.pallas import tpu as pltpu
from jax.sharding import PartitionSpec as P

H = 3
C = 128
F32 = jnp.float32
BF16 = jnp.bfloat16
ANY = pl.BlockSpec(memory_space=pl.ANY)
VMEM = pl.BlockSpec(memory_space=pltpu.VMEM)
SMEM = pl.BlockSpec(memory_space=pltpu.SMEM)


def params(mib):
    return pltpu.CompilerParams(vmem_limit_bytes=mib << 20)


def cost(flops, nbytes):
    return pl.CostEstimate(flops=int(flops), bytes_accessed=int(nbytes), transcendentals=0)


def to_blocks(rows):
    cols = rows[0].shape[0]
    v = [r.reshape(cols // 8, 8, C) for r in rows]
    low = lax.broadcasted_iota(jnp.int32, v[0].shape, 1) < 4

    def swap(a, b):
        return jnp.where(low, a, pltpu.roll(b, 4, 1)), jnp.where(low, pltpu.roll(a, 4, 1), b)

    a, b = swap(v[0], v[1])
    c, d = swap(v[2], v[3])
    y = jnp.stack([jnp.concatenate([a, c], axis=1), jnp.concatenate([b, d], axis=1)], axis=1)
    return y.reshape(4 * cols, C)


def from_blocks(y):
    cols = y.shape[0] // 4
    y = y.reshape(cols // 8, 2, 2, 8, C)
    a, b, c, d = y[:, 0, 0], y[:, 1, 0], y[:, 0, 1], y[:, 1, 1]
    low = lax.broadcasted_iota(jnp.int32, a.shape, 1) < 4

    def swap(a, b):
        return jnp.where(low, a, pltpu.roll(b, 4, 1)), jnp.where(low, pltpu.roll(a, 4, 1), b)

    r0, r1 = swap(a, b)
    r2, r3 = swap(c, d)
    return [r.reshape(cols, C) for r in (r0, r1, r2, r3)]


def column_mask(meta, nj):
    shape = (nj + 2 * H, 16, C)
    j = lax.broadcasted_iota(jnp.int32, shape, 0)
    s = lax.broadcasted_iota(jnp.int32, shape, 1)
    col = meta[1] + 4 * (j - H) + (s & 3)
    return ((col >= 0) & (col < meta[2])).astype(F32).reshape(-1, C)


def live(meta, cm, a, start, size):
    s = lax.broadcasted_iota(jnp.int32, (1, 16, C), 1)
    row = meta[0] + 4 * a + (s >> 2)
    row_mask = ((row >= 0) & (row < meta[2])).astype(F32)
    return (cm[start : start + size, :].reshape(size // 16, 16, C) * row_mask).reshape(size, C)


def elu_parts(v):
    e = jnp.exp(jnp.minimum(v, 0.0))
    return jnp.maximum(v, 0.0) + (e - 1.0), e


def conv_pairs(read, pairs, d, weights):
    parts = []
    for a in pairs:
        cells = []
        for q in range(3):
            cells += [read(a, q), read(a + d, q), read(a - d, q), read(a + 2 * d, q)]
        parts.append(jnp.concatenate(cells, axis=1))
    left = jnp.concatenate(parts, axis=0) if len(parts) > 1 else parts[0]
    return jnp.dot(left, weights, preferred_element_type=F32)


def outer(left, right):
    return lax.dot_general(left, right, (((0,), (0,)), ((), ())), preferred_element_type=F32)


def pack_kernel(k_ref, conv_ref, back_ref, *, conv_layer, back_layer):
    zero = jnp.zeros((C, C), BF16)

    def conv_tap(p, q):
        return k_ref[conv_layer, p, q]

    def back_tap(p, q):
        return k_ref[back_layer, 2 - p, 2 - q].T

    for tap, w_ref in ((conv_tap, conv_ref), (back_tap, back_ref)):
        for q in range(3):
            t0, t1, t2 = tap(0, q), tap(1, q), tap(2, q)
            o = 4 * C * q
            blocks = ((t1, t0), (t2, t1), (t0, zero), (zero, t2))
            for i, (x, y) in enumerate(blocks):
                w_ref[o + C * i : o + C * (i + 1), :C] = x
                w_ref[o + C * i : o + C * (i + 1), C:] = y


def layout_kernel(meta, f_ref, g_ref, fx, gx, ua, da, ub, db, *, step, nj, na):
    m0 = 16 * nj
    i = pl.program_id(0)
    base = i * step
    shape = (nj, 16, C)
    s = lax.broadcasted_iota(jnp.int32, shape, 1)
    j = lax.broadcasted_iota(jnp.int32, shape, 0)
    cm = (meta[1] + 4 * j + (s & 3) < meta[2]).astype(F32)
    s1 = lax.broadcasted_iota(jnp.int32, (1, 16, C), 1)
    own = pl.ds(16 * H, m0)

    def blocks(ref, k):
        return to_blocks([ref[4 * k + t].astype(F32) for t in range(4)])

    for k in range(step):
        fx[k, own] = blocks(f_ref, k).astype(BF16)
        rm = (meta[0] + 4 * (base + k) + (s1 >> 2) < meta[2]).astype(F32)
        g = blocks(g_ref, k).reshape(shape)
        gx[k, own] = (g * (cm * rm)).reshape(m0, C).astype(BF16)

    @pl.when(i == 0)
    def _():
        for out, rows in ((ua, (fx.at[0], gx.at[0], gx.at[1])), (ub, (fx.at[1], fx.at[2], gx.at[2]))):
            for t in range(3):
                out[t, own] = rows[t][own]

    @pl.when(i == na // step - 1)
    def _():
        for out, rows in (
            (da, (fx.at[step - 1], gx.at[step - 2], gx.at[step - 1])),
            (db, (fx.at[step - 3], fx.at[step - 2], gx.at[step - 3])),
        ):
            for t in range(3):
                out[t, own] = rows[t][own]


def halo_kernel(meta, ev_ref, od_ref, *refs, nj, na):
    fx, gx, ua, da, ub, db, buf, sem = refs[6:]
    m0 = 16 * nj
    odd = meta[3] == 1
    shape = (2 * H, 16, C)
    s = lax.broadcasted_iota(jnp.int32, shape, 1)
    j = lax.broadcasted_iota(jnp.int32, shape, 0) - H
    col = meta[1] + 4 * jnp.where(j < 0, j, j + nj) + (s & 3)
    cm = ((col >= 0) & (col < meta[2])).astype(F32)
    s1 = lax.broadcasted_iota(jnp.int32, (1, 16, C), 1)

    def halos(n, k):
        def blocks(ref):
            return to_blocks([ref[n, 4 * k + t].astype(F32) for t in range(4)])

        ev, od = blocks(ev_ref), blocks(od_ref)
        low = jnp.where(odd, ev, od)[16 * (4 - H) :]
        high = jnp.where(odd, od, ev)[: 16 * H]
        return jnp.concatenate([low, high], axis=0)

    for k in range(na):
        f = halos(0, k).astype(BF16)
        rm = (meta[0] + 4 * k + (s1 >> 2) < meta[2]).astype(F32)
        g = (halos(1, k).reshape(shape) * (cm * rm)).reshape(2 * H * 16, C).astype(BF16)
        for n, v in enumerate((f, g)):
            buf[n, 0, k] = v[: 16 * H]
            buf[n, 1, k] = v[16 * H :]
    jobs = []
    go = copier(sem, jobs)
    for side, start in ((0, 0), (1, 16 * H + m0)):
        to = pl.ds(start, 16 * H)
        for out, f0, fn, g0, gn in ((ua, 0, 1, 0, 2), (da, na - 1, 1, na - 2, 2), (ub, 1, 2, 2, 1), (db, na - 3, 2, na - 3, 1)):
            go(buf.at[0, side, pl.ds(f0, fn)], out.at[pl.ds(0, fn), to])
            go(buf.at[1, side, pl.ds(g0, gn)], out.at[pl.ds(fn, gn), to])
        go(buf.at[0, side], fx.at[:, to])
        go(buf.at[1, side], gx.at[:, to])
    for c in jobs:
        c.wait()


def copier(sem, jobs):
    def go(src, dst):
        c = pltpu.make_async_copy(src, dst, sem.at[len(jobs)])
        c.start()
        jobs.append(c)

    return go


def inner_kernel(
    meta, fxi, gxi, wc, wb, _ub, _db, a1o, a2o, so, g1o, gfo, acc_o, _ubo, _dbo,
    fx, gx, a1, a2, st, es, g1, gf, cm, sem, insem, *, na, nj,
):
    m0, m1, m2, w = 16 * nj, 16 * (nj + 2), 16 * (nj + 4), 16 * (nj + 6)
    ni = na - 4
    jobs = []
    go = copier(insem, jobs)
    group = na // 4
    for i in range(4):
        go(fxi.at[pl.ds(group * i, group)], fx.at[pl.ds(group * i, group)])
    go(gxi, gx)
    cm[...] = column_mask(meta, nj)

    def activate(a, _):
        v, _e = elu_parts(fx[a].astype(F32))
        a1[a] = (v * live(meta, cm, a, 0, w)).astype(BF16)
        return 0

    for i in range(4):
        jobs[i].wait()
        lax.fori_loop(group * i, group * (i + 1), activate, 0)
    out_a1 = pltpu.make_async_copy(a1, a1o, sem.at[0])
    out_a1.start()
    for c in jobs[4:]:
        c.wait()

    def quad(t, _):
        r = 2 + 4 * t
        acc = conv_pairs(lambda row, q: a1[row, pl.ds(16 * q, m2), :], [r, r + 2], 1, wc[...])
        for k in range(2):
            for b in range(2):
                row = r + 2 * k + b
                v = fx[row, pl.ds(16, m2), :].astype(F32) + acc[k * m2 : (k + 1) * m2, b * C : (b + 1) * C]
                act, e = elu_parts(v)
                a2[row + 2] = (act * live(meta, cm, row, 16, m2)).astype(BF16)
                es[row - 2] = e[16 : 16 + m1]
                st[row - 2] = v[32 : 32 + m0]
        acc = conv_pairs(lambda row, q: gx[row, pl.ds(32 * q, m1), :], [r, r + 1], 2, wb[...])
        for k in range(2):
            for b in range(2):
                row = r + k + 2 * b
                back = acc[k * m1 : (k + 1) * m1, b * C : (b + 1) * C]
                full = gx[row, pl.ds(32, m1), :].astype(F32) + live(meta, cm, row, 32, m1) * es[row - 2] * back
                g1[row + 1] = full.astype(BF16)
                gf[row - 2] = full[16 : 16 + m0]
        return 0

    for t in range(ni // 4):
        quad(t, 0)
    copies = [
        pltpu.make_async_copy(a2.at[pl.ds(4, ni)], a2o.at[pl.ds(4, ni)], sem.at[1]),
        pltpu.make_async_copy(st, so.at[pl.ds(2, ni)], sem.at[2]),
        pltpu.make_async_copy(g1.at[pl.ds(3, ni)], g1o.at[pl.ds(3, ni)], sem.at[3]),
        pltpu.make_async_copy(gf, gfo.at[pl.ds(2, ni)], sem.at[4]),
    ]
    for c in copies:
        c.start()
    for i in (0, 1, 2, 3):
        a2[i] = jnp.zeros((m2, C), BF16)
        a2[na + i] = jnp.zeros((m2, C), BF16)
    for i in (0, 1, 2):
        g1[i] = jnp.zeros((m1, C), BF16)
        g1[na - 1 + i] = jnp.zeros((m1, C), BF16)

    def second(rows):
        left = [jnp.concatenate([a2[b + 2 + s, 32 : 32 + m0] for s in (2, 0, -2)], axis=1) for b in rows]
        right = [jnp.concatenate([gx[b, 16 + 32 * q : 16 + 32 * q + m0] for q in range(3)], axis=1) for b in rows]
        return outer(jnp.concatenate(left, axis=0), jnp.concatenate(right, axis=0))

    def first(rows):
        left = [jnp.concatenate([g1[b + 1 + s, 16 : 16 + m0] for s in (1, 0, -1)], axis=1) for b in rows]
        right = [jnp.concatenate([a1[b, 32 + 16 * q : 32 + 16 * q + m0] for q in range(3)], axis=1) for b in rows]
        return outer(jnp.concatenate(left, axis=0), jnp.concatenate(right, axis=0))

    half = na // 2
    acc_o[1] = second(range(half))
    acc_o[1] += second(range(half, na))
    acc_o[0] = first(range(1, half))
    acc_o[0] += first(range(half, na - 1))
    out_a1.wait()
    for c in copies:
        c.wait()


def edge_kernel(
    meta, fxi, gxi, a1i, up, dn, wc, wb, acc_i, _a2, _s, _g1, _gf, a2o, so, g1o, gfo, keep, send,
    a1, g, f, fh, a2, st, es, g1, gf, cm, kg, sem, *, na, nj,
):
    m0, m1, m2, w = 16 * nj, 16 * (nj + 2), 16 * (nj + 4), 16 * (nj + 6)
    jobs = []

    go = copier(sem, jobs)
    go(up.at[pl.ds(0, 1)], fh.at[0])
    go(dn.at[pl.ds(0, 1)], fh.at[1])
    go(a1i.at[pl.ds(0, 3)], a1.at[0, pl.ds(1, 3)])
    go(a1i.at[pl.ds(na - 3, 3)], a1.at[1, pl.ds(0, 3)])
    go(fxi.at[pl.ds(0, 2)], f.at[0])
    go(fxi.at[pl.ds(na - 2, 2)], f.at[1])
    go(up.at[pl.ds(1, 2)], g.at[0, pl.ds(0, 2)])
    go(gxi.at[pl.ds(0, 6)], g.at[0, pl.ds(2, 6)])
    go(gxi.at[pl.ds(na - 6, 6)], g.at[1, pl.ds(0, 6)])
    go(dn.at[pl.ds(1, 2)], g.at[1, pl.ds(6, 2)])
    cm[...] = column_mask(meta, nj)
    for c in jobs:
        c.wait()
    for s, row, slot in ((0, -1, 0), (1, na, 3)):
        v, _e = elu_parts(fh[s, 0].astype(F32))
        a1[s, slot] = (v * live(meta, cm, row, 0, w)).astype(BF16)
    acc = conv_pairs(lambda i, q: a1[i // 8, i % 8, 16 * q : 16 * q + m2], [1, 9], 1, wc[...])
    for s in range(2):
        for b in range(2):
            row = (na - 2) * s + b
            v = f[s, b, 16 : 16 + m2].astype(F32) + acc[s * m2 : (s + 1) * m2, b * C : (b + 1) * C]
            act, e = elu_parts(v)
            a2[s, b] = (act * live(meta, cm, row, 16, m2)).astype(BF16)
            es[s, b] = e[16 : 16 + m1]
            st[s, b] = v[32 : 32 + m0]
    acc = conv_pairs(lambda i, q: g[i // 16, i % 16, 32 * q : 32 * q + m1], [2, 3, 18, 19], 2, wb[...])
    for s in range(2):
        for b in range(2):
            row = (na - 2) * s + b
            k = 2 * s + b
            back = acc[k * m1 : (k + 1) * m1, s * C : (s + 1) * C]
            full = g[s, 2 + 2 * s + b, 32 : 32 + m1].astype(F32) + live(meta, cm, row, 32, m1) * es[s, b] * back
            g1[s, b] = full.astype(BF16)
            gf[s, b] = full[16 : 16 + m0]
    outs = len(jobs)
    for s in range(2):
        go(a2.at[s], a2o.at[pl.ds(2 + (na - 2) * s, 2)])
        go(st.at[s], so.at[pl.ds((na - 2) * s, 2)])
        go(g1.at[s], g1o.at[pl.ds(1 + (na - 2) * s, 2)])
        go(gf.at[s], gfo.at[pl.ds((na - 2) * s, 2)])

    rows = [(s, b) for s in range(2) for b in range(2)]
    left = jnp.concatenate([a2[s, b, 32 : 32 + m0] for s, b in rows], axis=0)
    for p in range(3):
        right = [
            jnp.concatenate([g[s, 2 * s + b + 2 * p, 16 + 32 * q : 16 + 32 * q + m0] for q in range(3)], axis=1)
            for s, b in rows
        ]
        total = acc_i[1, C * p : C * (p + 1)] + outer(left, jnp.concatenate(right, axis=0))
        for q in range(3):
            kg[1, 3 * (2 - p) + 2 - q] = total[:, C * q : C * (q + 1)]
    left = jnp.concatenate([g1[s, b, 16 : 16 + m0] for s, b in rows], axis=0)
    for p in range(3):
        right = [
            jnp.concatenate([a1[s, b + p, 32 + 16 * q : 32 + 16 * q + m0] for q in range(3)], axis=1) for s, b in rows
        ]
        total = acc_i[0, C * p : C * (p + 1)] + outer(left, jnp.concatenate(right, axis=0))
        for q in range(3):
            kg[0, 3 * p + q] = total[:, C * q : C * (q + 1)].T
    mine = meta[3]
    keep[...] = kg[mine]
    send[...] = kg[1 - mine].astype(BF16)
    for c in jobs[outs:]:
        c.wait()


def finish_rows(meta, cm, rows, acc2, acc1, state, grads, feats, put):
    m0 = feats(rows[0]).shape[0]
    for row in rows:
        mask = live(meta, cm, row, 16 * H, m0)
        put(0, row, from_blocks((state(row) + acc2(row)) * mask))
        slope = jnp.exp(jnp.minimum(feats(row).astype(F32), 0.0))
        put(1, row, from_blocks(grads(row) + mask * slope * acc1(row)))


def middle_kernel(
    meta, fxi, wc2i, wb1i, a2i, si, g1i, gfi, out, fg,
    fm, a2, st, g1, gf, cm, ot, ft, wc2, wb1, sem, osem, *, na, nj,
):
    m0 = 16 * nj
    ni = na - 4
    quads = ni // 4
    jobs = []
    go = copier(sem, jobs)

    def later(t, first, per):
        return (0, first) if t == 0 else (first + per * (t - 1), per)

    go(wc2i, wc2)
    go(wb1i, wb1)
    for t in range(quads):
        r, n = later(t, 8, 4)
        go(a2i.at[pl.ds(2 + r, n)], a2.at[pl.ds(r, n)])
        r, n = later(t, 6, 4)
        go(g1i.at[pl.ds(2 + r, n)], g1.at[pl.ds(r, n)])
        here, there = pl.ds(4 * t, 4), pl.ds(2 + 4 * t, 4)
        go(si.at[there], st.at[here])
        go(fxi.at[there, pl.ds(16 * H, m0)], fm.at[here])
        go(gfi.at[there], gf.at[here])
    cm[...] = column_mask(meta, nj)
    for c in jobs[:2]:
        c.wait()

    def quad(t, _):
        r = 2 + 4 * t
        if t < 2:
            for c in jobs[2:7] if t == 0 else jobs[7:]:
                c.wait()
        acc2 = conv_pairs(lambda row, q: a2[row, pl.ds(32 * q, m0), :], [r, r + 1], 2, wc2[...])
        acc1 = conv_pairs(lambda row, q: g1[row - 1, pl.ds(16 * q, m0), :], [r, r + 2], 1, wb1[...])

        def put(n, row, parts):
            for i, x in enumerate(parts):
                (ot, ft)[n][4 * (row - 2) + i] = x.astype(BF16)

        for k in range(4):
            i2, j2, i1, j1 = k % 2, k // 2, k // 2, k % 2
            finish_rows(
                meta, cm, [r + k],
                lambda _: acc2[i2 * m0 : (i2 + 1) * m0, j2 * C : (j2 + 1) * C],
                lambda _: acc1[i1 * m0 : (i1 + 1) * m0, j1 * C : (j1 + 1) * C],
                lambda row: st[row - 2], lambda row: gf[row - 2], lambda row: fm[row - 2], put,
            )
        here, there = pl.ds(16 * t, 16), pl.ds(16 * t + 8, 16)
        pltpu.make_async_copy(ot.at[here], out.at[there], osem.at[0]).start()
        pltpu.make_async_copy(ft.at[here], fg.at[there], osem.at[1]).start()
        return 0

    for t in range(ni // 4):
        quad(t, 0)
    pltpu.make_async_copy(ot, out.at[pl.ds(8, 4 * ni)], osem.at[0]).wait()
    pltpu.make_async_copy(ft, fg.at[pl.ds(8, 4 * ni)], osem.at[1]).wait()


def mask_kernel(meta, cm, *, nj):
    cm[...] = column_mask(meta, nj)


def last_kernel(
    meta, cm, fxi, gxi, a1i, upa, dna, upb, dnb, wci, wbi, wc2i, wb1i, a2i, si, g1i, gfi, _out, _fg, out, fg,
    a1, g, f, fm, a2, st, es, g1, gf, ot, ft, wc, wb, wc2, wb1, sem, *, na, nj,
):
    m0, m1, m2, w = 16 * nj, 16 * (nj + 2), 16 * (nj + 4), 16 * (nj + 6)
    jobs = []
    go = copier(sem, jobs)
    go(upb.at[pl.ds(0, 2)], f.at[0, pl.ds(0, 2)])
    go(upa.at[pl.ds(0, 1)], f.at[0, pl.ds(2, 1)])
    go(dna.at[pl.ds(0, 1)], f.at[1, pl.ds(0, 1)])
    go(dnb.at[pl.ds(0, 2)], f.at[1, pl.ds(1, 2)])
    go(upb.at[pl.ds(2, 1)], g.at[0, pl.ds(0, 1)])
    go(upa.at[pl.ds(2, 1)], g.at[0, pl.ds(1, 1)])
    go(gxi.at[pl.ds(1, 1)], g.at[0, pl.ds(2, 1)])
    go(gxi.at[pl.ds(3, 1)], g.at[0, pl.ds(3, 1)])
    go(gxi.at[pl.ds(na - 4, 1)], g.at[1, pl.ds(0, 1)])
    go(gxi.at[pl.ds(na - 2, 1)], g.at[1, pl.ds(1, 1)])
    go(dna.at[pl.ds(1, 1)], g.at[1, pl.ds(2, 1)])
    go(dnb.at[pl.ds(2, 1)], g.at[1, pl.ds(3, 1)])
    go(a1i.at[pl.ds(0, 1)], a1.at[0, pl.ds(3, 1)])
    go(a1i.at[pl.ds(na - 1, 1)], a1.at[1, pl.ds(0, 1)])
    go(wci, wc)
    go(wbi, wb)
    early = len(jobs)
    go(wc2i, wc2)
    go(wb1i, wb1)
    go(a2i.at[pl.ds(2, 6)], a2.at[0, pl.ds(2, 6)])
    go(a2i.at[pl.ds(na - 4, 6)], a2.at[1, pl.ds(0, 6)])
    go(g1i.at[pl.ds(1, 3)], g1.at[0, pl.ds(1, 3)])
    go(g1i.at[pl.ds(na - 2, 3)], g1.at[1, pl.ds(0, 3)])
    for s in range(2):
        two = pl.ds((na - 2) * s, 2)
        go(si.at[two], st.at[s])
        go(fxi.at[two, pl.ds(16 * H, m0)], fm.at[s])
        go(gfi.at[two], gf.at[s])
    for c in jobs[:early]:
        c.wait()
    for s in range(2):
        for i in range(3):
            row = i - 3 if s == 0 else na + i
            v, _e = elu_parts(f[s, i].astype(F32))
            a1[s, i + s] = (v * live(meta, cm, row, 0, w)).astype(BF16)
    acc = conv_pairs(lambda i, q: a1[i // 8, i % 8, 16 * q : 16 * q + m2], [1, 9], 1, wc[...])
    for s in range(2):
        for b in range(2):
            row = b - 2 if s == 0 else na + b
            v = f[s, 1 - s + b, 16 : 16 + m2].astype(F32) + acc[s * m2 : (s + 1) * m2, b * C : (b + 1) * C]
            act, e = elu_parts(v)
            a2[s, 6 * s + b] = (act * live(meta, cm, row, 16, m2)).astype(BF16)
            if b != s:
                es[s] = e[16 : 16 + m1]
    acc = conv_pairs(lambda i, q: g[i // 8, i % 8, 32 * q : 32 * q + m1], [1, 9], 1, wb[...])
    for s in range(2):
        row = -1 if s == 0 else na
        back = acc[s * m1 : (s + 1) * m1, s * C : (s + 1) * C]
        full = g[s, 1 + s, 32 : 32 + m1].astype(F32) + live(meta, cm, row, 32, m1) * es[s] * back
        g1[s, 3 * s] = full.astype(BF16)
    for c in jobs[early:]:
        c.wait()
    acc2 = conv_pairs(lambda i, q: a2[i // 16, i % 16, 32 * q : 32 * q + m0], [2, 3, 18, 19], 2, wc2[...])
    acc1 = conv_pairs(lambda i, q: g1[i // 8, i % 8, 16 * q : 16 * q + m0], [1, 9], 1, wb1[...])
    for s in range(2):
        for b in range(2):
            row = (na - 2) * s + b
            k = 2 * s + b

            def put(n, row, parts):
                for i, x in enumerate(parts):
                    (ot, ft)[n][s, 4 * b + i] = x.astype(BF16)

            finish_rows(
                meta, cm, [row],
                lambda _: acc2[k * m0 : (k + 1) * m0, s * C : (s + 1) * C],
                lambda _: acc1[s * m0 : (s + 1) * m0, b * C : (b + 1) * C],
                lambda _: st[s, b], lambda _: gf[s, b], lambda _: fm[s, b], put,
            )
    done = len(jobs)
    for s in range(2):
        go(ot.at[s], out.at[pl.ds(4 * (na - 2) * s, 8)])
        go(ft.at[s], fg.at[pl.ds(4 * (na - 2) * s, 8)])
    for c in jobs[done:]:
        c.wait()


def sum_kernel(meta, x_ref, _out, o_ref):
    total = jnp.sum(x_ref[...].astype(F32), axis=0) / meta[2].astype(F32)
    o_ref[...] = jnp.broadcast_to(total.astype(BF16)[None], o_ref.shape)


def hold_kernel(x_ref, o_ref):
    del x_ref, o_ref


def after_kernel(x_ref, _out, o_ref):
    o_ref[...] = x_ref[...]


def join_kernel(meta, mine_ref, other_ref, o_ref):
    mine = meta[3]
    o_ref[mine] = mine_ref[...].astype(F32)
    o_ref[1 - mine] = other_ref[...].astype(F32)


def in_hbm(*arrays):
    return [pltpu.with_memory_space_constraint(x, pltpu.HBM) for x in arrays]


def shift(x, axis, step):
    n = lax.axis_size(axis)
    return lax.ppermute(x, axis, [(i, i + step) for i in range(n) if 0 <= i + step < n])


def body(features, kernels, length, cotangent):
    rows, cols, _ = features.shape
    na, nj = rows // 4, cols // 4
    m0, m1, m2, w = 16 * nj, 16 * (nj + 2), 16 * (nj + 4), 16 * (nj + 6)
    ni = na - 4
    odd = lax.rem(lax.axis_index("col"), 2)
    meta = jnp.stack([lax.axis_index("row") * rows, lax.axis_index("col") * cols, length[0], odd]).astype(jnp.int32)
    sds = jax.ShapeDtypeStruct

    near = jnp.where(odd == 1, 0, cols - 16)
    far = jnp.where(odd == 1, cols - 16, 0)

    def edges(start):
        return jnp.stack([lax.dynamic_slice_in_dim(x, start, 16, axis=1) for x in (features, cotangent)])

    n = lax.axis_size("col")
    inner = [(i, i ^ 1) for i in range(n)]
    outer_pairs = [(i, i + 1) for i in range(1, n - 1, 2)]
    od = lax.ppermute(edges(far), "col", outer_pairs + [(j, i) for i, j in outer_pairs])
    ev = lax.ppermute(edges(near), "col", inner)

    def pack(conv_layer, back_layer, space):
        return pl.pallas_call(
            functools.partial(pack_kernel, conv_layer=conv_layer, back_layer=back_layer),
            in_specs=[VMEM],
            out_specs=[VMEM] * 2,
            out_shape=[space((12 * C, 2 * C), BF16)] * 2,
            compiler_params=params(12),
            cost_estimate=cost(0, 8 << 20),
        )(kernels)

    w_one, w_two_back = pack(0, 1, sds)
    w_two, w_one_back = pack(1, 0, pltpu.HBM)
    step = 4
    row_block = pl.BlockSpec((4 * step, cols, C), lambda i: (i, 0, 0))
    shapes = [pltpu.HBM((na, w, C), BF16)] * 2 + [pltpu.HBM((3, w, C), BF16)] * 4
    extended = pl.pallas_call(
        functools.partial(layout_kernel, step=step, nj=nj, na=na),
        grid=(na // step,),
        in_specs=[SMEM, row_block, row_block],
        out_specs=[pl.BlockSpec((step, w, C), lambda i: (i, 0, 0))] * 2
        + [pl.BlockSpec((3, w, C), lambda i: (0, 0, 0))] * 4,
        out_shape=shapes,
        compiler_params=params(56),
        cost_estimate=cost(0, 12 << 20),
    )(meta, *in_hbm(features, cotangent))
    fx, gx, ua, da, ub, db = pl.pallas_call(
        functools.partial(halo_kernel, nj=nj, na=na),
        in_specs=[SMEM, VMEM, VMEM] + [ANY] * 6,
        out_specs=[ANY] * 6,
        out_shape=shapes,
        scratch_shapes=[pltpu.VMEM((2, 2, na, 16 * H, C), BF16), pltpu.SemaphoreType.DMA((20,))],
        input_output_aliases={3 + i: i for i in range(6)},
        compiler_params=params(12),
        cost_estimate=cost(0, 4 << 20),
    )(meta, ev, od, *extended)
    dna = shift(ua, "row", -1)
    upa = shift(da, "row", 1)

    conv_flops = 2 * rows * cols * 9 * C * C
    a1, a2, st, g1, gf, acc, ub, db = pl.pallas_call(
        functools.partial(inner_kernel, na=na, nj=nj),
        in_specs=[SMEM] + [ANY] * 2 + [VMEM] * 2 + [ANY] * 2,
        out_specs=[ANY] * 5 + [VMEM] + [ANY] * 2,
        out_shape=[
            pltpu.HBM((na, w, C), BF16),
            pltpu.HBM((na + 4, m2, C), BF16),
            pltpu.HBM((na, m0, C), F32),
            pltpu.HBM((na + 2, m1, C), BF16),
            pltpu.HBM((na, m0, C), F32),
            sds((2, 3 * C, 3 * C), F32),
            pltpu.HBM((3, w, C), BF16),
            pltpu.HBM((3, w, C), BF16),
        ],
        scratch_shapes=[
            pltpu.VMEM((na, w, C), BF16),
            pltpu.VMEM((na, w, C), BF16),
            pltpu.VMEM((na, w, C), BF16),
            pltpu.VMEM((na + 4, m2, C), BF16),
            pltpu.VMEM((ni, m0, C), F32),
            pltpu.VMEM((ni, m1, C), F32),
            pltpu.VMEM((na + 2, m1, C), BF16),
            pltpu.VMEM((ni, m0, C), F32),
            pltpu.VMEM((w, C), F32),
            pltpu.SemaphoreType.DMA((5,)),
            pltpu.SemaphoreType.DMA((5,)),
        ],
        input_output_aliases={5: 6, 6: 7},
        compiler_params=params(36),
        cost_estimate=cost(0, 1 << 20),
    )(meta, *in_hbm(fx, gx), w_one, w_two_back, *in_hbm(ub, db))
    dnb = shift(ub, "row", -1)
    upb = shift(db, "row", 1)

    a2, st, g1, gf, keep, send = pl.pallas_call(
        functools.partial(edge_kernel, na=na, nj=nj),
        in_specs=[SMEM] + [ANY] * 5 + [VMEM] * 3 + [ANY] * 4,
        out_specs=[ANY] * 4 + [VMEM] * 2,
        out_shape=[
            pltpu.HBM((na + 4, m2, C), BF16),
            pltpu.HBM((na, m0, C), F32),
            pltpu.HBM((na + 2, m1, C), BF16),
            pltpu.HBM((na, m0, C), F32),
            sds((9, C, C), F32),
            sds((9, C, C), BF16),
        ],
        scratch_shapes=[
            pltpu.VMEM((2, 4, w, C), BF16),
            pltpu.VMEM((2, 8, w, C), BF16),
            pltpu.VMEM((2, 2, w, C), BF16),
            pltpu.VMEM((2, 1, w, C), BF16),
            pltpu.VMEM((2, 2, m2, C), BF16),
            pltpu.VMEM((2, 2, m0, C), F32),
            pltpu.VMEM((2, 2, m1, C), F32),
            pltpu.VMEM((2, 2, m1, C), BF16),
            pltpu.VMEM((2, 2, m0, C), F32),
            pltpu.VMEM((w, C), F32),
            pltpu.VMEM((2, 9, C, C), F32),
            pltpu.SemaphoreType.DMA((18,)),
        ],
        input_output_aliases={9: 0, 10: 1, 11: 2, 12: 3},
        compiler_params=params(24),
        cost_estimate=cost(0, 1 << 20),
    )(meta, *in_hbm(fx, gx, a1), upa, dna, w_one, w_two_back, acc, *in_hbm(a2, st, g1, gf))

    out, fg = pl.pallas_call(
        functools.partial(middle_kernel, na=na, nj=nj),
        in_specs=[SMEM] + [ANY] * 7,
        out_specs=[ANY] * 2,
        out_shape=[pltpu.HBM(features.shape, BF16)] * 2,
        scratch_shapes=[
            pltpu.VMEM((ni, m0, C), BF16),
            pltpu.VMEM((na, m2, C), BF16),
            pltpu.VMEM((ni, m0, C), F32),
            pltpu.VMEM((na - 2, m1, C), BF16),
            pltpu.VMEM((ni, m0, C), F32),
            pltpu.VMEM((w, C), F32),
            pltpu.VMEM((4 * ni, cols, C), BF16),
            pltpu.VMEM((4 * ni, cols, C), BF16),
            pltpu.VMEM((12 * C, 2 * C), BF16),
            pltpu.VMEM((12 * C, 2 * C), BF16),
            pltpu.SemaphoreType.DMA((2 + 5 * (ni // 4),)),
            pltpu.SemaphoreType.DMA((2,)),
        ],
        compiler_params=params(28),
        cost_estimate=cost(20 * conv_flops, 24 << 20),
    )(meta, *in_hbm(fx, w_two, w_one_back), *in_hbm(a2, st, g1, gf))
    received = lax.ppermute(send, "col", inner)
    axes = ("row", "col")
    groups = [
        [r * n + c for r in range(lax.axis_size("row")) for c in range(side, n, 2)] for side in range(2)
    ]
    keep = pl.pallas_call(
        hold_kernel,
        in_specs=[ANY],
        out_specs=ANY,
        out_shape=sds((9, C, C), F32),
        input_output_aliases={0: 0},
        compiler_params=params(10),
        cost_estimate=cost(20 * conv_flops, 1 << 20),
    )(keep)
    share = (keep + received.astype(F32)).astype(BF16).reshape(len(groups[0]), -1, C)
    shares = lax.all_to_all(share, axes, 0, 0, axis_index_groups=groups, tiled=True)
    spread = pl.pallas_call(
        sum_kernel,
        in_specs=[SMEM, VMEM, ANY],
        out_specs=VMEM,
        out_shape=sds(shares.shape, BF16),
        compiler_params=params(10),
        cost_estimate=cost(0, 2 << 20),
    )(meta, shares, *in_hbm(out))
    mine = lax.all_to_all(spread, axes, 0, 0, axis_index_groups=groups, tiled=True).reshape(9, C, C)
    cm = pl.pallas_call(
        functools.partial(mask_kernel, nj=nj),
        in_specs=[SMEM],
        out_specs=VMEM,
        out_shape=sds((w, C), F32),
        compiler_params=params(8),
        cost_estimate=cost(0, 1 << 20),
    )(meta)
    out, fg = pl.pallas_call(
        functools.partial(last_kernel, na=na, nj=nj),
        in_specs=[SMEM, VMEM] + [ANY] * 17,
        out_specs=[ANY] * 2,
        out_shape=[pltpu.HBM(features.shape, BF16)] * 2,
        scratch_shapes=[
            pltpu.VMEM((2, 4, w, C), BF16),
            pltpu.VMEM((2, 4, w, C), BF16),
            pltpu.VMEM((2, 3, w, C), BF16),
            pltpu.VMEM((2, 2, m0, C), BF16),
            pltpu.VMEM((2, 8, m2, C), BF16),
            pltpu.VMEM((2, 2, m0, C), F32),
            pltpu.VMEM((2, m1, C), F32),
            pltpu.VMEM((2, 4, m1, C), BF16),
            pltpu.VMEM((2, 2, m0, C), F32),
            pltpu.VMEM((2, 8, cols, C), BF16),
            pltpu.VMEM((2, 8, cols, C), BF16),
            pltpu.VMEM((12 * C, 2 * C), BF16),
            pltpu.VMEM((12 * C, 2 * C), BF16),
            pltpu.VMEM((12 * C, 2 * C), BF16),
            pltpu.VMEM((12 * C, 2 * C), BF16),
            pltpu.SemaphoreType.DMA((32,)),
        ],
        input_output_aliases={17: 0, 18: 1},
        compiler_params=params(24),
        cost_estimate=cost(20 * conv_flops, 24 << 20),
    )(meta, cm, *in_hbm(fx, gx, a1), upa, dna, upb, dnb, w_one, w_two_back, *in_hbm(w_two, w_one_back, a2, st, g1, gf, out, fg))
    mine = pl.pallas_call(
        after_kernel,
        in_specs=[VMEM, ANY],
        out_specs=VMEM,
        out_shape=sds((9, C, C), BF16),
        compiler_params=params(10),
        cost_estimate=cost(0, 1 << 20),
    )(mine, *in_hbm(out))
    other = lax.ppermute(mine, "col", inner)
    kernel_gradient = pl.pallas_call(
        join_kernel,
        in_specs=[SMEM, VMEM, VMEM],
        out_specs=VMEM,
        out_shape=sds((2, 9, C, C), F32),
        compiler_params=params(10),
        cost_estimate=cost(0, 2 << 20),
    )(meta, mine, other).reshape(kernels.shape)

    return out, fg, kernel_gradient


def solution(mesh):
    spec = P("row", "col", None)
    return jax.shard_map(
        body, mesh=mesh, in_specs=(spec, P(), P(), spec), out_specs=(spec, spec, P()), check_vma=False
    )
```

```python
import functools

import jax
import jax.numpy as jnp
from jax import lax
from jax.experimental import pallas as pl
from jax.experimental.pallas import tpu as pltpu
from jax.sharding import PartitionSpec as P

H = 3
C = 128
F32 = jnp.float32
BF16 = jnp.bfloat16
ANY = pl.BlockSpec(memory_space=pl.ANY)
VMEM = pl.BlockSpec(memory_space=pltpu.VMEM)
SMEM = pl.BlockSpec(memory_space=pltpu.SMEM)


def params(mib):
    return pltpu.CompilerParams(vmem_limit_bytes=mib << 20)


def cost(flops, nbytes):
    return pl.CostEstimate(flops=int(flops), bytes_accessed=int(nbytes), transcendentals=0)


def to_blocks(rows):
    cols = rows[0].shape[0]
    v = [r.reshape(cols // 8, 8, C) for r in rows]
    low = lax.broadcasted_iota(jnp.int32, v[0].shape, 1) < 4

    def swap(a, b):
        return jnp.where(low, a, pltpu.roll(b, 4, 1)), jnp.where(low, pltpu.roll(a, 4, 1), b)

    a, b = swap(v[0], v[1])
    c, d = swap(v[2], v[3])
    y = jnp.stack([jnp.concatenate([a, c], axis=1), jnp.concatenate([b, d], axis=1)], axis=1)
    return y.reshape(4 * cols, C)


def from_blocks(y):
    cols = y.shape[0] // 4
    y = y.reshape(cols // 8, 2, 2, 8, C)
    a, b, c, d = y[:, 0, 0], y[:, 1, 0], y[:, 0, 1], y[:, 1, 1]
    low = lax.broadcasted_iota(jnp.int32, a.shape, 1) < 4

    def swap(a, b):
        return jnp.where(low, a, pltpu.roll(b, 4, 1)), jnp.where(low, pltpu.roll(a, 4, 1), b)

    r0, r1 = swap(a, b)
    r2, r3 = swap(c, d)
    return [r.reshape(cols, C) for r in (r0, r1, r2, r3)]


def column_mask(meta, nj):
    shape = (nj + 2 * H, 16, C)
    j = lax.broadcasted_iota(jnp.int32, shape, 0)
    s = lax.broadcasted_iota(jnp.int32, shape, 1)
    col = meta[1] + 4 * (j - H) + (s & 3)
    return ((col >= 0) & (col < meta[2])).astype(F32).reshape(-1, C)


def live(meta, cm, a, start, size):
    s = lax.broadcasted_iota(jnp.int32, (1, 16, C), 1)
    row = meta[0] + 4 * a + (s >> 2)
    row_mask = ((row >= 0) & (row < meta[2])).astype(F32)
    return (cm[start : start + size, :].reshape(size // 16, 16, C) * row_mask).reshape(size, C)


def elu_parts(v):
    e = jnp.exp(jnp.minimum(v, 0.0))
    return jnp.maximum(v, 0.0) + (e - 1.0), e


def conv_pairs(read, pairs, d, weights):
    parts = []
    for a in pairs:
        cells = []
        for q in range(3):
            cells += [read(a, q), read(a + d, q), read(a - d, q), read(a + 2 * d, q)]
        parts.append(jnp.concatenate(cells, axis=1))
    left = jnp.concatenate(parts, axis=0) if len(parts) > 1 else parts[0]
    return jnp.dot(left, weights, preferred_element_type=F32)


def outer(left, right):
    return lax.dot_general(left, right, (((0,), (0,)), ((), ())), preferred_element_type=F32)


def pack_kernel(k_ref, conv_ref, back_ref, *, conv_layer, back_layer):
    zero = jnp.zeros((C, C), BF16)

    def conv_tap(p, q):
        return k_ref[conv_layer, p, q]

    def back_tap(p, q):
        return k_ref[back_layer, 2 - p, 2 - q].T

    for tap, w_ref in ((conv_tap, conv_ref), (back_tap, back_ref)):
        for q in range(3):
            t0, t1, t2 = tap(0, q), tap(1, q), tap(2, q)
            o = 4 * C * q
            blocks = ((t1, t0), (t2, t1), (t0, zero), (zero, t2))
            for i, (x, y) in enumerate(blocks):
                w_ref[o + C * i : o + C * (i + 1), :C] = x
                w_ref[o + C * i : o + C * (i + 1), C:] = y


def copier(sem, jobs):
    def go(src, dst):
        c = pltpu.make_async_copy(src, dst, sem.at[len(jobs)])
        c.start()
        jobs.append(c)

    return go


def columns_kernel(meta, f, g, near, far, sem, *, cols):
    last = cols - 16
    starts = pl.multiple_of((1 - meta[3]) * last, 16), pl.multiple_of(meta[3] * last, 16)
    jobs = []
    go = copier(sem, jobs)
    for out, start in zip((far, near), starts[::-1]):
        for n, x in enumerate((f, g)):
            go(x.at[:, pl.ds(start, 16)], out.at[n])
    for c in jobs:
        c.wait()


def layout_kernel(meta, fi, gi, fx, gx, f, g, sem, *, nj, na):
    m0 = 16 * nj
    jobs = []
    go = copier(sem, jobs)
    group = na // 4
    for t in range(4):
        rows = pl.ds(4 * group * t, 4 * group)
        go(fi.at[rows], f.at[rows])
        go(gi.at[rows], g.at[rows])
    shape = (nj, 16, C)
    s = lax.broadcasted_iota(jnp.int32, shape, 1)
    j = lax.broadcasted_iota(jnp.int32, shape, 0)
    cm = (meta[1] + 4 * j + (s & 3) < meta[2]).astype(F32)
    s1 = lax.broadcasted_iota(jnp.int32, (1, 16, C), 1)

    def blocks(ref, k):
        return to_blocks([ref[4 * k + t].astype(F32) for t in range(4)])

    for t in range(4):
        jobs[2 * t].wait()
        jobs[2 * t + 1].wait()
        for k in range(group * t, group * (t + 1)):
            fx[k] = blocks(f, k).astype(BF16)
            rm = (meta[0] + 4 * k + (s1 >> 2) < meta[2]).astype(F32)
            gx[k] = (blocks(g, k).reshape(shape) * (cm * rm)).reshape(m0, C).astype(BF16)


def halo_kernel(meta, ev_ref, od_ref, fo, go_ref, _w, _cm, fx, gx, ua, da, ub, db, sem, *, nj, na):
    m0 = 16 * nj
    odd = meta[3] == 1
    shape = (2 * H, 16, C)
    s = lax.broadcasted_iota(jnp.int32, shape, 1)
    j = lax.broadcasted_iota(jnp.int32, shape, 0) - H
    col = meta[1] + 4 * jnp.where(j < 0, j, j + nj) + (s & 3)
    cm = ((col >= 0) & (col < meta[2])).astype(F32)
    s1 = lax.broadcasted_iota(jnp.int32, (1, 16, C), 1)

    def halos(n, k):
        def blocks(ref):
            return to_blocks([ref[n, 4 * k + t].astype(F32) for t in range(4)])

        ev, od = blocks(ev_ref), blocks(od_ref)
        low = jnp.where(odd, ev, od)[16 * (4 - H) :]
        high = jnp.where(odd, od, ev)[: 16 * H]
        return jnp.concatenate([low, high], axis=0)

    def extend(k):
        f = halos(0, k).astype(BF16)
        rm = (meta[0] + 4 * k + (s1 >> 2) < meta[2]).astype(F32)
        g = (halos(1, k).reshape(shape) * (cm * rm)).reshape(2 * H * 16, C).astype(BF16)
        for v, own, ref in ((f, fo, fx), (g, go_ref, gx)):
            ref[k, : 16 * H] = v[: 16 * H]
            ref[k, 16 * H : 16 * H + m0] = own[k]
            ref[k, 16 * H + m0 :] = v[16 * H :]

    ends = [0, 1, 2, na - 3, na - 2, na - 1]
    for k in ends:
        extend(k)
    jobs = []
    go = copier(sem, jobs)
    go(fx.at[pl.ds(1, 2)], ub.at[pl.ds(0, 2)])
    go(gx.at[pl.ds(2, 1)], ub.at[pl.ds(2, 1)])
    go(fx.at[pl.ds(na - 3, 2)], db.at[pl.ds(0, 2)])
    go(gx.at[pl.ds(na - 3, 1)], db.at[pl.ds(2, 1)])
    ua[0], ua[1], ua[2] = fx[0], gx[0], gx[1]
    da[0], da[1], da[2] = fx[na - 1], gx[na - 2], gx[na - 1]
    for k in range(3, na - 3):
        extend(k)
    for c in jobs:
        c.wait()


def inner_kernel(
    meta, fx, gx, wc, wb, _ub, _db, a1, acc_o, wco, wbo, fxo, gxo, a1o, a2o, so, g1o, lo, _ubo, _dbo,
    a2, st, g1, rest, es, cm, sem, *, na, nj,
):
    m0, m1, m2, w = 16 * nj, 16 * (nj + 2), 16 * (nj + 4), 16 * (nj + 6)
    ni = na - 4
    out = []
    send = copier(sem, out)
    send(wc, wco)
    send(wb, wbo)
    send(fx.at[:, pl.ds(16 * H, m0)], fxo)
    for i, row in enumerate((1, 3, na - 4, na - 2)):
        send(gx.at[pl.ds(row, 1)], gxo.at[pl.ds(i, 1)])
    cm[...] = column_mask(meta, nj)

    def activate(a, _):
        v, _e = elu_parts(fx[a].astype(F32))
        a1[a] = (v * live(meta, cm, a, 0, w)).astype(BF16)
        return 0

    lax.fori_loop(0, na, activate, 0)

    for t in range(ni // 4):
        r = 2 + 4 * t
        acc = conv_pairs(lambda row, q: a1[row, 16 * q : 16 * q + m2, :], [r, r + 2], 1, wc[...])
        for k in range(2):
            for b in range(2):
                row = r + 2 * k + b
                v = fx[row, 16 : 16 + m2, :].astype(F32) + acc[k * m2 : (k + 1) * m2, b * C : (b + 1) * C]
                act, e = elu_parts(v)
                a2[row + 2] = (act * live(meta, cm, row, 16, m2)).astype(BF16)
                es[row - 2] = e[16 : 16 + m1]
                st[row - 2] = v[32 : 32 + m0]
        acc = conv_pairs(lambda row, q: gx[row, 32 * q : 32 * q + m1, :], [r, r + 1], 2, wb[...])
        for k in range(2):
            for b in range(2):
                row = r + k + 2 * b
                back = acc[k * m1 : (k + 1) * m1, b * C : (b + 1) * C]
                full = gx[row, 32 : 32 + m1, :].astype(F32) + live(meta, cm, row, 32, m1) * es[row - 2] * back
                rounded = full.astype(BF16)
                g1[row + 1] = rounded
                rest[row - 2] = (full - rounded.astype(F32))[16 : 16 + m0].astype(BF16)

    send(a2.at[pl.ds(4, ni)], a2o)
    send(st, so)
    send(g1.at[pl.ds(3, ni)], g1o)
    send(rest, lo)
    send(a1.at[pl.ds(0, 1)], a1o.at[pl.ds(0, 1)])
    send(a1.at[pl.ds(na - 1, 1)], a1o.at[pl.ds(1, 1)])
    for i in (0, 1, 2, 3):
        a2[i] = jnp.zeros((m2, C), BF16)
        a2[na + i] = jnp.zeros((m2, C), BF16)
    for i in (0, 1, 2):
        g1[i] = jnp.zeros((m1, C), BF16)
        g1[na - 1 + i] = jnp.zeros((m1, C), BF16)

    def second(rows):
        left = [jnp.concatenate([a2[b + 2 + s, 32 : 32 + m0] for s in (2, 0, -2)], axis=1) for b in rows]
        right = [jnp.concatenate([gx[b, 16 + 32 * q : 16 + 32 * q + m0] for q in range(3)], axis=1) for b in rows]
        return outer(jnp.concatenate(left, axis=0), jnp.concatenate(right, axis=0))

    def first(rows):
        left = [jnp.concatenate([g1[b + 1 + s, 16 : 16 + m0] for s in (1, 0, -1)], axis=1) for b in rows]
        right = [jnp.concatenate([a1[b, 32 + 16 * q : 32 + 16 * q + m0] for q in range(3)], axis=1) for b in rows]
        return outer(jnp.concatenate(left, axis=0), jnp.concatenate(right, axis=0))

    half = na // 2
    acc_o[1] = second(range(half))
    acc_o[1] += second(range(half, na))
    acc_o[0] = first(range(1, half))
    acc_o[0] += first(range(half, na - 1))
    for c in out:
        c.wait()


def edge_kernel(
    meta, fx, gx, a1, up, dn, wc, wb, acc_i, a2o, so, g1o, lo, keep, send,
    a2, st, g1, rest, ah, es, cm, kg, sem, *, na, nj,
):
    m0, m1, m2, w = 16 * nj, 16 * (nj + 2), 16 * (nj + 4), 16 * (nj + 6)
    cm[...] = column_mask(meta, nj)
    for i, (ref, row) in enumerate(((up, -1), (dn, na))):
        v, _e = elu_parts(ref[0].astype(F32))
        ah[i] = (v * live(meta, cm, row, 0, w)).astype(BF16)

    def act_one(row, start, size):
        part = slice(start, start + size)
        return ah[0, part] if row < 0 else ah[1, part] if row >= na else a1[row, part]

    def grad_two(row, start, size):
        part = slice(start, start + size)
        return up[3 + row, part] if row < 0 else dn[1 + row - na, part] if row >= na else gx[row, part]

    acc = conv_pairs(lambda row, q: act_one(row, 16 * q, m2), [0, na - 2], 1, wc[...])
    for s in range(2):
        for b in range(2):
            row = (na - 2) * s + b
            v = fx[row, 16 : 16 + m2].astype(F32) + acc[s * m2 : (s + 1) * m2, b * C : (b + 1) * C]
            act, e = elu_parts(v)
            a2[s, b] = (act * live(meta, cm, row, 16, m2)).astype(BF16)
            es[s, b] = e[16 : 16 + m1]
            st[s, b] = v[32 : 32 + m0]
    acc = conv_pairs(lambda row, q: grad_two(row, 32 * q, m1), [0, 1, na - 4, na - 3], 2, wb[...])
    for s in range(2):
        for b in range(2):
            row = (na - 2) * s + b
            k = 2 * s + b
            back = acc[k * m1 : (k + 1) * m1, s * C : (s + 1) * C]
            full = gx[row, 32 : 32 + m1].astype(F32) + live(meta, cm, row, 32, m1) * es[s, b] * back
            rounded = full.astype(BF16)
            g1[s, b] = rounded
            rest[s, b] = (full - rounded.astype(F32))[16 : 16 + m0].astype(BF16)
    jobs = []
    go = copier(sem, jobs)
    for src, dst in ((a2, a2o), (st, so), (g1, g1o), (rest, lo)):
        go(src, dst)

    rows = [(s, b, (na - 2) * s + b) for s in range(2) for b in range(2)]
    left = jnp.concatenate([a2[s, b, 32 : 32 + m0] for s, b, _ in rows], axis=0)
    for p in range(3):
        right = [
            jnp.concatenate([grad_two(row + 2 * (p - 1), 16 + 32 * q, m0) for q in range(3)], axis=1)
            for _, _, row in rows
        ]
        total = acc_i[1, C * p : C * (p + 1)] + outer(left, jnp.concatenate(right, axis=0))
        for q in range(3):
            kg[1, 3 * (2 - p) + 2 - q] = total[:, C * q : C * (q + 1)]
    left = jnp.concatenate([g1[s, b, 16 : 16 + m0] for s, b, _ in rows], axis=0)
    for p in range(3):
        right = [
            jnp.concatenate([act_one(row + p - 1, 32 + 16 * q, m0) for q in range(3)], axis=1) for _, _, row in rows
        ]
        total = acc_i[0, C * p : C * (p + 1)] + outer(left, jnp.concatenate(right, axis=0))
        for q in range(3):
            kg[0, 3 * p + q] = total[:, C * q : C * (q + 1)].T
    mine = meta[3]
    keep[...] = kg[mine]
    send[...] = kg[1 - mine].astype(BF16)
    for c in jobs:
        c.wait()


def finish_state(meta, cm, row, state, product):
    m0 = state.shape[0]
    return from_blocks((state + product) * live(meta, cm, row, 16 * H, m0))


def finish_gradient(meta, cm, row, rounded, rest, feats, product):
    m0 = rest.shape[0]
    slope = jnp.exp(jnp.minimum(feats.astype(F32), 0.0))
    grads = rounded.astype(F32) + rest.astype(F32)
    return from_blocks(grads + live(meta, cm, row, 16 * H, m0) * slope * product)


def middle_kernel(
    meta, wc2, wb1, fxi, a2i, a2e, si, g1i, g1e, loi, out, fg,
    fm, a2, st, g1, lo, cm, ot, ft, sem, osem, *, na, nj,
):
    m0 = 16 * nj
    ni = na - 4
    quads = ni // 4
    jobs = []
    go = copier(sem, jobs)

    def fetch(t, src, edge, dst, reach):
        low = 2 if t == 0 else 6 + reach + 4 * (t - 1)
        high = min(6 + reach + 4 * t, na - 2)
        go(src.at[pl.ds(low - 2, high - low)], dst.at[pl.ds(low, high - low)])
        if t == 0:
            go(edge.at[0], dst.at[pl.ds(0, 2)])
        if t == quads - 1:
            go(edge.at[1], dst.at[pl.ds(na - 2, 2)])

    fetch(0, a2i, a2e, a2, 2)
    fetch(0, g1i, g1e, g1, 1)
    for t in range(quads):
        if t > 0:
            fetch(t, a2i, a2e, a2, 2)
            fetch(t, g1i, g1e, g1, 1)
        here = pl.ds(4 * t, 4)
        go(si.at[here], st.at[here])
        go(fxi.at[pl.ds(2 + 4 * t, 4)], fm.at[here])
        go(loi.at[here], lo.at[here])
        if t == 0:
            stage_three = len(jobs)
    cm[...] = column_mask(meta, nj)

    def arrive(first, last):
        for c in jobs[first:last]:
            c.wait()

    for t in range(quads):
        r = 2 + 4 * t
        if t == 0:
            arrive(0, stage_three)
        elif t == 1:
            arrive(stage_three, len(jobs))
        acc2 = conv_pairs(lambda row, q: a2[row, 32 * q : 32 * q + m0], [r, r + 1], 2, wc2[...])
        acc1 = conv_pairs(lambda row, q: g1[row, 16 * q : 16 * q + m0], [r, r + 2], 1, wb1[...])
        for k in range(2):
            for b in range(2):
                row = r + k + 2 * b
                product = acc2[k * m0 : (k + 1) * m0, b * C : (b + 1) * C]
                for i, x in enumerate(finish_state(meta, cm, row, st[row - 2], product)):
                    ot[4 * (row - 2) + i] = x.astype(BF16)
                row = r + 2 * k + b
                product = acc1[k * m0 : (k + 1) * m0, b * C : (b + 1) * C]
                parts = finish_gradient(
                    meta, cm, row, g1[row, 16 : 16 + m0], lo[row - 2], fm[row - 2], product
                )
                for i, x in enumerate(parts):
                    ft[4 * (row - 2) + i] = x.astype(BF16)
        here, there = pl.ds(16 * t, 16), pl.ds(16 * t + 8, 16)
        pltpu.make_async_copy(ot.at[here], out.at[there], osem.at[0]).start()
        pltpu.make_async_copy(ft.at[here], fg.at[there], osem.at[1]).start()
    pltpu.make_async_copy(ot, out.at[pl.ds(8, 4 * ni)], osem.at[0]).wait()
    pltpu.make_async_copy(ft, fg.at[pl.ds(8, 4 * ni)], osem.at[1]).wait()


def mask_kernel(meta, cm, *, nj):
    cm[...] = column_mask(meta, nj)


def last_kernel(
    meta, cm, fxi, gxi, a1i, upa, dna, upb, dnb, wc2, wb1, wci, wbi, a2i, a2e, g1i, g1e, si, loi, _out, _fg, out, fg,
    own, near, a1, a2, g1, st, lo, ah, a2h, es, g1h, ot, ft, wc, wb, sem, *, na, nj,
):
    m0, m1, m2, w = 16 * nj, 16 * (nj + 2), 16 * (nj + 4), 16 * (nj + 6)
    jobs = []
    go = copier(sem, jobs)
    go(a1i, a1)
    go(wci, wc)
    go(gxi, near)
    go(wbi, wb)
    early = len(jobs)
    go(a2e.at[0], a2.at[0, pl.ds(0, 2)])
    go(a2i.at[pl.ds(0, 4)], a2.at[0, pl.ds(2, 4)])
    go(a2i.at[pl.ds(na - 8, 4)], a2.at[1, pl.ds(0, 4)])
    go(a2e.at[1], a2.at[1, pl.ds(4, 2)])
    go(g1e.at[0], g1.at[0, pl.ds(0, 2)])
    go(g1i.at[pl.ds(0, 1)], g1.at[0, pl.ds(2, 1)])
    go(g1i.at[pl.ds(na - 5, 1)], g1.at[1, pl.ds(0, 1)])
    go(g1e.at[1], g1.at[1, pl.ds(1, 2)])
    go(si, st)
    go(loi, lo)
    for s in range(2):
        go(fxi.at[pl.ds((na - 2) * s, 2)], own.at[s])
    feats = {-3: upb.at[0], -2: upb.at[1], -1: upa.at[0], na: dna.at[0], na + 1: dnb.at[0], na + 2: dnb.at[1]}
    grads = {-3: upb.at[2], -1: upa.at[2], na: dna.at[1], na + 2: dnb.at[2]}
    order = list(feats)
    for i, row in enumerate(order):
        v, _e = elu_parts(feats[row][...].astype(F32))
        ah[i] = (v * live(meta, cm, row, 0, w)).astype(BF16)

    def act_one(row, start):
        part = slice(start, start + m2)
        return ah[order.index(row), part] if row in feats else a1[0 if row == 0 else 1, part]

    def grad_two(row, start):
        part = slice(start, start + m1)
        return grads[row][part] if row in grads else near[(1, 3, na - 4, na - 2).index(row), part]

    def act_two(row, start):
        part = slice(start, start + m0)
        if row < 0 or row >= na:
            return a2h[row + 2 if row < 0 else row - na + 2, part]
        return a2[0, row, part] if row < 6 else a2[1, row - (na - 6), part]

    def grad_one(row, start):
        part = slice(start, start + m0)
        if row < 0 or row >= na:
            return g1h[0 if row < 0 else 1, part]
        return g1[0, row, part] if row < 3 else g1[1, row - (na - 3), part]

    for c in jobs[:early]:
        c.wait()
    acc = conv_pairs(lambda row, q: act_one(row, 16 * q), [-2, na], 1, wc[...])
    for s in range(2):
        for b in range(2):
            row = b - 2 if s == 0 else na + b
            v = feats[row][16 : 16 + m2].astype(F32) + acc[s * m2 : (s + 1) * m2, b * C : (b + 1) * C]
            act, e = elu_parts(v)
            a2h[2 * s + b] = (act * live(meta, cm, row, 16, m2)).astype(BF16)
            if b != s:
                es[s] = e[16 : 16 + m1]
    acc = conv_pairs(lambda row, q: grad_two(row, 32 * q), [-1, na - 2], 2, wb[...])
    for s in range(2):
        row = -1 if s == 0 else na
        back = acc[s * m1 : (s + 1) * m1, s * C : (s + 1) * C]
        full = grads[row][32 : 32 + m1].astype(F32) + live(meta, cm, row, 32, m1) * es[s] * back
        g1h[s] = full.astype(BF16)
    for c in jobs[early:]:
        c.wait()
    acc2 = conv_pairs(lambda row, q: act_two(row, 32 * q), [0, 1, na - 4, na - 3], 2, wc2[...])
    acc1 = conv_pairs(lambda row, q: grad_one(row, 16 * q), [0, na - 2], 1, wb1[...])
    for s in range(2):
        for b in range(2):
            row = (na - 2) * s + b
            k = 2 * s + b
            product = acc2[k * m0 : (k + 1) * m0, s * C : (s + 1) * C]
            for i, x in enumerate(finish_state(meta, cm, row, st[s, b], product)):
                ot[s, 4 * b + i] = x.astype(BF16)
            product = acc1[s * m0 : (s + 1) * m0, b * C : (b + 1) * C]
            rounded = g1[s, s + b, 16 : 16 + m0]
            for i, x in enumerate(finish_gradient(meta, cm, row, rounded, lo[s, b], own[s, b], product)):
                ft[s, 4 * b + i] = x.astype(BF16)
    done = len(jobs)
    for s in range(2):
        go(ot.at[s], out.at[pl.ds(4 * (na - 2) * s, 8)])
        go(ft.at[s], fg.at[pl.ds(4 * (na - 2) * s, 8)])
    for c in jobs[done:]:
        c.wait()


def sum_kernel(meta, x_ref, _out, o_ref):
    total = jnp.sum(x_ref[...].astype(F32), axis=0) / meta[2].astype(F32)
    o_ref[...] = jnp.broadcast_to(total.astype(BF16)[None], o_ref.shape)


def add_kernel(x_ref, y_ref, o_ref):
    o_ref[...] = (x_ref[...] + y_ref[...].astype(F32)).astype(BF16)


def hold_kernel(x_ref, o_ref):
    del x_ref, o_ref


def after_kernel(x_ref, _out, o_ref):
    o_ref[...] = x_ref[...]


def join_kernel(meta, mine_ref, other_ref, o_ref):
    mine = meta[3]
    o_ref[mine] = mine_ref[...].astype(F32)
    o_ref[1 - mine] = other_ref[...].astype(F32)


def in_hbm(*arrays):
    return [pltpu.with_memory_space_constraint(x, pltpu.HBM) for x in arrays]


def in_vmem(*arrays):
    return [pltpu.with_memory_space_constraint(x, pltpu.VMEM) for x in arrays]


def shift(x, axis, step):
    n = lax.axis_size(axis)
    return lax.ppermute(x, axis, [(i, i + step) for i in range(n) if 0 <= i + step < n])


def body(features, kernels, length, cotangent):
    rows, cols, _ = features.shape
    na, nj = rows // 4, cols // 4
    m0, m1, m2, w = 16 * nj, 16 * (nj + 2), 16 * (nj + 4), 16 * (nj + 6)
    ni = na - 4
    odd = lax.rem(lax.axis_index("col"), 2)
    meta = jnp.stack([lax.axis_index("row") * rows, lax.axis_index("col") * cols, length[0], odd]).astype(jnp.int32)
    sds = jax.ShapeDtypeStruct

    near, far = pl.pallas_call(
        functools.partial(columns_kernel, cols=cols),
        in_specs=[SMEM] + [ANY] * 2,
        out_specs=[VMEM] * 2,
        out_shape=[pltpu.VMEM((2, rows, 16, C), BF16)] * 2,
        scratch_shapes=[pltpu.SemaphoreType.DMA((4,))],
        compiler_params=params(8),
        cost_estimate=cost(0, 2 << 20),
    )(meta, *in_hbm(features, cotangent))
    n = lax.axis_size("col")
    inner = [(i, i ^ 1) for i in range(n)]
    outer_pairs = [(i, i + 1) for i in range(1, n - 1, 2)]
    od = lax.ppermute(far, "col", outer_pairs + [(j, i) for i, j in outer_pairs])
    ev = lax.ppermute(near, "col", inner)

    def pack(conv_layer, back_layer):
        return pl.pallas_call(
            functools.partial(pack_kernel, conv_layer=conv_layer, back_layer=back_layer),
            in_specs=[VMEM],
            out_specs=[VMEM] * 2,
            out_shape=[pltpu.VMEM((12 * C, 2 * C), BF16)] * 2,
            compiler_params=params(12),
            cost_estimate=cost(0, 8 << 20),
        )(kernels)

    w_one, w_two_back = pack(0, 1)
    w_two, w_one_back = pack(1, 0)
    cm = pl.pallas_call(
        functools.partial(mask_kernel, nj=nj),
        in_specs=[SMEM],
        out_specs=VMEM,
        out_shape=sds((w, C), F32),
        compiler_params=params(8),
        cost_estimate=cost(0, 1 << 20),
    )(meta)
    vm, hbm = pltpu.VMEM, pltpu.HBM
    fx, gx = pl.pallas_call(
        functools.partial(layout_kernel, nj=nj, na=na),
        in_specs=[SMEM] + [ANY] * 2,
        out_specs=[VMEM] * 2,
        out_shape=[vm((na, m0, C), BF16)] * 2,
        scratch_shapes=[vm(features.shape, BF16), vm(features.shape, BF16), pltpu.SemaphoreType.DMA((8,))],
        compiler_params=params(16),
        cost_estimate=cost(0, 12 << 20),
    )(meta, *in_hbm(features, cotangent))
    fx, gx, ua, da, ub, db = pl.pallas_call(
        functools.partial(halo_kernel, nj=nj, na=na),
        in_specs=[SMEM] + [VMEM] * 4 + [ANY] * 2,
        out_specs=[VMEM] * 4 + [ANY] * 2,
        out_shape=[vm((na, w, C), BF16)] * 2 + [vm((3, w, C), BF16)] * 2 + [hbm((3, w, C), BF16)] * 2,
        scratch_shapes=[pltpu.SemaphoreType.DMA((4,))],
        compiler_params=params(12),
        cost_estimate=cost(0, 4 << 20),
    )(meta, ev, od, *in_vmem(fx, gx), w_two, cm)
    dna = shift(ua, "row", -1)
    upa = shift(da, "row", 1)

    conv_flops = 2 * rows * cols * 9 * C * C
    a1, acc, w_one_far, w_two_back_far, fxo, gxo, a1o, a2, st, g1, lo, ub, db = pl.pallas_call(
        functools.partial(inner_kernel, na=na, nj=nj),
        in_specs=[SMEM] + [VMEM] * 4 + [ANY] * 2,
        out_specs=[VMEM] * 2 + [ANY] * 11,
        out_shape=[
            vm((na, w, C), BF16),
            vm((2, 3 * C, 3 * C), F32),
            hbm((12 * C, 2 * C), BF16),
            hbm((12 * C, 2 * C), BF16),
            hbm((na, m0, C), BF16),
            hbm((4, w, C), BF16),
            hbm((2, w, C), BF16),
            hbm((ni, m2, C), BF16),
            hbm((ni, m0, C), F32),
            hbm((ni, m1, C), BF16),
            hbm((ni, m0, C), BF16),
            hbm((3, w, C), BF16),
            hbm((3, w, C), BF16),
        ],
        scratch_shapes=[
            vm((na + 4, m2, C), BF16),
            vm((ni, m0, C), F32),
            vm((na + 2, m1, C), BF16),
            vm((ni, m0, C), BF16),
            vm((ni, m1, C), F32),
            vm((w, C), F32),
            pltpu.SemaphoreType.DMA((13,)),
        ],
        input_output_aliases={5: 11, 6: 12},
        compiler_params=params(30),
        cost_estimate=cost(0, 1 << 20),
    )(meta, *in_vmem(fx, gx, w_one, w_two_back), *in_hbm(ub, db))
    dnb = shift(ub, "row", -1)
    upb = shift(db, "row", 1)

    a2e, ste, g1e, loe, keep, send = pl.pallas_call(
        functools.partial(edge_kernel, na=na, nj=nj),
        in_specs=[SMEM] + [VMEM] * 8,
        out_specs=[ANY] * 4 + [VMEM] * 2,
        out_shape=[
            hbm((2, 2, m2, C), BF16),
            hbm((2, 2, m0, C), F32),
            hbm((2, 2, m1, C), BF16),
            hbm((2, 2, m0, C), BF16),
            sds((9, C, C), F32),
            sds((9, C, C), BF16),
        ],
        scratch_shapes=[
            vm((2, 2, m2, C), BF16),
            vm((2, 2, m0, C), F32),
            vm((2, 2, m1, C), BF16),
            vm((2, 2, m0, C), BF16),
            vm((2, w, C), BF16),
            vm((2, 2, m1, C), F32),
            vm((w, C), F32),
            vm((2, 9, C, C), F32),
            pltpu.SemaphoreType.DMA((4,)),
        ],
        compiler_params=params(20),
        cost_estimate=cost(0, 1 << 20),
    )(meta, *in_vmem(fx, gx, a1), upa, dna, *in_vmem(w_one, w_two_back, acc))

    out, fg = pl.pallas_call(
        functools.partial(middle_kernel, na=na, nj=nj),
        in_specs=[SMEM] + [VMEM] * 2 + [ANY] * 7,
        out_specs=[ANY] * 2,
        out_shape=[hbm(features.shape, BF16)] * 2,
        scratch_shapes=[
            vm((ni, m0, C), BF16),
            vm((na, m2, C), BF16),
            vm((ni, m0, C), F32),
            vm((na, m1, C), BF16),
            vm((ni, m0, C), BF16),
            vm((w, C), F32),
            vm((4 * ni, cols, C), BF16),
            vm((4 * ni, cols, C), BF16),
            pltpu.SemaphoreType.DMA((4 + 5 * (ni // 4),)),
            pltpu.SemaphoreType.DMA((2,)),
        ],
        compiler_params=params(28),
        cost_estimate=cost(20 * conv_flops, 24 << 20),
    )(meta, *in_vmem(w_two, w_one_back), *in_hbm(fxo, a2, a2e, st, g1, g1e, lo))

    received = lax.ppermute(send, "col", inner)
    axes = ("row", "col")
    groups = [
        [r * n + c for r in range(lax.axis_size("row")) for c in range(side, n, 2)] for side in range(2)
    ]
    keep = pl.pallas_call(
        hold_kernel,
        in_specs=[ANY],
        out_specs=ANY,
        out_shape=sds((9, C, C), F32),
        input_output_aliases={0: 0},
        compiler_params=params(10),
        cost_estimate=cost(20 * conv_flops, 1 << 20),
    )(keep)
    share = pl.pallas_call(
        add_kernel,
        in_specs=[VMEM] * 2,
        out_specs=VMEM,
        out_shape=sds((9, C, C), BF16),
        compiler_params=params(10),
        cost_estimate=cost(0, 1 << 20),
    )(keep, received).reshape(len(groups[0]), -1, C)
    shares = lax.all_to_all(share, axes, 0, 0, axis_index_groups=groups, tiled=True)
    spread = pl.pallas_call(
        sum_kernel,
        in_specs=[SMEM, VMEM, ANY],
        out_specs=VMEM,
        out_shape=sds(shares.shape, BF16),
        compiler_params=params(10),
        cost_estimate=cost(0, 2 << 20),
    )(meta, shares, *in_hbm(out))
    mine = lax.all_to_all(spread, axes, 0, 0, axis_index_groups=groups, tiled=True).reshape(9, C, C)
    out, fg = pl.pallas_call(
        functools.partial(last_kernel, na=na, nj=nj),
        in_specs=[SMEM, VMEM] + [ANY] * 3 + [VMEM] * 6 + [ANY] * 10,
        out_specs=[ANY] * 2,
        out_shape=[hbm(features.shape, BF16)] * 2,
        scratch_shapes=[
            vm((2, 2, m0, C), BF16),
            vm((4, w, C), BF16),
            vm((2, w, C), BF16),
            vm((2, 6, m2, C), BF16),
            vm((2, 3, m1, C), BF16),
            vm((2, 2, m0, C), F32),
            vm((2, 2, m0, C), BF16),
            vm((6, w, C), BF16),
            vm((4, m2, C), BF16),
            vm((2, m1, C), F32),
            vm((2, m1, C), BF16),
            vm((2, 8, cols, C), BF16),
            vm((2, 8, cols, C), BF16),
            vm((12 * C, 2 * C), BF16),
            vm((12 * C, 2 * C), BF16),
            pltpu.SemaphoreType.DMA((24,)),
        ],
        input_output_aliases={19: 0, 20: 1},
        compiler_params=params(24),
        cost_estimate=cost(20 * conv_flops, 24 << 20),
    )(
        meta, cm, *in_hbm(fxo, gxo, a1o), upa, dna, upb, dnb, *in_vmem(w_two, w_one_back),
        *in_hbm(w_one_far, w_two_back_far, a2, a2e, g1, g1e, ste, loe, out, fg),
    )
    mine = pl.pallas_call(
        after_kernel,
        in_specs=[VMEM, ANY],
        out_specs=VMEM,
        out_shape=sds((9, C, C), BF16),
        compiler_params=params(10),
        cost_estimate=cost(0, 1 << 20),
    )(mine, *in_hbm(out))
    other = lax.ppermute(mine, "col", inner)
    kernel_gradient = pl.pallas_call(
        join_kernel,
        in_specs=[SMEM, VMEM, VMEM],
        out_specs=VMEM,
        out_shape=sds((2, 9, C, C), F32),
        compiler_params=params(10),
        cost_estimate=cost(0, 2 << 20),
    )(meta, mine, other).reshape(kernels.shape)

    return out, fg, kernel_gradient


def solution(mesh):
    spec = P("row", "col", None)
    return jax.shard_map(
        body, mesh=mesh, in_specs=(spec, P(), P(), spec), out_specs=(spec, spec, P()), check_vma=False
    )
```

```python
import functools

import jax
import jax.numpy as jnp
from jax import lax
from jax.experimental import pallas as pl
from jax.experimental.pallas import tpu as pltpu
from jax.sharding import PartitionSpec as P

H = 3
C = 128
F32 = jnp.float32
BF16 = jnp.bfloat16
ANY = pl.BlockSpec(memory_space=pl.ANY)
VMEM = pl.BlockSpec(memory_space=pltpu.VMEM)
SMEM = pl.BlockSpec(memory_space=pltpu.SMEM)


def params(mib):
    return pltpu.CompilerParams(vmem_limit_bytes=mib << 20)


def cost(flops, nbytes):
    return pl.CostEstimate(flops=int(flops), bytes_accessed=int(nbytes), transcendentals=0)


def to_blocks(rows):
    cols = rows[0].shape[0]
    v = [r.reshape(cols // 8, 8, C) for r in rows]
    low = lax.broadcasted_iota(jnp.int32, v[0].shape, 1) < 4

    def swap(a, b):
        return jnp.where(low, a, pltpu.roll(b, 4, 1)), jnp.where(low, pltpu.roll(a, 4, 1), b)

    a, b = swap(v[0], v[1])
    c, d = swap(v[2], v[3])
    y = jnp.stack([jnp.concatenate([a, c], axis=1), jnp.concatenate([b, d], axis=1)], axis=1)
    return y.reshape(4 * cols, C)


def from_blocks(y):
    cols = y.shape[0] // 4
    y = y.reshape(cols // 8, 2, 2, 8, C)
    a, b, c, d = y[:, 0, 0], y[:, 1, 0], y[:, 0, 1], y[:, 1, 1]
    low = lax.broadcasted_iota(jnp.int32, a.shape, 1) < 4

    def swap(a, b):
        return jnp.where(low, a, pltpu.roll(b, 4, 1)), jnp.where(low, pltpu.roll(a, 4, 1), b)

    r0, r1 = swap(a, b)
    r2, r3 = swap(c, d)
    return [r.reshape(cols, C) for r in (r0, r1, r2, r3)]


def column_mask(meta, nj):
    shape = (nj + 2 * H, 16, C)
    j = lax.broadcasted_iota(jnp.int32, shape, 0)
    s = lax.broadcasted_iota(jnp.int32, shape, 1)
    col = meta[1] + 4 * (j - H) + (s & 3)
    return ((col >= 0) & (col < meta[2])).astype(F32).reshape(-1, C)


def live(meta, cm, a, start, size):
    s = lax.broadcasted_iota(jnp.int32, (1, 16, C), 1)
    row = meta[0] + 4 * a + (s >> 2)
    row_mask = ((row >= 0) & (row < meta[2])).astype(F32)
    return (cm[start : start + size, :].reshape(size // 16, 16, C) * row_mask).reshape(size, C)


def elu_parts(v):
    e = jnp.exp(jnp.minimum(v, 0.0))
    return jnp.maximum(v, 0.0) + (e - 1.0), e


def conv_pairs(read, pairs, d, weights):
    parts = []
    for a in pairs:
        cells = []
        for q in range(3):
            cells += [read(a, q), read(a + d, q), read(a - d, q), read(a + 2 * d, q)]
        parts.append(jnp.concatenate(cells, axis=1))
    left = jnp.concatenate(parts, axis=0) if len(parts) > 1 else parts[0]
    return jnp.dot(left, weights, preferred_element_type=F32)


def outer(left, right):
    return lax.dot_general(left, right, (((0,), (0,)), ((), ())), preferred_element_type=F32)


def gather(total, lefts, rights, inside, reach):
    runs = {}
    for b in range(min(inside) - reach, max(inside) + reach + 1):
        taps = tuple(p for p in range(3) if b - reach * (p - 1) in inside)
        if taps:
            runs.setdefault(taps, []).append(b)
    for taps, rows in runs.items():
        left = [jnp.concatenate([lefts(b - reach * (p - 1)) for p in taps], axis=1) for b in rows]
        right = [jnp.concatenate([rights(b, q) for q in range(3)], axis=1) for b in rows]
        product = outer(jnp.concatenate(left, axis=0), jnp.concatenate(right, axis=0))
        for i, p in enumerate(taps):
            total[C * p : C * (p + 1)] += product[C * i : C * (i + 1)]


def pack_kernel(k_ref, conv_ref, back_ref, *, conv_layer, back_layer):
    zero = jnp.zeros((C, C), BF16)

    def conv_tap(p, q):
        return k_ref[conv_layer, p, q]

    def back_tap(p, q):
        return k_ref[back_layer, 2 - p, 2 - q].T

    for tap, w_ref in ((conv_tap, conv_ref), (back_tap, back_ref)):
        for q in range(3):
            t0, t1, t2 = tap(0, q), tap(1, q), tap(2, q)
            o = 4 * C * q
            blocks = ((t1, t0), (t2, t1), (t0, zero), (zero, t2))
            for i, (x, y) in enumerate(blocks):
                w_ref[o + C * i : o + C * (i + 1), :C] = x
                w_ref[o + C * i : o + C * (i + 1), C:] = y


def copier(sem, jobs):
    def go(src, dst):
        c = pltpu.make_async_copy(src, dst, sem.at[len(jobs)])
        c.start()
        jobs.append(c)

    return go


def columns_kernel(meta, f, g, near, far, raw, sem, *, cols, na):
    last = cols - 16
    jobs = []
    go = copier(sem, jobs)
    for i in range(2):
        start = pl.multiple_of((meta[3] if i == 0 else 1 - meta[3]) * last, 16)
        for n, x in enumerate((f, g)):
            go(x.at[:, pl.ds(start, 16)], raw.at[i, n])
    for c in jobs:
        c.wait()
    for i, out in enumerate((far, near)):
        right = meta[3] == 1 - i
        for n in range(2):
            for k in range(na):
                v = to_blocks([raw[i, n, 4 * k + t].astype(F32) for t in range(4)])
                out[n, k] = jnp.where(right, v[16 * (4 - H) :], v[: 16 * H]).astype(BF16)


def layout_kernel(meta, fi, gi, fx, gx, f, g, sem, *, nj, na):
    m0 = 16 * nj
    jobs = []
    go = copier(sem, jobs)
    group = na // 4
    for t in range(4):
        rows = pl.ds(4 * group * t, 4 * group)
        go(fi.at[rows], f.at[rows])
        go(gi.at[rows], g.at[rows])
    shape = (nj, 16, C)
    s = lax.broadcasted_iota(jnp.int32, shape, 1)
    j = lax.broadcasted_iota(jnp.int32, shape, 0)
    cm = (meta[1] + 4 * j + (s & 3) < meta[2]).astype(F32)
    s1 = lax.broadcasted_iota(jnp.int32, (1, 16, C), 1)

    def blocks(ref, k):
        return to_blocks([ref[4 * k + t].astype(F32) for t in range(4)])

    for t in range(4):
        jobs[2 * t].wait()
        jobs[2 * t + 1].wait()
        for k in range(group * t, group * (t + 1)):
            fx[k] = blocks(f, k).astype(BF16)
            rm = (meta[0] + 4 * k + (s1 >> 2) < meta[2]).astype(F32)
            gx[k] = (blocks(g, k).reshape(shape) * (cm * rm)).reshape(m0, C).astype(BF16)


def halo_kernel(meta, ev_ref, od_ref, fo, go_ref, _w, _cm, fx, gx, ua, da, ub, db, sem, *, nj, na):
    m0 = 16 * nj
    odd = meta[3] == 1
    shape = (2 * H, 16, C)
    s = lax.broadcasted_iota(jnp.int32, shape, 1)
    j = lax.broadcasted_iota(jnp.int32, shape, 0) - H
    col = meta[1] + 4 * jnp.where(j < 0, j, j + nj) + (s & 3)
    cm = ((col >= 0) & (col < meta[2])).astype(F32)
    s1 = lax.broadcasted_iota(jnp.int32, (1, 16, C), 1)

    def halos(n, k):
        ev, od = ev_ref[n, k].astype(F32), od_ref[n, k].astype(F32)
        return jnp.concatenate([jnp.where(odd, ev, od), jnp.where(odd, od, ev)], axis=0)

    def extend(k):
        f = halos(0, k).astype(BF16)
        rm = (meta[0] + 4 * k + (s1 >> 2) < meta[2]).astype(F32)
        g = (halos(1, k).reshape(shape) * (cm * rm)).reshape(2 * H * 16, C).astype(BF16)
        for v, own, ref in ((f, fo, fx), (g, go_ref, gx)):
            ref[k, : 16 * H] = v[: 16 * H]
            ref[k, 16 * H : 16 * H + m0] = own[k]
            ref[k, 16 * H + m0 :] = v[16 * H :]

    ends = [0, 1, 2, na - 3, na - 2, na - 1]
    for k in ends:
        extend(k)
    jobs = []
    go = copier(sem, jobs)
    go(fx.at[pl.ds(1, 2)], ub.at[pl.ds(0, 2)])
    go(gx.at[pl.ds(2, 1)], ub.at[pl.ds(2, 1)])
    go(fx.at[pl.ds(na - 3, 2)], db.at[pl.ds(0, 2)])
    go(gx.at[pl.ds(na - 3, 1)], db.at[pl.ds(2, 1)])
    ua[0], ua[1], ua[2] = fx[0], gx[0], gx[1]
    da[0], da[1], da[2] = fx[na - 1], gx[na - 2], gx[na - 1]
    for k in range(3, na - 3):
        extend(k)
    for c in jobs:
        c.wait()


def inner_kernel(
    meta, fx, gx, wc, wb, _ub, _db, a1, acc_o, wco, wbo, fxo, gxo, a1o, a2o, so, g1o, lo, _ubo, _dbo,
    a2, st, g1, rest, es, cm, sem, *, na, nj,
):
    m0, m1, m2, w = 16 * nj, 16 * (nj + 2), 16 * (nj + 4), 16 * (nj + 6)
    ni = na - 4
    out = []
    send = copier(sem, out)
    send(wc, wco)
    send(wb, wbo)
    send(fx.at[:, pl.ds(16 * H, m0)], fxo)
    for i, row in enumerate((1, 3, na - 4, na - 2)):
        send(gx.at[pl.ds(row, 1)], gxo.at[pl.ds(i, 1)])
    cm[...] = column_mask(meta, nj)

    def activate(a, _):
        v, _e = elu_parts(fx[a].astype(F32))
        a1[a] = (v * live(meta, cm, a, 0, w)).astype(BF16)
        return 0

    lax.fori_loop(0, na, activate, 0)

    for t in range(ni // 4):
        r = 2 + 4 * t
        acc = conv_pairs(lambda row, q: a1[row, 16 * q : 16 * q + m2, :], [r, r + 2], 1, wc[...])
        for k in range(2):
            for b in range(2):
                row = r + 2 * k + b
                v = fx[row, 16 : 16 + m2, :].astype(F32) + acc[k * m2 : (k + 1) * m2, b * C : (b + 1) * C]
                act, e = elu_parts(v)
                a2[row + 2] = (act * live(meta, cm, row, 16, m2)).astype(BF16)
                es[row - 2] = e[16 : 16 + m1]
                st[row - 2] = v[32 : 32 + m0]
        acc = conv_pairs(lambda row, q: gx[row, 32 * q : 32 * q + m1, :], [r, r + 1], 2, wb[...])
        for k in range(2):
            for b in range(2):
                row = r + k + 2 * b
                back = acc[k * m1 : (k + 1) * m1, b * C : (b + 1) * C]
                full = gx[row, 32 : 32 + m1, :].astype(F32) + live(meta, cm, row, 32, m1) * es[row - 2] * back
                rounded = full.astype(BF16)
                g1[row + 1] = rounded
                rest[row - 2] = (full - rounded.astype(F32))[16 : 16 + m0].astype(BF16)

    send(a2.at[pl.ds(4, ni)], a2o)
    send(st, so)
    send(g1.at[pl.ds(3, ni)], g1o)
    send(rest, lo)
    send(a1.at[pl.ds(0, 1)], a1o.at[pl.ds(0, 1)])
    send(a1.at[pl.ds(na - 1, 1)], a1o.at[pl.ds(1, 1)])
    acc_o[...] = jnp.zeros_like(acc_o)
    inside = range(2, na - 2)
    gather(
        acc_o.at[1], lambda l: a2[l + 2, 32 : 32 + m0], lambda b, q: gx[b, 16 + 32 * q : 16 + 32 * q + m0], inside, 2
    )
    gather(
        acc_o.at[0], lambda l: g1[l + 1, 16 : 16 + m0], lambda b, q: a1[b, 32 + 16 * q : 32 + 16 * q + m0], inside, 1
    )
    for c in out:
        c.wait()


def edge_kernel(
    meta, fx, gx, a1, up, dn, wc, wb, acc_i, a2o, so, g1o, lo, keep, send,
    a2, st, g1, rest, ah, es, cm, total, kg, sem, *, na, nj,
):
    m0, m1, m2, w = 16 * nj, 16 * (nj + 2), 16 * (nj + 4), 16 * (nj + 6)
    cm[...] = column_mask(meta, nj)
    for i, (ref, row) in enumerate(((up, -1), (dn, na))):
        v, _e = elu_parts(ref[0].astype(F32))
        ah[i] = (v * live(meta, cm, row, 0, w)).astype(BF16)

    def act_one(row, start, size):
        part = slice(start, start + size)
        return ah[0, part] if row < 0 else ah[1, part] if row >= na else a1[row, part]

    def grad_two(row, start, size):
        part = slice(start, start + size)
        return up[3 + row, part] if row < 0 else dn[1 + row - na, part] if row >= na else gx[row, part]

    acc = conv_pairs(lambda row, q: act_one(row, 16 * q, m2), [0, na - 2], 1, wc[...])
    for s in range(2):
        for b in range(2):
            row = (na - 2) * s + b
            v = fx[row, 16 : 16 + m2].astype(F32) + acc[s * m2 : (s + 1) * m2, b * C : (b + 1) * C]
            act, e = elu_parts(v)
            a2[s, b] = (act * live(meta, cm, row, 16, m2)).astype(BF16)
            es[s, b] = e[16 : 16 + m1]
            st[s, b] = v[32 : 32 + m0]
    acc = conv_pairs(lambda row, q: grad_two(row, 32 * q, m1), [0, 1, na - 4, na - 3], 2, wb[...])
    for s in range(2):
        for b in range(2):
            row = (na - 2) * s + b
            k = 2 * s + b
            back = acc[k * m1 : (k + 1) * m1, s * C : (s + 1) * C]
            full = gx[row, 32 : 32 + m1].astype(F32) + live(meta, cm, row, 32, m1) * es[s, b] * back
            rounded = full.astype(BF16)
            g1[s, b] = rounded
            rest[s, b] = (full - rounded.astype(F32))[16 : 16 + m0].astype(BF16)
    jobs = []
    go = copier(sem, jobs)
    for src, dst in ((a2, a2o), (st, so), (g1, g1o), (rest, lo)):
        go(src, dst)

    total[...] = acc_i[...]
    inside = (0, 1, na - 2, na - 1)

    def slot(row):
        return (0, row) if row < 2 else (1, row - (na - 2))

    gather(
        total.at[1], lambda l: a2[*slot(l), 32 : 32 + m0], lambda b, q: grad_two(b, 16 + 32 * q, m0), inside, 2
    )
    gather(
        total.at[0], lambda l: g1[*slot(l), 16 : 16 + m0], lambda b, q: act_one(b, 32 + 16 * q, m0), inside, 1
    )
    for p in range(3):
        for q in range(3):
            block = slice(C * p, C * (p + 1)), slice(C * q, C * (q + 1))
            kg[1, 3 * (2 - p) + 2 - q] = total[1, *block]
            kg[0, 3 * p + q] = total[0, *block].T
    mine = meta[3]
    keep[...] = kg[mine]
    send[...] = kg[1 - mine].astype(BF16)
    for c in jobs:
        c.wait()


def finish_state(meta, cm, row, state, product):
    m0 = state.shape[0]
    return from_blocks((state + product) * live(meta, cm, row, 16 * H, m0))


def finish_gradient(meta, cm, row, rounded, rest, feats, product):
    m0 = rest.shape[0]
    slope = jnp.exp(jnp.minimum(feats.astype(F32), 0.0))
    grads = rounded.astype(F32) + rest.astype(F32)
    return from_blocks(grads + live(meta, cm, row, 16 * H, m0) * slope * product)


def middle_kernel(
    meta, wc2, wb1, fxi, a2i, a2e, si, g1i, g1e, loi, out, fg,
    fm, a2, st, g1, lo, cm, ot, ft, sem, osem, *, na, nj,
):
    m0 = 16 * nj
    ni = na - 4
    quads = ni // 4
    jobs = []
    go = copier(sem, jobs)

    def fetch(t, src, edge, dst, reach):
        low = 2 if t == 0 else 6 + reach + 4 * (t - 1)
        high = min(6 + reach + 4 * t, na - 2)
        go(src.at[pl.ds(low - 2, high - low)], dst.at[pl.ds(low, high - low)])
        if t == 0:
            go(edge.at[0], dst.at[pl.ds(0, 2)])
        if t == quads - 1:
            go(edge.at[1], dst.at[pl.ds(na - 2, 2)])

    fetch(0, a2i, a2e, a2, 2)
    fetch(0, g1i, g1e, g1, 1)
    for t in range(quads):
        if t > 0:
            fetch(t, a2i, a2e, a2, 2)
            fetch(t, g1i, g1e, g1, 1)
        here = pl.ds(4 * t, 4)
        go(si.at[here], st.at[here])
        go(fxi.at[pl.ds(2 + 4 * t, 4)], fm.at[here])
        go(loi.at[here], lo.at[here])
        if t == 0:
            stage_three = len(jobs)
    cm[...] = column_mask(meta, nj)

    def arrive(first, last):
        for c in jobs[first:last]:
            c.wait()

    for t in range(quads):
        r = 2 + 4 * t
        if t == 0:
            arrive(0, stage_three)
        elif t == 1:
            arrive(stage_three, len(jobs))
        acc2 = conv_pairs(lambda row, q: a2[row, 32 * q : 32 * q + m0], [r, r + 1], 2, wc2[...])
        acc1 = conv_pairs(lambda row, q: g1[row, 16 * q : 16 * q + m0], [r, r + 2], 1, wb1[...])
        for k in range(2):
            for b in range(2):
                row = r + k + 2 * b
                product = acc2[k * m0 : (k + 1) * m0, b * C : (b + 1) * C]
                for i, x in enumerate(finish_state(meta, cm, row, st[row - 2], product)):
                    ot[4 * (row - 2) + i] = x.astype(BF16)
                row = r + 2 * k + b
                product = acc1[k * m0 : (k + 1) * m0, b * C : (b + 1) * C]
                parts = finish_gradient(
                    meta, cm, row, g1[row, 16 : 16 + m0], lo[row - 2], fm[row - 2], product
                )
                for i, x in enumerate(parts):
                    ft[4 * (row - 2) + i] = x.astype(BF16)
        here, there = pl.ds(16 * t, 16), pl.ds(16 * t + 8, 16)
        pltpu.make_async_copy(ot.at[here], out.at[there], osem.at[0]).start()
        pltpu.make_async_copy(ft.at[here], fg.at[there], osem.at[1]).start()
    pltpu.make_async_copy(ot, out.at[pl.ds(8, 4 * ni)], osem.at[0]).wait()
    pltpu.make_async_copy(ft, fg.at[pl.ds(8, 4 * ni)], osem.at[1]).wait()


def mask_kernel(meta, cm, *, nj):
    cm[...] = column_mask(meta, nj)


def last_kernel(
    meta, cm, fxi, gxi, a1i, upa, dna, upb, dnb, wc2, wb1, wci, wbi, a2i, a2e, g1i, g1e, si, loi, _out, _fg, out, fg,
    own, near, a1, a2, g1, st, lo, ah, a2h, es, g1h, ot, ft, wc, wb, sem, *, na, nj,
):
    m0, m1, m2, w = 16 * nj, 16 * (nj + 2), 16 * (nj + 4), 16 * (nj + 6)
    jobs = []
    go = copier(sem, jobs)
    go(a1i, a1)
    go(wci, wc)
    go(gxi, near)
    go(wbi, wb)
    early = len(jobs)
    go(a2e.at[0], a2.at[0, pl.ds(0, 2)])
    go(a2i.at[pl.ds(0, 4)], a2.at[0, pl.ds(2, 4)])
    go(a2i.at[pl.ds(na - 8, 4)], a2.at[1, pl.ds(0, 4)])
    go(a2e.at[1], a2.at[1, pl.ds(4, 2)])
    go(g1e.at[0], g1.at[0, pl.ds(0, 2)])
    go(g1i.at[pl.ds(0, 1)], g1.at[0, pl.ds(2, 1)])
    go(g1i.at[pl.ds(na - 5, 1)], g1.at[1, pl.ds(0, 1)])
    go(g1e.at[1], g1.at[1, pl.ds(1, 2)])
    go(si, st)
    go(loi, lo)
    for s in range(2):
        go(fxi.at[pl.ds((na - 2) * s, 2)], own.at[s])
    feats = {-3: upb.at[0], -2: upb.at[1], -1: upa.at[0], na: dna.at[0], na + 1: dnb.at[0], na + 2: dnb.at[1]}
    grads = {-3: upb.at[2], -1: upa.at[2], na: dna.at[1], na + 2: dnb.at[2]}
    order = list(feats)
    for i, row in enumerate(order):
        v, _e = elu_parts(feats[row][...].astype(F32))
        ah[i] = (v * live(meta, cm, row, 0, w)).astype(BF16)

    def act_one(row, start):
        part = slice(start, start + m2)
        return ah[order.index(row), part] if row in feats else a1[0 if row == 0 else 1, part]

    def grad_two(row, start):
        part = slice(start, start + m1)
        return grads[row][part] if row in grads else near[(1, 3, na - 4, na - 2).index(row), part]

    def act_two(row, start):
        part = slice(start, start + m0)
        if row < 0 or row >= na:
            return a2h[row + 2 if row < 0 else row - na + 2, part]
        return a2[0, row, part] if row < 6 else a2[1, row - (na - 6), part]

    def grad_one(row, start):
        part = slice(start, start + m0)
        if row < 0 or row >= na:
            return g1h[0 if row < 0 else 1, part]
        return g1[0, row, part] if row < 3 else g1[1, row - (na - 3), part]

    for c in jobs[:early]:
        c.wait()
    acc = conv_pairs(lambda row, q: act_one(row, 16 * q), [-2, na], 1, wc[...])
    for s in range(2):
        for b in range(2):
            row = b - 2 if s == 0 else na + b
            v = feats[row][16 : 16 + m2].astype(F32) + acc[s * m2 : (s + 1) * m2, b * C : (b + 1) * C]
            act, e = elu_parts(v)
            a2h[2 * s + b] = (act * live(meta, cm, row, 16, m2)).astype(BF16)
            if b != s:
                es[s] = e[16 : 16 + m1]
    acc = conv_pairs(lambda row, q: grad_two(row, 32 * q), [-1, na - 2], 2, wb[...])
    for s in range(2):
        row = -1 if s == 0 else na
        back = acc[s * m1 : (s + 1) * m1, s * C : (s + 1) * C]
        full = grads[row][32 : 32 + m1].astype(F32) + live(meta, cm, row, 32, m1) * es[s] * back
        g1h[s] = full.astype(BF16)
    for c in jobs[early:]:
        c.wait()
    acc2 = conv_pairs(lambda row, q: act_two(row, 32 * q), [0, 1, na - 4, na - 3], 2, wc2[...])
    acc1 = conv_pairs(lambda row, q: grad_one(row, 16 * q), [0, na - 2], 1, wb1[...])
    for s in range(2):
        for b in range(2):
            row = (na - 2) * s + b
            k = 2 * s + b
            product = acc2[k * m0 : (k + 1) * m0, s * C : (s + 1) * C]
            for i, x in enumerate(finish_state(meta, cm, row, st[s, b], product)):
                ot[s, 4 * b + i] = x.astype(BF16)
            product = acc1[s * m0 : (s + 1) * m0, b * C : (b + 1) * C]
            rounded = g1[s, s + b, 16 : 16 + m0]
            for i, x in enumerate(finish_gradient(meta, cm, row, rounded, lo[s, b], own[s, b], product)):
                ft[s, 4 * b + i] = x.astype(BF16)
    done = len(jobs)
    for s in range(2):
        go(ot.at[s], out.at[pl.ds(4 * (na - 2) * s, 8)])
        go(ft.at[s], fg.at[pl.ds(4 * (na - 2) * s, 8)])
    for c in jobs[done:]:
        c.wait()


def sum_kernel(meta, x_ref, _out, o_ref):
    total = jnp.sum(x_ref[...].astype(F32), axis=0) / meta[2].astype(F32)
    o_ref[...] = jnp.broadcast_to(total.astype(BF16)[None], o_ref.shape)


def add_kernel(x_ref, y_ref, o_ref):
    o_ref[...] = (x_ref[...] + y_ref[...].astype(F32)).astype(BF16)


def hold_kernel(x_ref, o_ref):
    del x_ref, o_ref


def after_kernel(x_ref, _out, o_ref):
    o_ref[...] = x_ref[...]


def join_kernel(meta, mine_ref, other_ref, o_ref):
    mine = meta[3]
    o_ref[mine] = mine_ref[...].astype(F32)
    o_ref[1 - mine] = other_ref[...].astype(F32)


def in_hbm(*arrays):
    return [pltpu.with_memory_space_constraint(x, pltpu.HBM) for x in arrays]


def in_vmem(*arrays):
    return [pltpu.with_memory_space_constraint(x, pltpu.VMEM) for x in arrays]


def shift(x, axis, step):
    n = lax.axis_size(axis)
    return lax.ppermute(x, axis, [(i, i + step) for i in range(n) if 0 <= i + step < n])


def body(features, kernels, length, cotangent):
    rows, cols, _ = features.shape
    na, nj = rows // 4, cols // 4
    m0, m1, m2, w = 16 * nj, 16 * (nj + 2), 16 * (nj + 4), 16 * (nj + 6)
    ni = na - 4
    odd = lax.rem(lax.axis_index("col"), 2)
    meta = jnp.stack([lax.axis_index("row") * rows, lax.axis_index("col") * cols, length[0], odd]).astype(jnp.int32)
    sds = jax.ShapeDtypeStruct

    near, far = pl.pallas_call(
        functools.partial(columns_kernel, cols=cols, na=na),
        in_specs=[SMEM] + [ANY] * 2,
        out_specs=[VMEM] * 2,
        out_shape=[pltpu.VMEM((2, na, 16 * H, C), BF16)] * 2,
        scratch_shapes=[pltpu.VMEM((2, 2, rows, 16, C), BF16), pltpu.SemaphoreType.DMA((4,))],
        compiler_params=params(10),
        cost_estimate=cost(0, 2 << 20),
    )(meta, *in_hbm(features, cotangent))
    n = lax.axis_size("col")
    inner = [(i, i ^ 1) for i in range(n)]
    outer_pairs = [(i, i + 1) for i in range(1, n - 1, 2)]
    od = lax.ppermute(far, "col", outer_pairs + [(j, i) for i, j in outer_pairs])
    ev = lax.ppermute(near, "col", inner)

    def pack(conv_layer, back_layer):
        return pl.pallas_call(
            functools.partial(pack_kernel, conv_layer=conv_layer, back_layer=back_layer),
            in_specs=[VMEM],
            out_specs=[VMEM] * 2,
            out_shape=[pltpu.VMEM((12 * C, 2 * C), BF16)] * 2,
            compiler_params=params(12),
            cost_estimate=cost(0, 8 << 20),
        )(kernels)

    w_one, w_two_back = pack(0, 1)
    w_two, w_one_back = pack(1, 0)
    cm = pl.pallas_call(
        functools.partial(mask_kernel, nj=nj),
        in_specs=[SMEM],
        out_specs=VMEM,
        out_shape=sds((w, C), F32),
        compiler_params=params(8),
        cost_estimate=cost(0, 1 << 20),
    )(meta)
    vm, hbm = pltpu.VMEM, pltpu.HBM
    fx, gx = pl.pallas_call(
        functools.partial(layout_kernel, nj=nj, na=na),
        in_specs=[SMEM] + [ANY] * 2,
        out_specs=[VMEM] * 2,
        out_shape=[vm((na, m0, C), BF16)] * 2,
        scratch_shapes=[vm(features.shape, BF16), vm(features.shape, BF16), pltpu.SemaphoreType.DMA((8,))],
        compiler_params=params(16),
        cost_estimate=cost(0, 12 << 20),
    )(meta, *in_hbm(features, cotangent))
    fx, gx, ua, da, ub, db = pl.pallas_call(
        functools.partial(halo_kernel, nj=nj, na=na),
        in_specs=[SMEM] + [VMEM] * 4 + [ANY] * 2,
        out_specs=[VMEM] * 4 + [ANY] * 2,
        out_shape=[vm((na, w, C), BF16)] * 2 + [vm((3, w, C), BF16)] * 2 + [hbm((3, w, C), BF16)] * 2,
        scratch_shapes=[pltpu.SemaphoreType.DMA((4,))],
        compiler_params=params(12),
        cost_estimate=cost(0, 4 << 20),
    )(meta, ev, od, *in_vmem(fx, gx), w_two, cm)
    dna = shift(ua, "row", -1)
    upa = shift(da, "row", 1)

    conv_flops = 2 * rows * cols * 9 * C * C
    a1, acc, w_one_far, w_two_back_far, fxo, gxo, a1o, a2, st, g1, lo, ub, db = pl.pallas_call(
        functools.partial(inner_kernel, na=na, nj=nj),
        in_specs=[SMEM] + [VMEM] * 4 + [ANY] * 2,
        out_specs=[VMEM] * 2 + [ANY] * 11,
        out_shape=[
            vm((na, w, C), BF16),
            vm((2, 3 * C, 3 * C), F32),
            hbm((12 * C, 2 * C), BF16),
            hbm((12 * C, 2 * C), BF16),
            hbm((na, m0, C), BF16),
            hbm((4, w, C), BF16),
            hbm((2, w, C), BF16),
            hbm((ni, m2, C), BF16),
            hbm((ni, m0, C), F32),
            hbm((ni, m1, C), BF16),
            hbm((ni, m0, C), BF16),
            hbm((3, w, C), BF16),
            hbm((3, w, C), BF16),
        ],
        scratch_shapes=[
            vm((na + 4, m2, C), BF16),
            vm((ni, m0, C), F32),
            vm((na + 2, m1, C), BF16),
            vm((ni, m0, C), BF16),
            vm((ni, m1, C), F32),
            vm((w, C), F32),
            pltpu.SemaphoreType.DMA((13,)),
        ],
        input_output_aliases={5: 11, 6: 12},
        compiler_params=params(30),
        cost_estimate=cost(0, 1 << 20),
    )(meta, *in_vmem(fx, gx, w_one, w_two_back), *in_hbm(ub, db))
    dnb = shift(ub, "row", -1)
    upb = shift(db, "row", 1)

    a2e, ste, g1e, loe, keep, send = pl.pallas_call(
        functools.partial(edge_kernel, na=na, nj=nj),
        in_specs=[SMEM] + [VMEM] * 8,
        out_specs=[ANY] * 4 + [VMEM] * 2,
        out_shape=[
            hbm((2, 2, m2, C), BF16),
            hbm((2, 2, m0, C), F32),
            hbm((2, 2, m1, C), BF16),
            hbm((2, 2, m0, C), BF16),
            sds((9, C, C), F32),
            sds((9, C, C), BF16),
        ],
        scratch_shapes=[
            vm((2, 2, m2, C), BF16),
            vm((2, 2, m0, C), F32),
            vm((2, 2, m1, C), BF16),
            vm((2, 2, m0, C), BF16),
            vm((2, w, C), BF16),
            vm((2, 2, m1, C), F32),
            vm((w, C), F32),
            vm((2, 3 * C, 3 * C), F32),
            vm((2, 9, C, C), F32),
            pltpu.SemaphoreType.DMA((4,)),
        ],
        compiler_params=params(20),
        cost_estimate=cost(0, 1 << 20),
    )(meta, *in_vmem(fx, gx, a1), upa, dna, *in_vmem(w_one, w_two_back, acc))

    out, fg = pl.pallas_call(
        functools.partial(middle_kernel, na=na, nj=nj),
        in_specs=[SMEM] + [VMEM] * 2 + [ANY] * 7,
        out_specs=[ANY] * 2,
        out_shape=[hbm(features.shape, BF16)] * 2,
        scratch_shapes=[
            vm((ni, m0, C), BF16),
            vm((na, m2, C), BF16),
            vm((ni, m0, C), F32),
            vm((na, m1, C), BF16),
            vm((ni, m0, C), BF16),
            vm((w, C), F32),
            vm((4 * ni, cols, C), BF16),
            vm((4 * ni, cols, C), BF16),
            pltpu.SemaphoreType.DMA((4 + 5 * (ni // 4),)),
            pltpu.SemaphoreType.DMA((2,)),
        ],
        compiler_params=params(28),
        cost_estimate=cost(20 * conv_flops, 24 << 20),
    )(meta, *in_vmem(w_two, w_one_back), *in_hbm(fxo, a2, a2e, st, g1, g1e, lo))

    received = lax.ppermute(send, "col", inner)
    axes = ("row", "col")
    groups = [
        [r * n + c for r in range(lax.axis_size("row")) for c in range(side, n, 2)] for side in range(2)
    ]
    keep = pl.pallas_call(
        hold_kernel,
        in_specs=[ANY],
        out_specs=ANY,
        out_shape=sds((9, C, C), F32),
        input_output_aliases={0: 0},
        compiler_params=params(10),
        cost_estimate=cost(20 * conv_flops, 1 << 20),
    )(keep)
    share = pl.pallas_call(
        add_kernel,
        in_specs=[VMEM] * 2,
        out_specs=VMEM,
        out_shape=sds((9, C, C), BF16),
        compiler_params=params(10),
        cost_estimate=cost(0, 1 << 20),
    )(keep, received).reshape(len(groups[0]), -1, C)
    shares = lax.all_to_all(share, axes, 0, 0, axis_index_groups=groups, tiled=True)
    spread = pl.pallas_call(
        sum_kernel,
        in_specs=[SMEM, VMEM, ANY],
        out_specs=VMEM,
        out_shape=sds(shares.shape, BF16),
        compiler_params=params(10),
        cost_estimate=cost(0, 2 << 20),
    )(meta, shares, *in_hbm(out))
    mine = lax.all_to_all(spread, axes, 0, 0, axis_index_groups=groups, tiled=True).reshape(9, C, C)
    out, fg = pl.pallas_call(
        functools.partial(last_kernel, na=na, nj=nj),
        in_specs=[SMEM, VMEM] + [ANY] * 3 + [VMEM] * 6 + [ANY] * 10,
        out_specs=[ANY] * 2,
        out_shape=[hbm(features.shape, BF16)] * 2,
        scratch_shapes=[
            vm((2, 2, m0, C), BF16),
            vm((4, w, C), BF16),
            vm((2, w, C), BF16),
            vm((2, 6, m2, C), BF16),
            vm((2, 3, m1, C), BF16),
            vm((2, 2, m0, C), F32),
            vm((2, 2, m0, C), BF16),
            vm((6, w, C), BF16),
            vm((4, m2, C), BF16),
            vm((2, m1, C), F32),
            vm((2, m1, C), BF16),
            vm((2, 8, cols, C), BF16),
            vm((2, 8, cols, C), BF16),
            vm((12 * C, 2 * C), BF16),
            vm((12 * C, 2 * C), BF16),
            pltpu.SemaphoreType.DMA((24,)),
        ],
        input_output_aliases={19: 0, 20: 1},
        compiler_params=params(24),
        cost_estimate=cost(20 * conv_flops, 24 << 20),
    )(
        meta, cm, *in_hbm(fxo, gxo, a1o), upa, dna, upb, dnb, *in_vmem(w_two, w_one_back),
        *in_hbm(w_one_far, w_two_back_far, a2, a2e, g1, g1e, ste, loe, out, fg),
    )
    mine = pl.pallas_call(
        after_kernel,
        in_specs=[VMEM, ANY],
        out_specs=VMEM,
        out_shape=sds((9, C, C), BF16),
        compiler_params=params(10),
        cost_estimate=cost(0, 1 << 20),
    )(mine, *in_hbm(out))
    other = lax.ppermute(mine, "col", inner)
    kernel_gradient = pl.pallas_call(
        join_kernel,
        in_specs=[SMEM, VMEM, VMEM],
        out_specs=VMEM,
        out_shape=sds((2, 9, C, C), F32),
        compiler_params=params(10),
        cost_estimate=cost(0, 2 << 20),
    )(meta, mine, other).reshape(kernels.shape)

    return out, fg, kernel_gradient


def solution(mesh):
    spec = P("row", "col", None)
    return jax.shard_map(
        body, mesh=mesh, in_specs=(spec, P(), P(), spec), out_specs=(spec, spec, P()), check_vma=False
    )
```

```python
import functools

import jax
import jax.numpy as jnp
from jax import lax
from jax.experimental import pallas as pl
from jax.experimental.pallas import tpu as pltpu
from jax.sharding import PartitionSpec as P

H = 3
C = 128
F32 = jnp.float32
BF16 = jnp.bfloat16
ANY = pl.BlockSpec(memory_space=pl.ANY)
VMEM = pl.BlockSpec(memory_space=pltpu.VMEM)
SMEM = pl.BlockSpec(memory_space=pltpu.SMEM)


def params(mib):
    return pltpu.CompilerParams(vmem_limit_bytes=mib << 20)


def cost(flops, nbytes):
    return pl.CostEstimate(flops=int(flops), bytes_accessed=int(nbytes), transcendentals=0)


def to_blocks(rows):
    cols = rows[0].shape[0]
    v = [r.reshape(cols // 8, 8, C) for r in rows]
    low = lax.broadcasted_iota(jnp.int32, v[0].shape, 1) < 4

    def swap(a, b):
        return jnp.where(low, a, pltpu.roll(b, 4, 1)), jnp.where(low, pltpu.roll(a, 4, 1), b)

    a, b = swap(v[0], v[1])
    c, d = swap(v[2], v[3])
    y = jnp.stack([jnp.concatenate([a, c], axis=1), jnp.concatenate([b, d], axis=1)], axis=1)
    return y.reshape(4 * cols, C)


def from_blocks(y):
    cols = y.shape[0] // 4
    y = y.reshape(cols // 8, 2, 2, 8, C)
    a, b, c, d = y[:, 0, 0], y[:, 1, 0], y[:, 0, 1], y[:, 1, 1]
    low = lax.broadcasted_iota(jnp.int32, a.shape, 1) < 4

    def swap(a, b):
        return jnp.where(low, a, pltpu.roll(b, 4, 1)), jnp.where(low, pltpu.roll(a, 4, 1), b)

    r0, r1 = swap(a, b)
    r2, r3 = swap(c, d)
    return [r.reshape(cols, C) for r in (r0, r1, r2, r3)]


def column_mask(meta, nj):
    shape = (nj + 2 * H, 16, C)
    j = lax.broadcasted_iota(jnp.int32, shape, 0)
    s = lax.broadcasted_iota(jnp.int32, shape, 1)
    col = meta[1] + 4 * (j - H) + (s & 3)
    return ((col >= 0) & (col < meta[2])).astype(F32).reshape(-1, C)


def live(meta, cm, a, start, size):
    s = lax.broadcasted_iota(jnp.int32, (1, 16, C), 1)
    row = meta[0] + 4 * a + (s >> 2)
    row_mask = ((row >= 0) & (row < meta[2])).astype(F32)
    return (cm[start : start + size, :].reshape(size // 16, 16, C) * row_mask).reshape(size, C)


def elu_parts(v):
    e = jnp.exp(jnp.minimum(v, 0.0))
    return jnp.maximum(v, 0.0) + (e - 1.0), e


def conv_pairs(read, pairs, d, weights):
    parts = []
    for a in pairs:
        cells = []
        for q in range(3):
            cells += [read(a, q), read(a + d, q), read(a - d, q), read(a + 2 * d, q)]
        parts.append(jnp.concatenate(cells, axis=1))
    left = jnp.concatenate(parts, axis=0) if len(parts) > 1 else parts[0]
    return jnp.dot(left, weights, preferred_element_type=F32)


def outer(left, right):
    return lax.dot_general(left, right, (((0,), (0,)), ((), ())), preferred_element_type=F32)


def gather(total, lefts, rights, inside, reach):
    runs = {}
    for b in range(min(inside) - reach, max(inside) + reach + 1):
        taps = tuple(p for p in range(3) if b - reach * (p - 1) in inside)
        if taps:
            runs.setdefault(taps, []).append(b)
    for taps, rows in runs.items():
        left = [jnp.concatenate([lefts(b - reach * (p - 1)) for p in taps], axis=1) for b in rows]
        right = [jnp.concatenate([rights(b, q) for q in range(3)], axis=1) for b in rows]
        product = outer(jnp.concatenate(left, axis=0), jnp.concatenate(right, axis=0))
        for i, p in enumerate(taps):
            total[C * p : C * (p + 1)] += product[C * i : C * (i + 1)]


def pack_kernel(k_ref, conv_ref, back_ref, *, conv_layer, back_layer):
    zero = jnp.zeros((C, C), BF16)

    def conv_tap(p, q):
        return k_ref[conv_layer, p, q]

    def back_tap(p, q):
        return k_ref[back_layer, 2 - p, 2 - q].T

    for tap, w_ref in ((conv_tap, conv_ref), (back_tap, back_ref)):
        for q in range(3):
            t0, t1, t2 = tap(0, q), tap(1, q), tap(2, q)
            o = 4 * C * q
            blocks = ((t1, t0), (t2, t1), (t0, zero), (zero, t2))
            for i, (x, y) in enumerate(blocks):
                w_ref[o + C * i : o + C * (i + 1), :C] = x
                w_ref[o + C * i : o + C * (i + 1), C:] = y


def copier(sem, jobs):
    def go(src, dst):
        c = pltpu.make_async_copy(src, dst, sem.at[len(jobs)])
        c.start()
        jobs.append(c)

    return go


def columns_kernel(meta, f, g, near, far, raw, sem, *, cols, na):
    last = cols - 16
    jobs = []
    go = copier(sem, jobs)
    for i in range(2):
        start = pl.multiple_of((meta[3] if i == 0 else 1 - meta[3]) * last, 16)
        for n, x in enumerate((f, g)):
            go(x.at[:, pl.ds(start, 16)], raw.at[i, n])
    for c in jobs:
        c.wait()
    for i, out in enumerate((far, near)):
        right = meta[3] == 1 - i
        for n in range(2):
            for k in range(na):
                v = to_blocks([raw[i, n, 4 * k + t].astype(F32) for t in range(4)])
                out[n, k] = jnp.where(right, v[16 * (4 - H) :], v[: 16 * H]).astype(BF16)


def layout_kernel(meta, fi, gi, fx, gx, ax, f, g, sem, *, nj, na):
    m0 = 16 * nj
    jobs = []
    go = copier(sem, jobs)
    group = na // 4
    for t in range(4):
        rows = pl.ds(4 * group * t, 4 * group)
        go(fi.at[rows], f.at[rows])
        go(gi.at[rows], g.at[rows])
    shape = (nj, 16, C)
    s = lax.broadcasted_iota(jnp.int32, shape, 1)
    j = lax.broadcasted_iota(jnp.int32, shape, 0)
    cm = (meta[1] + 4 * j + (s & 3) < meta[2]).astype(F32)
    s1 = lax.broadcasted_iota(jnp.int32, (1, 16, C), 1)

    def blocks(ref, k):
        return to_blocks([ref[4 * k + t].astype(F32) for t in range(4)])

    for t in range(4):
        jobs[2 * t].wait()
        jobs[2 * t + 1].wait()
        for k in range(group * t, group * (t + 1)):
            mask = (cm * (meta[0] + 4 * k + (s1 >> 2) < meta[2]).astype(F32)).reshape(m0, C)
            v = blocks(f, k)
            fx[k] = v.astype(BF16)
            ax[k] = (elu_parts(v)[0] * mask).astype(BF16)
            gx[k] = (blocks(g, k) * mask).astype(BF16)


def halo_kernel(meta, ev_ref, od_ref, fo, go_ref, ao, _w, _cm, fx, gx, ax, ua, da, ub, db, sem, *, nj, na):
    m0 = 16 * nj
    odd = meta[3] == 1
    shape = (2 * H, 16, C)
    s = lax.broadcasted_iota(jnp.int32, shape, 1)
    j = lax.broadcasted_iota(jnp.int32, shape, 0) - H
    col = meta[1] + 4 * jnp.where(j < 0, j, j + nj) + (s & 3)
    cm = ((col >= 0) & (col < meta[2])).astype(F32)
    s1 = lax.broadcasted_iota(jnp.int32, (1, 16, C), 1)

    def halos(n, k):
        ev, od = ev_ref[n, k].astype(F32), od_ref[n, k].astype(F32)
        return jnp.concatenate([jnp.where(odd, ev, od), jnp.where(odd, od, ev)], axis=0)

    def extend(k):
        mask = (cm * (meta[0] + 4 * k + (s1 >> 2) < meta[2]).astype(F32)).reshape(2 * H * 16, C)
        v = halos(0, k)
        f, a = v.astype(BF16), (elu_parts(v)[0] * mask).astype(BF16)
        g = (halos(1, k) * mask).astype(BF16)
        for v, own, ref in ((f, fo, fx), (g, go_ref, gx), (a, ao, ax)):
            ref[k, : 16 * H] = v[: 16 * H]
            ref[k, 16 * H : 16 * H + m0] = own[k]
            ref[k, 16 * H + m0 :] = v[16 * H :]

    ends = [0, 1, 2, na - 3, na - 2, na - 1]
    for k in ends:
        extend(k)
    jobs = []
    go = copier(sem, jobs)
    go(fx.at[pl.ds(1, 2)], ub.at[pl.ds(0, 2)])
    go(gx.at[pl.ds(2, 1)], ub.at[pl.ds(2, 1)])
    go(fx.at[pl.ds(na - 3, 2)], db.at[pl.ds(0, 2)])
    go(gx.at[pl.ds(na - 3, 1)], db.at[pl.ds(2, 1)])
    ua[0], ua[1], ua[2] = fx[0], gx[0], gx[1]
    da[0], da[1], da[2] = fx[na - 1], gx[na - 2], gx[na - 1]
    for k in range(3, na - 3):
        extend(k)
    for c in jobs:
        c.wait()


def inner_kernel(
    meta, fx, gx, a1, wc, wb, wc2, wb1, _ub, _db, acc_o, wco, wbo, fxo, gxo, a1o, a2o, so, g1o, lo, _ubo, _dbo, o, fg,
    a2, st, g1, rest, es, cm, ot, ft, sem, *, na, nj,
):
    m0, m1, m2, w = 16 * nj, 16 * (nj + 2), 16 * (nj + 4), 16 * (nj + 6)
    ni = na - 4
    out = []
    send = copier(sem, out)
    send(wc, wco)
    send(wb, wbo)
    send(fx.at[:, pl.ds(16 * H, m0)], fxo)
    for i, row in enumerate((1, 3, na - 4, na - 2)):
        send(gx.at[pl.ds(row, 1)], gxo.at[pl.ds(i, 1)])
    cm[...] = column_mask(meta, nj)

    for t in range(ni // 4):
        r = 2 + 4 * t
        acc = conv_pairs(lambda row, q: a1[row, 16 * q : 16 * q + m2, :], [r, r + 2], 1, wc[...])
        for k in range(2):
            for b in range(2):
                row = r + 2 * k + b
                v = fx[row, 16 : 16 + m2, :].astype(F32) + acc[k * m2 : (k + 1) * m2, b * C : (b + 1) * C]
                act, e = elu_parts(v)
                a2[row + 2] = (act * live(meta, cm, row, 16, m2)).astype(BF16)
                es[row - 2] = e[16 : 16 + m1]
                st[row - 2] = v[32 : 32 + m0]
        acc = conv_pairs(lambda row, q: gx[row, 32 * q : 32 * q + m1, :], [r, r + 1], 2, wb[...])
        for k in range(2):
            for b in range(2):
                row = r + k + 2 * b
                back = acc[k * m1 : (k + 1) * m1, b * C : (b + 1) * C]
                full = gx[row, 32 : 32 + m1, :].astype(F32) + live(meta, cm, row, 32, m1) * es[row - 2] * back
                rounded = full.astype(BF16)
                g1[row + 1] = rounded
                rest[row - 2] = (full - rounded.astype(F32))[16 : 16 + m0].astype(BF16)

    send(a2.at[pl.ds(4, ni)], a2o)
    send(st, so)
    send(g1.at[pl.ds(3, ni)], g1o)
    send(rest, lo)
    send(a1.at[pl.ds(0, 1)], a1o.at[pl.ds(0, 1)])
    send(a1.at[pl.ds(na - 1, 1)], a1o.at[pl.ds(1, 1)])
    for i, t in enumerate(middle_quads(na)):
        r = 2 + 4 * t
        acc2 = conv_pairs(lambda row, q: a2[row + 2, 32 * q : 32 * q + m0], [r, r + 1], 2, wc2[...])
        acc1 = conv_pairs(lambda row, q: g1[row + 1, 16 * q : 16 * q + m0], [r, r + 2], 1, wb1[...])
        finish_quad(
            meta, cm, r, acc2, acc1, lambda row: st[row - 2], lambda row: g1[row + 1, 16 : 16 + m0],
            lambda row: rest[row - 2], lambda row: fx[row, 16 * H : 16 * H + m0], ot, ft, 16 * i,
        )
        send(ot.at[pl.ds(16 * i, 16)], o.at[pl.ds(4 * r, 16)])
        send(ft.at[pl.ds(16 * i, 16)], fg.at[pl.ds(4 * r, 16)])
    acc_o[...] = jnp.zeros_like(acc_o)
    inside = range(2, na - 2)
    gather(
        acc_o.at[1], lambda l: a2[l + 2, 32 : 32 + m0], lambda b, q: gx[b, 16 + 32 * q : 16 + 32 * q + m0], inside, 2
    )
    gather(
        acc_o.at[0], lambda l: g1[l + 1, 16 : 16 + m0], lambda b, q: a1[b, 32 + 16 * q : 32 + 16 * q + m0], inside, 1
    )
    for c in out:
        c.wait()


def edge_kernel(
    meta, fx, gx, a1, up, dn, wc, wb, acc_i, a2o, so, g1o, lo, keep, send,
    a2, st, g1, rest, ah, es, cm, total, kg, sem, *, na, nj,
):
    m0, m1, m2, w = 16 * nj, 16 * (nj + 2), 16 * (nj + 4), 16 * (nj + 6)
    cm[...] = column_mask(meta, nj)
    for i, (ref, row) in enumerate(((up, -1), (dn, na))):
        v, _e = elu_parts(ref[0].astype(F32))
        ah[i] = (v * live(meta, cm, row, 0, w)).astype(BF16)

    def act_one(row, start, size):
        part = slice(start, start + size)
        return ah[0, part] if row < 0 else ah[1, part] if row >= na else a1[row, part]

    def grad_two(row, start, size):
        part = slice(start, start + size)
        return up[3 + row, part] if row < 0 else dn[1 + row - na, part] if row >= na else gx[row, part]

    acc = conv_pairs(lambda row, q: act_one(row, 16 * q, m2), [0, na - 2], 1, wc[...])
    for s in range(2):
        for b in range(2):
            row = (na - 2) * s + b
            v = fx[row, 16 : 16 + m2].astype(F32) + acc[s * m2 : (s + 1) * m2, b * C : (b + 1) * C]
            act, e = elu_parts(v)
            a2[s, b] = (act * live(meta, cm, row, 16, m2)).astype(BF16)
            es[s, b] = e[16 : 16 + m1]
            st[s, b] = v[32 : 32 + m0]
    acc = conv_pairs(lambda row, q: grad_two(row, 32 * q, m1), [0, 1, na - 4, na - 3], 2, wb[...])
    for s in range(2):
        for b in range(2):
            row = (na - 2) * s + b
            k = 2 * s + b
            back = acc[k * m1 : (k + 1) * m1, s * C : (s + 1) * C]
            full = gx[row, 32 : 32 + m1].astype(F32) + live(meta, cm, row, 32, m1) * es[s, b] * back
            rounded = full.astype(BF16)
            g1[s, b] = rounded
            rest[s, b] = (full - rounded.astype(F32))[16 : 16 + m0].astype(BF16)
    jobs = []
    go = copier(sem, jobs)
    for src, dst in ((a2, a2o), (st, so), (g1, g1o), (rest, lo)):
        go(src, dst)

    total[...] = acc_i[...]
    inside = (0, 1, na - 2, na - 1)

    def slot(row):
        return (0, row) if row < 2 else (1, row - (na - 2))

    gather(
        total.at[1], lambda l: a2[*slot(l), 32 : 32 + m0], lambda b, q: grad_two(b, 16 + 32 * q, m0), inside, 2
    )
    gather(
        total.at[0], lambda l: g1[*slot(l), 16 : 16 + m0], lambda b, q: act_one(b, 32 + 16 * q, m0), inside, 1
    )
    for p in range(3):
        for q in range(3):
            block = slice(C * p, C * (p + 1)), slice(C * q, C * (q + 1))
            kg[1, 3 * (2 - p) + 2 - q] = total[1, *block]
            kg[0, 3 * p + q] = total[0, *block].T
    mine = meta[3]
    keep[...] = kg[mine]
    send[...] = kg[1 - mine].astype(BF16)
    for c in jobs:
        c.wait()


def finish_state(meta, cm, row, state, product):
    m0 = state.shape[0]
    return from_blocks((state + product) * live(meta, cm, row, 16 * H, m0))


def finish_gradient(meta, cm, row, rounded, rest, feats, product):
    m0 = rest.shape[0]
    slope = jnp.exp(jnp.minimum(feats.astype(F32), 0.0))
    grads = rounded.astype(F32) + rest.astype(F32)
    return from_blocks(grads + live(meta, cm, row, 16 * H, m0) * slope * product)


def middle_quads(na):
    return [t for t in range((na - 4) // 4) if 2 + 4 * t >= 4 and 2 + 4 * t + 5 <= na - 3]


def finish_quad(meta, cm, r, acc2, acc1, state, rounded, rest, feats, ot, ft, at):
    m0 = acc2.shape[0] // 2
    for k in range(2):
        for b in range(2):
            row = r + k + 2 * b
            product = acc2[k * m0 : (k + 1) * m0, b * C : (b + 1) * C]
            for i, x in enumerate(finish_state(meta, cm, row, state(row), product)):
                ot[at + 4 * (row - r) + i] = x.astype(BF16)
            row = r + 2 * k + b
            product = acc1[k * m0 : (k + 1) * m0, b * C : (b + 1) * C]
            parts = finish_gradient(meta, cm, row, rounded(row), rest(row), feats(row), product)
            for i, x in enumerate(parts):
                ft[at + 4 * (row - r) + i] = x.astype(BF16)


def middle_kernel(
    meta, wc2, wb1, fxi, a2i, a2e, si, g1i, g1e, loi, _out, _fg, out, fg,
    fm, a2, st, g1, lo, cm, ot, ft, sem, *, na, nj,
):
    m0 = 16 * nj
    ni = na - 4
    quads = ni // 4
    jobs = []
    go = copier(sem, jobs)

    def fetch(t, src, edge, dst, reach):
        low = 2 if t == 0 else 6 + reach + 4 * (t - 1)
        high = min(6 + reach + 4 * t, na - 2)
        go(src.at[pl.ds(low - 2, high - low)], dst.at[pl.ds(low, high - low)])
        if t == 0:
            go(edge.at[0], dst.at[pl.ds(0, 2)])
        if t == quads - 1:
            go(edge.at[1], dst.at[pl.ds(na - 2, 2)])

    fetch(0, a2i, a2e, a2, 2)
    fetch(0, g1i, g1e, g1, 1)
    for t in range(quads):
        if t > 0:
            fetch(t, a2i, a2e, a2, 2)
            fetch(t, g1i, g1e, g1, 1)
        here = pl.ds(4 * t, 4)
        if t not in middle_quads(na):
            go(si.at[here], st.at[here])
            go(fxi.at[pl.ds(2 + 4 * t, 4)], fm.at[here])
            go(loi.at[here], lo.at[here])
        if t == 0:
            stage_three = len(jobs)
    cm[...] = column_mask(meta, nj)
    loads = len(jobs)
    rest_of = [t for t in range(quads) if t not in middle_quads(na)]

    def arrive(first, last):
        for c in jobs[first:last]:
            c.wait()

    for t in rest_of:
        r = 2 + 4 * t
        if t == 0:
            arrive(0, stage_three)
        elif t == rest_of[1]:
            arrive(stage_three, loads)
        acc2 = conv_pairs(lambda row, q: a2[row, 32 * q : 32 * q + m0], [r, r + 1], 2, wc2[...])
        acc1 = conv_pairs(lambda row, q: g1[row, 16 * q : 16 * q + m0], [r, r + 2], 1, wb1[...])
        finish_quad(
            meta, cm, r, acc2, acc1, lambda row: st[row - 2], lambda row: g1[row, 16 : 16 + m0],
            lambda row: lo[row - 2], lambda row: fm[row - 2], ot, ft, 16 * t,
        )
        here, there = pl.ds(16 * t, 16), pl.ds(16 * t + 8, 16)
        go(ot.at[here], out.at[there])
        go(ft.at[here], fg.at[there])
    arrive(loads, len(jobs))


def mask_kernel(meta, cm, *, nj):
    cm[...] = column_mask(meta, nj)


def last_kernel(
    meta, cm, fxi, gxi, a1i, upa, dna, upb, dnb, wc2, wb1, wci, wbi, a2i, a2e, g1i, g1e, si, loi, _out, _fg, out, fg,
    own, near, a1, a2, g1, st, lo, ah, a2h, es, g1h, ot, ft, wc, wb, sem, *, na, nj,
):
    m0, m1, m2, w = 16 * nj, 16 * (nj + 2), 16 * (nj + 4), 16 * (nj + 6)
    jobs = []
    go = copier(sem, jobs)
    go(a1i, a1)
    go(wci, wc)
    go(gxi, near)
    go(wbi, wb)
    early = len(jobs)
    go(a2e.at[0], a2.at[0, pl.ds(0, 2)])
    go(a2i.at[pl.ds(0, 4)], a2.at[0, pl.ds(2, 4)])
    go(a2i.at[pl.ds(na - 8, 4)], a2.at[1, pl.ds(0, 4)])
    go(a2e.at[1], a2.at[1, pl.ds(4, 2)])
    go(g1e.at[0], g1.at[0, pl.ds(0, 2)])
    go(g1i.at[pl.ds(0, 1)], g1.at[0, pl.ds(2, 1)])
    go(g1i.at[pl.ds(na - 5, 1)], g1.at[1, pl.ds(0, 1)])
    go(g1e.at[1], g1.at[1, pl.ds(1, 2)])
    go(si, st)
    go(loi, lo)
    for s in range(2):
        go(fxi.at[pl.ds((na - 2) * s, 2)], own.at[s])
    feats = {-3: upb.at[0], -2: upb.at[1], -1: upa.at[0], na: dna.at[0], na + 1: dnb.at[0], na + 2: dnb.at[1]}
    grads = {-3: upb.at[2], -1: upa.at[2], na: dna.at[1], na + 2: dnb.at[2]}
    order = list(feats)
    for i, row in enumerate(order):
        v, _e = elu_parts(feats[row][...].astype(F32))
        ah[i] = (v * live(meta, cm, row, 0, w)).astype(BF16)

    def act_one(row, start):
        part = slice(start, start + m2)
        return ah[order.index(row), part] if row in feats else a1[0 if row == 0 else 1, part]

    def grad_two(row, start):
        part = slice(start, start + m1)
        return grads[row][part] if row in grads else near[(1, 3, na - 4, na - 2).index(row), part]

    def act_two(row, start):
        part = slice(start, start + m0)
        if row < 0 or row >= na:
            return a2h[row + 2 if row < 0 else row - na + 2, part]
        return a2[0, row, part] if row < 6 else a2[1, row - (na - 6), part]

    def grad_one(row, start):
        part = slice(start, start + m0)
        if row < 0 or row >= na:
            return g1h[0 if row < 0 else 1, part]
        return g1[0, row, part] if row < 3 else g1[1, row - (na - 3), part]

    for c in jobs[:early]:
        c.wait()
    acc = conv_pairs(lambda row, q: act_one(row, 16 * q), [-2, na], 1, wc[...])
    for s in range(2):
        for b in range(2):
            row = b - 2 if s == 0 else na + b
            v = feats[row][16 : 16 + m2].astype(F32) + acc[s * m2 : (s + 1) * m2, b * C : (b + 1) * C]
            act, e = elu_parts(v)
            a2h[2 * s + b] = (act * live(meta, cm, row, 16, m2)).astype(BF16)
            if b != s:
                es[s] = e[16 : 16 + m1]
    acc = conv_pairs(lambda row, q: grad_two(row, 32 * q), [-1, na - 2], 2, wb[...])
    for s in range(2):
        row = -1 if s == 0 else na
        back = acc[s * m1 : (s + 1) * m1, s * C : (s + 1) * C]
        full = grads[row][32 : 32 + m1].astype(F32) + live(meta, cm, row, 32, m1) * es[s] * back
        g1h[s] = full.astype(BF16)
    for c in jobs[early:]:
        c.wait()
    acc2 = conv_pairs(lambda row, q: act_two(row, 32 * q), [0, 1, na - 4, na - 3], 2, wc2[...])
    acc1 = conv_pairs(lambda row, q: grad_one(row, 16 * q), [0, na - 2], 1, wb1[...])
    for s in range(2):
        for b in range(2):
            row = (na - 2) * s + b
            k = 2 * s + b
            product = acc2[k * m0 : (k + 1) * m0, s * C : (s + 1) * C]
            for i, x in enumerate(finish_state(meta, cm, row, st[s, b], product)):
                ot[s, 4 * b + i] = x.astype(BF16)
            product = acc1[s * m0 : (s + 1) * m0, b * C : (b + 1) * C]
            rounded = g1[s, s + b, 16 : 16 + m0]
            for i, x in enumerate(finish_gradient(meta, cm, row, rounded, lo[s, b], own[s, b], product)):
                ft[s, 4 * b + i] = x.astype(BF16)
    done = len(jobs)
    for s in range(2):
        go(ot.at[s], out.at[pl.ds(4 * (na - 2) * s, 8)])
        go(ft.at[s], fg.at[pl.ds(4 * (na - 2) * s, 8)])
    for c in jobs[done:]:
        c.wait()


def sum_kernel(meta, x_ref, _out, o_ref):
    total = jnp.sum(x_ref[...].astype(F32), axis=0) / meta[2].astype(F32)
    o_ref[...] = jnp.broadcast_to(total.astype(BF16)[None], o_ref.shape)


def add_kernel(x_ref, y_ref, o_ref):
    o_ref[...] = (x_ref[...] + y_ref[...].astype(F32)).astype(BF16)


def hold_kernel(x_ref, o_ref):
    del x_ref, o_ref


def after_kernel(x_ref, _out, o_ref):
    o_ref[...] = x_ref[...]


def join_kernel(meta, mine_ref, other_ref, o_ref):
    mine = meta[3]
    o_ref[mine] = mine_ref[...].astype(F32)
    o_ref[1 - mine] = other_ref[...].astype(F32)


def in_hbm(*arrays):
    return [pltpu.with_memory_space_constraint(x, pltpu.HBM) for x in arrays]


def in_vmem(*arrays):
    return [pltpu.with_memory_space_constraint(x, pltpu.VMEM) for x in arrays]


def shift(x, axis, step):
    n = lax.axis_size(axis)
    return lax.ppermute(x, axis, [(i, i + step) for i in range(n) if 0 <= i + step < n])


def body(features, kernels, length, cotangent):
    rows, cols, _ = features.shape
    na, nj = rows // 4, cols // 4
    m0, m1, m2, w = 16 * nj, 16 * (nj + 2), 16 * (nj + 4), 16 * (nj + 6)
    ni = na - 4
    odd = lax.rem(lax.axis_index("col"), 2)
    meta = jnp.stack([lax.axis_index("row") * rows, lax.axis_index("col") * cols, length[0], odd]).astype(jnp.int32)
    sds = jax.ShapeDtypeStruct

    near, far = pl.pallas_call(
        functools.partial(columns_kernel, cols=cols, na=na),
        in_specs=[SMEM] + [ANY] * 2,
        out_specs=[VMEM] * 2,
        out_shape=[pltpu.VMEM((2, na, 16 * H, C), BF16)] * 2,
        scratch_shapes=[pltpu.VMEM((2, 2, rows, 16, C), BF16), pltpu.SemaphoreType.DMA((4,))],
        compiler_params=params(10),
        cost_estimate=cost(0, 2 << 20),
    )(meta, *in_hbm(features, cotangent))
    n = lax.axis_size("col")
    inner = [(i, i ^ 1) for i in range(n)]
    outer_pairs = [(i, i + 1) for i in range(1, n - 1, 2)]
    od = lax.ppermute(far, "col", outer_pairs + [(j, i) for i, j in outer_pairs])
    ev = lax.ppermute(near, "col", inner)

    def pack(conv_layer, back_layer):
        return pl.pallas_call(
            functools.partial(pack_kernel, conv_layer=conv_layer, back_layer=back_layer),
            in_specs=[VMEM],
            out_specs=[VMEM] * 2,
            out_shape=[pltpu.VMEM((12 * C, 2 * C), BF16)] * 2,
            compiler_params=params(12),
            cost_estimate=cost(0, 8 << 20),
        )(kernels)

    w_one, w_two_back = pack(0, 1)
    w_two, w_one_back = pack(1, 0)
    cm = pl.pallas_call(
        functools.partial(mask_kernel, nj=nj),
        in_specs=[SMEM],
        out_specs=VMEM,
        out_shape=sds((w, C), F32),
        compiler_params=params(8),
        cost_estimate=cost(0, 1 << 20),
    )(meta)
    vm, hbm = pltpu.VMEM, pltpu.HBM
    fx, gx, a1 = pl.pallas_call(
        functools.partial(layout_kernel, nj=nj, na=na),
        in_specs=[SMEM] + [ANY] * 2,
        out_specs=[VMEM] * 3,
        out_shape=[vm((na, m0, C), BF16)] * 3,
        scratch_shapes=[vm(features.shape, BF16), vm(features.shape, BF16), pltpu.SemaphoreType.DMA((8,))],
        compiler_params=params(16),
        cost_estimate=cost(0, 12 << 20),
    )(meta, *in_hbm(features, cotangent))
    fx, gx, a1, ua, da, ub, db = pl.pallas_call(
        functools.partial(halo_kernel, nj=nj, na=na),
        in_specs=[SMEM] + [VMEM] * 5 + [ANY] * 2,
        out_specs=[VMEM] * 5 + [ANY] * 2,
        out_shape=[vm((na, w, C), BF16)] * 3 + [vm((3, w, C), BF16)] * 2 + [hbm((3, w, C), BF16)] * 2,
        scratch_shapes=[pltpu.SemaphoreType.DMA((4,))],
        compiler_params=params(12),
        cost_estimate=cost(0, 4 << 20),
    )(meta, ev, od, *in_vmem(fx, gx, a1), w_two, cm)
    dna = shift(ua, "row", -1)
    upa = shift(da, "row", 1)

    conv_flops = 2 * rows * cols * 9 * C * C
    acc, w_one_far, w_two_back_far, fxo, gxo, a1o, a2, st, g1, lo, ub, db, out, fg = pl.pallas_call(
        functools.partial(inner_kernel, na=na, nj=nj),
        in_specs=[SMEM] + [VMEM] * 7 + [ANY] * 2,
        out_specs=[VMEM] + [ANY] * 13,
        out_shape=[
            vm((2, 3 * C, 3 * C), F32),
            hbm((12 * C, 2 * C), BF16),
            hbm((12 * C, 2 * C), BF16),
            hbm((na, m0, C), BF16),
            hbm((4, w, C), BF16),
            hbm((2, w, C), BF16),
            hbm((ni, m2, C), BF16),
            hbm((ni, m0, C), F32),
            hbm((ni, m1, C), BF16),
            hbm((ni, m0, C), BF16),
            hbm((3, w, C), BF16),
            hbm((3, w, C), BF16),
            hbm(features.shape, BF16),
            hbm(features.shape, BF16),
        ],
        scratch_shapes=[
            vm((na + 4, m2, C), BF16),
            vm((ni, m0, C), F32),
            vm((na + 2, m1, C), BF16),
            vm((ni, m0, C), BF16),
            vm((ni, m1, C), F32),
            vm((w, C), F32),
            vm((16 * max(1, len(middle_quads(na))), cols, C), BF16),
            vm((16 * max(1, len(middle_quads(na))), cols, C), BF16),
            pltpu.SemaphoreType.DMA((13 + 2 * len(middle_quads(na)),)),
        ],
        input_output_aliases={8: 10, 9: 11},
        compiler_params=params(30),
        cost_estimate=cost(0, 1 << 20),
    )(meta, *in_vmem(fx, gx, a1, w_one, w_two_back, w_two, w_one_back), *in_hbm(ub, db))
    dnb = shift(ub, "row", -1)
    upb = shift(db, "row", 1)

    a2e, ste, g1e, loe, keep, send = pl.pallas_call(
        functools.partial(edge_kernel, na=na, nj=nj),
        in_specs=[SMEM] + [VMEM] * 8,
        out_specs=[ANY] * 4 + [VMEM] * 2,
        out_shape=[
            hbm((2, 2, m2, C), BF16),
            hbm((2, 2, m0, C), F32),
            hbm((2, 2, m1, C), BF16),
            hbm((2, 2, m0, C), BF16),
            sds((9, C, C), F32),
            sds((9, C, C), BF16),
        ],
        scratch_shapes=[
            vm((2, 2, m2, C), BF16),
            vm((2, 2, m0, C), F32),
            vm((2, 2, m1, C), BF16),
            vm((2, 2, m0, C), BF16),
            vm((2, w, C), BF16),
            vm((2, 2, m1, C), F32),
            vm((w, C), F32),
            vm((2, 3 * C, 3 * C), F32),
            vm((2, 9, C, C), F32),
            pltpu.SemaphoreType.DMA((4,)),
        ],
        compiler_params=params(20),
        cost_estimate=cost(0, 1 << 20),
    )(meta, *in_vmem(fx, gx, a1), upa, dna, *in_vmem(w_one, w_two_back, acc))

    out, fg = pl.pallas_call(
        functools.partial(middle_kernel, na=na, nj=nj),
        in_specs=[SMEM] + [VMEM] * 2 + [ANY] * 9,
        out_specs=[ANY] * 2,
        out_shape=[hbm(features.shape, BF16)] * 2,
        scratch_shapes=[
            vm((ni, m0, C), BF16),
            vm((na, m2, C), BF16),
            vm((ni, m0, C), F32),
            vm((na, m1, C), BF16),
            vm((ni, m0, C), BF16),
            vm((w, C), F32),
            vm((4 * ni, cols, C), BF16),
            vm((4 * ni, cols, C), BF16),
            pltpu.SemaphoreType.DMA((4 + 7 * (ni // 4),)),
        ],
        input_output_aliases={10: 0, 11: 1},
        compiler_params=params(28),
        cost_estimate=cost(20 * conv_flops, 24 << 20),
    )(meta, *in_vmem(w_two, w_one_back), *in_hbm(fxo, a2, a2e, st, g1, g1e, lo, out, fg))

    received = lax.ppermute(send, "col", inner)
    axes = ("row", "col")
    groups = [
        [r * n + c for r in range(lax.axis_size("row")) for c in range(side, n, 2)] for side in range(2)
    ]
    keep = pl.pallas_call(
        hold_kernel,
        in_specs=[ANY],
        out_specs=ANY,
        out_shape=sds((9, C, C), F32),
        input_output_aliases={0: 0},
        compiler_params=params(10),
        cost_estimate=cost(20 * conv_flops, 1 << 20),
    )(keep)
    share = pl.pallas_call(
        add_kernel,
        in_specs=[VMEM] * 2,
        out_specs=VMEM,
        out_shape=sds((9, C, C), BF16),
        compiler_params=params(10),
        cost_estimate=cost(0, 1 << 20),
    )(keep, received).reshape(len(groups[0]), -1, C)
    shares = lax.all_to_all(share, axes, 0, 0, axis_index_groups=groups, tiled=True)
    spread = pl.pallas_call(
        sum_kernel,
        in_specs=[SMEM, VMEM, ANY],
        out_specs=VMEM,
        out_shape=sds(shares.shape, BF16),
        compiler_params=params(10),
        cost_estimate=cost(0, 2 << 20),
    )(meta, shares, *in_hbm(out))
    mine = lax.all_to_all(spread, axes, 0, 0, axis_index_groups=groups, tiled=True).reshape(9, C, C)
    out, fg = pl.pallas_call(
        functools.partial(last_kernel, na=na, nj=nj),
        in_specs=[SMEM, VMEM] + [ANY] * 3 + [VMEM] * 6 + [ANY] * 10,
        out_specs=[ANY] * 2,
        out_shape=[hbm(features.shape, BF16)] * 2,
        scratch_shapes=[
            vm((2, 2, m0, C), BF16),
            vm((4, w, C), BF16),
            vm((2, w, C), BF16),
            vm((2, 6, m2, C), BF16),
            vm((2, 3, m1, C), BF16),
            vm((2, 2, m0, C), F32),
            vm((2, 2, m0, C), BF16),
            vm((6, w, C), BF16),
            vm((4, m2, C), BF16),
            vm((2, m1, C), F32),
            vm((2, m1, C), BF16),
            vm((2, 8, cols, C), BF16),
            vm((2, 8, cols, C), BF16),
            vm((12 * C, 2 * C), BF16),
            vm((12 * C, 2 * C), BF16),
            pltpu.SemaphoreType.DMA((24,)),
        ],
        input_output_aliases={19: 0, 20: 1},
        compiler_params=params(24),
        cost_estimate=cost(20 * conv_flops, 24 << 20),
    )(
        meta, cm, *in_hbm(fxo, gxo, a1o), upa, dna, upb, dnb, *in_vmem(w_two, w_one_back),
        *in_hbm(w_one_far, w_two_back_far, a2, a2e, g1, g1e, ste, loe, out, fg),
    )
    mine = pl.pallas_call(
        after_kernel,
        in_specs=[VMEM, ANY],
        out_specs=VMEM,
        out_shape=sds((9, C, C), BF16),
        compiler_params=params(10),
        cost_estimate=cost(0, 1 << 20),
    )(mine, *in_hbm(out))
    other = lax.ppermute(mine, "col", inner)
    kernel_gradient = pl.pallas_call(
        join_kernel,
        in_specs=[SMEM, VMEM, VMEM],
        out_specs=VMEM,
        out_shape=sds((2, 9, C, C), F32),
        compiler_params=params(10),
        cost_estimate=cost(0, 2 << 20),
    )(meta, mine, other).reshape(kernels.shape)

    return out, fg, kernel_gradient


def solution(mesh):
    spec = P("row", "col", None)
    return jax.shard_map(
        body, mesh=mesh, in_specs=(spec, P(), P(), spec), out_specs=(spec, spec, P()), check_vma=False
    )
```

```python
import functools

import jax
import jax.numpy as jnp
from jax import lax
from jax.experimental import pallas as pl
from jax.experimental.pallas import tpu as pltpu
from jax.sharding import PartitionSpec as P

H = 3
C = 128
F32 = jnp.float32
BF16 = jnp.bfloat16
ANY = pl.BlockSpec(memory_space=pl.ANY)
VMEM = pl.BlockSpec(memory_space=pltpu.VMEM)
SMEM = pl.BlockSpec(memory_space=pltpu.SMEM)


def params(mib):
    return pltpu.CompilerParams(vmem_limit_bytes=mib << 20)


def cost(flops, nbytes):
    return pl.CostEstimate(flops=int(flops), bytes_accessed=int(nbytes), transcendentals=0)


def to_blocks(rows):
    cols = rows[0].shape[0]
    v = [r.reshape(cols // 8, 8, C) for r in rows]
    low = lax.broadcasted_iota(jnp.int32, v[0].shape, 1) < 4

    def swap(a, b):
        return jnp.where(low, a, pltpu.roll(b, 4, 1)), jnp.where(low, pltpu.roll(a, 4, 1), b)

    a, b = swap(v[0], v[1])
    c, d = swap(v[2], v[3])
    y = jnp.stack([jnp.concatenate([a, c], axis=1), jnp.concatenate([b, d], axis=1)], axis=1)
    return y.reshape(4 * cols, C)


def from_blocks(y):
    cols = y.shape[0] // 4
    y = y.reshape(cols // 8, 2, 2, 8, C)
    a, b, c, d = y[:, 0, 0], y[:, 1, 0], y[:, 0, 1], y[:, 1, 1]
    low = lax.broadcasted_iota(jnp.int32, a.shape, 1) < 4

    def swap(a, b):
        return jnp.where(low, a, pltpu.roll(b, 4, 1)), jnp.where(low, pltpu.roll(a, 4, 1), b)

    r0, r1 = swap(a, b)
    r2, r3 = swap(c, d)
    return [r.reshape(cols, C) for r in (r0, r1, r2, r3)]


def column_mask(meta, nj):
    shape = (nj + 2 * H, 16, C)
    j = lax.broadcasted_iota(jnp.int32, shape, 0)
    s = lax.broadcasted_iota(jnp.int32, shape, 1)
    col = meta[1] + 4 * (j - H) + (s & 3)
    return ((col >= 0) & (col < meta[2])).astype(F32).reshape(-1, C)


def live(meta, cm, a, start, size):
    s = lax.broadcasted_iota(jnp.int32, (1, 16, C), 1)
    row = meta[0] + 4 * a + (s >> 2)
    row_mask = ((row >= 0) & (row < meta[2])).astype(F32)
    return (cm[start : start + size, :].reshape(size // 16, 16, C) * row_mask).reshape(size, C)


def elu_parts(v):
    e = jnp.exp(jnp.minimum(v, 0.0))
    return jnp.maximum(v, 0.0) + (e - 1.0), e


def conv_pairs(read, pairs, d, weights):
    parts = []
    for a in pairs:
        cells = []
        for q in range(3):
            cells += [read(a, q), read(a + d, q), read(a - d, q), read(a + 2 * d, q)]
        parts.append(jnp.concatenate(cells, axis=1))
    left = jnp.concatenate(parts, axis=0) if len(parts) > 1 else parts[0]
    return jnp.dot(left, weights, preferred_element_type=F32)


def outer(left, right):
    return lax.dot_general(left, right, (((0,), (0,)), ((), ())), preferred_element_type=F32)


def gather(total, lefts, rights, inside, reach):
    runs = {}
    for b in range(min(inside) - reach, max(inside) + reach + 1):
        taps = tuple(p for p in range(3) if b - reach * (p - 1) in inside)
        if taps:
            runs.setdefault(taps, []).append(b)
    for taps, rows in runs.items():
        left = [jnp.concatenate([lefts(b - reach * (p - 1)) for p in taps], axis=1) for b in rows]
        right = [jnp.concatenate([rights(b, q) for q in range(3)], axis=1) for b in rows]
        product = outer(jnp.concatenate(left, axis=0), jnp.concatenate(right, axis=0))
        for i, p in enumerate(taps):
            total[C * p : C * (p + 1)] += product[C * i : C * (i + 1)]


def pack_kernel(k_ref, conv_ref, back_ref, *, conv_layer, back_layer):
    zero = jnp.zeros((C, C), BF16)

    def conv_tap(p, q):
        return k_ref[conv_layer, p, q]

    def back_tap(p, q):
        return k_ref[back_layer, 2 - p, 2 - q].T

    for tap, w_ref in ((conv_tap, conv_ref), (back_tap, back_ref)):
        for q in range(3):
            t0, t1, t2 = tap(0, q), tap(1, q), tap(2, q)
            o = 4 * C * q
            blocks = ((t1, t0), (t2, t1), (t0, zero), (zero, t2))
            for i, (x, y) in enumerate(blocks):
                w_ref[o + C * i : o + C * (i + 1), :C] = x
                w_ref[o + C * i : o + C * (i + 1), C:] = y


def copier(sem, jobs):
    def go(src, dst):
        c = pltpu.make_async_copy(src, dst, sem.at[len(jobs)])
        c.start()
        jobs.append(c)

    return go


def columns_kernel(meta, f, g, out, raw, sem, *, cols, na, near):
    right = meta[3] == (0 if near else 1)
    start = pl.multiple_of((1 - meta[3] if near else meta[3]) * (cols - 16), 16)
    jobs = []
    go = copier(sem, jobs)
    for n, x in enumerate((f, g)):
        go(x.at[:, pl.ds(start, 16)], raw.at[n])
    for n in range(2):
        jobs[n].wait()
        for k in range(na):
            v = to_blocks([raw[n, 4 * k + t].astype(F32) for t in range(4)])
            out[n, k] = jnp.where(right, v[16 * (4 - H) :], v[: 16 * H]).astype(BF16)


def layout_kernel(meta, fi, gi, fx, gx, ax, f, g, sem, *, nj, na):
    m0 = 16 * nj
    jobs = []
    go = copier(sem, jobs)
    group = na // 4
    for t in range(4):
        rows = pl.ds(4 * group * t, 4 * group)
        go(fi.at[rows], f.at[rows])
        go(gi.at[rows], g.at[rows])
    shape = (nj, 16, C)
    s = lax.broadcasted_iota(jnp.int32, shape, 1)
    j = lax.broadcasted_iota(jnp.int32, shape, 0)
    cm = (meta[1] + 4 * j + (s & 3) < meta[2]).astype(F32)
    s1 = lax.broadcasted_iota(jnp.int32, (1, 16, C), 1)

    def blocks(ref, k):
        return to_blocks([ref[4 * k + t].astype(F32) for t in range(4)])

    for t in range(4):
        jobs[2 * t].wait()
        jobs[2 * t + 1].wait()
        for k in range(group * t, group * (t + 1)):
            mask = (cm * (meta[0] + 4 * k + (s1 >> 2) < meta[2]).astype(F32)).reshape(m0, C)
            v = blocks(f, k)
            fx[k] = v.astype(BF16)
            ax[k] = (elu_parts(v)[0] * mask).astype(BF16)
            gx[k] = (blocks(g, k) * mask).astype(BF16)


def halo_kernel(meta, ev_ref, od_ref, fo, go_ref, ao, _w, _cm, fx, gx, ax, ua, da, ub, db, sem, *, nj, na):
    m0 = 16 * nj
    odd = meta[3] == 1
    shape = (2 * H, 16, C)
    s = lax.broadcasted_iota(jnp.int32, shape, 1)
    j = lax.broadcasted_iota(jnp.int32, shape, 0) - H
    col = meta[1] + 4 * jnp.where(j < 0, j, j + nj) + (s & 3)
    cm = ((col >= 0) & (col < meta[2])).astype(F32)
    s1 = lax.broadcasted_iota(jnp.int32, (1, 16, C), 1)

    def halos(n, k):
        ev, od = ev_ref[n, k].astype(F32), od_ref[n, k].astype(F32)
        return jnp.concatenate([jnp.where(odd, ev, od), jnp.where(odd, od, ev)], axis=0)

    def extend(k):
        mask = (cm * (meta[0] + 4 * k + (s1 >> 2) < meta[2]).astype(F32)).reshape(2 * H * 16, C)
        v = halos(0, k)
        f, a = v.astype(BF16), (elu_parts(v)[0] * mask).astype(BF16)
        g = (halos(1, k) * mask).astype(BF16)
        for v, own, ref in ((f, fo, fx), (g, go_ref, gx), (a, ao, ax)):
            ref[k, : 16 * H] = v[: 16 * H]
            ref[k, 16 * H : 16 * H + m0] = own[k]
            ref[k, 16 * H + m0 :] = v[16 * H :]

    ends = [0, 1, 2, na - 3, na - 2, na - 1]
    for k in ends:
        extend(k)
    jobs = []
    go = copier(sem, jobs)
    go(fx.at[pl.ds(1, 2)], ub.at[pl.ds(0, 2)])
    go(gx.at[pl.ds(2, 1)], ub.at[pl.ds(2, 1)])
    go(fx.at[pl.ds(na - 3, 2)], db.at[pl.ds(0, 2)])
    go(gx.at[pl.ds(na - 3, 1)], db.at[pl.ds(2, 1)])
    ua[0], ua[1], ua[2] = fx[0], gx[0], gx[1]
    da[0], da[1], da[2] = fx[na - 1], gx[na - 2], gx[na - 1]
    for k in range(3, na - 3):
        extend(k)
    for c in jobs:
        c.wait()


def inner_kernel(
    meta, fx, gx, a1, wc, wb, wc2, wb1, _ub, _db, acc_o, wco, wbo, fxo, gxo, a1o, a2o, so, g1o, lo, _ubo, _dbo, o, fg,
    a2, st, g1, rest, es, cm, ot, ft, sem, *, na, nj,
):
    m0, m1, m2, w = 16 * nj, 16 * (nj + 2), 16 * (nj + 4), 16 * (nj + 6)
    ni = na - 4
    out = []
    send = copier(sem, out)
    send(wc, wco)
    send(wb, wbo)
    send(fx.at[:, pl.ds(16 * H, m0)], fxo)
    for i, row in enumerate((1, 3, na - 4, na - 2)):
        send(gx.at[pl.ds(row, 1)], gxo.at[pl.ds(i, 1)])
    cm[...] = column_mask(meta, nj)

    for t in range(ni // 4):
        r = 2 + 4 * t
        acc = conv_pairs(lambda row, q: a1[row, 16 * q : 16 * q + m2, :], [r, r + 2], 1, wc[...])
        for k in range(2):
            for b in range(2):
                row = r + 2 * k + b
                v = fx[row, 16 : 16 + m2, :].astype(F32) + acc[k * m2 : (k + 1) * m2, b * C : (b + 1) * C]
                act, e = elu_parts(v)
                a2[row + 2] = (act * live(meta, cm, row, 16, m2)).astype(BF16)
                es[row - 2] = e[16 : 16 + m1]
                st[row - 2] = v[32 : 32 + m0]
        acc = conv_pairs(lambda row, q: gx[row, 32 * q : 32 * q + m1, :], [r, r + 1], 2, wb[...])
        for k in range(2):
            for b in range(2):
                row = r + k + 2 * b
                back = acc[k * m1 : (k + 1) * m1, b * C : (b + 1) * C]
                full = gx[row, 32 : 32 + m1, :].astype(F32) + live(meta, cm, row, 32, m1) * es[row - 2] * back
                rounded = full.astype(BF16)
                g1[row + 1] = rounded
                rest[row - 2] = (full - rounded.astype(F32))[16 : 16 + m0].astype(BF16)

    send(a2.at[pl.ds(4, ni)], a2o)
    send(st, so)
    send(g1.at[pl.ds(3, ni)], g1o)
    send(rest, lo)
    send(a1.at[pl.ds(0, 1)], a1o.at[pl.ds(0, 1)])
    send(a1.at[pl.ds(na - 1, 1)], a1o.at[pl.ds(1, 1)])
    for i, t in enumerate(middle_quads(na)):
        r = 2 + 4 * t
        acc2 = conv_pairs(lambda row, q: a2[row + 2, 32 * q : 32 * q + m0], [r, r + 1], 2, wc2[...])
        acc1 = conv_pairs(lambda row, q: g1[row + 1, 16 * q : 16 * q + m0], [r, r + 2], 1, wb1[...])
        finish_quad(
            meta, cm, r, acc2, acc1, lambda row: st[row - 2], lambda row: g1[row + 1, 16 : 16 + m0],
            lambda row: rest[row - 2], lambda row: fx[row, 16 * H : 16 * H + m0], ot, ft, 16 * i,
        )
        send(ot.at[pl.ds(16 * i, 16)], o.at[pl.ds(4 * r, 16)])
        send(ft.at[pl.ds(16 * i, 16)], fg.at[pl.ds(4 * r, 16)])
    acc_o[...] = jnp.zeros_like(acc_o)
    inside = range(2, na - 2)
    gather(
        acc_o.at[1], lambda l: a2[l + 2, 32 : 32 + m0], lambda b, q: gx[b, 16 + 32 * q : 16 + 32 * q + m0], inside, 2
    )
    gather(
        acc_o.at[0], lambda l: g1[l + 1, 16 : 16 + m0], lambda b, q: a1[b, 32 + 16 * q : 32 + 16 * q + m0], inside, 1
    )
    for c in out:
        c.wait()


def edge_kernel(
    meta, fx, gx, a1, up, dn, wc, wb, acc_i, a2o, so, g1o, lo, keep, send,
    a2, st, g1, rest, ah, es, cm, total, kg, sem, *, na, nj,
):
    m0, m1, m2, w = 16 * nj, 16 * (nj + 2), 16 * (nj + 4), 16 * (nj + 6)
    cm[...] = column_mask(meta, nj)
    for i, (ref, row) in enumerate(((up, -1), (dn, na))):
        v, _e = elu_parts(ref[0].astype(F32))
        ah[i] = (v * live(meta, cm, row, 0, w)).astype(BF16)

    def act_one(row, start, size):
        part = slice(start, start + size)
        return ah[0, part] if row < 0 else ah[1, part] if row >= na else a1[row, part]

    def grad_two(row, start, size):
        part = slice(start, start + size)
        return up[3 + row, part] if row < 0 else dn[1 + row - na, part] if row >= na else gx[row, part]

    acc = conv_pairs(lambda row, q: act_one(row, 16 * q, m2), [0, na - 2], 1, wc[...])
    for s in range(2):
        for b in range(2):
            row = (na - 2) * s + b
            v = fx[row, 16 : 16 + m2].astype(F32) + acc[s * m2 : (s + 1) * m2, b * C : (b + 1) * C]
            act, e = elu_parts(v)
            a2[s, b] = (act * live(meta, cm, row, 16, m2)).astype(BF16)
            es[s, b] = e[16 : 16 + m1]
            st[s, b] = v[32 : 32 + m0]
    acc = conv_pairs(lambda row, q: grad_two(row, 32 * q, m1), [0, 1, na - 4, na - 3], 2, wb[...])
    for s in range(2):
        for b in range(2):
            row = (na - 2) * s + b
            k = 2 * s + b
            back = acc[k * m1 : (k + 1) * m1, s * C : (s + 1) * C]
            full = gx[row, 32 : 32 + m1].astype(F32) + live(meta, cm, row, 32, m1) * es[s, b] * back
            rounded = full.astype(BF16)
            g1[s, b] = rounded
            rest[s, b] = (full - rounded.astype(F32))[16 : 16 + m0].astype(BF16)
    jobs = []
    go = copier(sem, jobs)
    for src, dst in ((a2, a2o), (st, so), (g1, g1o), (rest, lo)):
        go(src, dst)

    total[...] = acc_i[...]
    inside = (0, 1, na - 2, na - 1)

    def slot(row):
        return (0, row) if row < 2 else (1, row - (na - 2))

    gather(
        total.at[1], lambda l: a2[*slot(l), 32 : 32 + m0], lambda b, q: grad_two(b, 16 + 32 * q, m0), inside, 2
    )
    gather(
        total.at[0], lambda l: g1[*slot(l), 16 : 16 + m0], lambda b, q: act_one(b, 32 + 16 * q, m0), inside, 1
    )
    for p in range(3):
        for q in range(3):
            block = slice(C * p, C * (p + 1)), slice(C * q, C * (q + 1))
            kg[1, 3 * (2 - p) + 2 - q] = total[1, *block]
            kg[0, 3 * p + q] = total[0, *block].T
    mine = meta[3]
    keep[...] = kg[mine]
    send[...] = kg[1 - mine].astype(BF16)
    for c in jobs:
        c.wait()


def finish_state(meta, cm, row, state, product):
    m0 = state.shape[0]
    return from_blocks((state + product) * live(meta, cm, row, 16 * H, m0))


def finish_gradient(meta, cm, row, rounded, rest, feats, product):
    m0 = rest.shape[0]
    slope = jnp.exp(jnp.minimum(feats.astype(F32), 0.0))
    grads = rounded.astype(F32) + rest.astype(F32)
    return from_blocks(grads + live(meta, cm, row, 16 * H, m0) * slope * product)


def middle_quads(na):
    return [t for t in range((na - 4) // 4) if 2 + 4 * t >= 4 and 2 + 4 * t + 5 <= na - 3]


def finish_quad(meta, cm, r, acc2, acc1, state, rounded, rest, feats, ot, ft, at):
    m0 = acc2.shape[0] // 2
    for k in range(2):
        for b in range(2):
            row = r + k + 2 * b
            product = acc2[k * m0 : (k + 1) * m0, b * C : (b + 1) * C]
            for i, x in enumerate(finish_state(meta, cm, row, state(row), product)):
                ot[at + 4 * (row - r) + i] = x.astype(BF16)
            row = r + 2 * k + b
            product = acc1[k * m0 : (k + 1) * m0, b * C : (b + 1) * C]
            parts = finish_gradient(meta, cm, row, rounded(row), rest(row), feats(row), product)
            for i, x in enumerate(parts):
                ft[at + 4 * (row - r) + i] = x.astype(BF16)


def middle_kernel(
    meta, wc2, wb1, fxi, a2i, a2e, si, g1i, g1e, loi, _out, _fg, out, fg,
    fm, a2, st, g1, lo, cm, ot, ft, sem, *, na, nj,
):
    m0 = 16 * nj
    ni = na - 4
    quads = ni // 4
    jobs = []
    go = copier(sem, jobs)

    def fetch(t, src, edge, dst, reach):
        low = 2 if t == 0 else 6 + reach + 4 * (t - 1)
        high = min(6 + reach + 4 * t, na - 2)
        go(src.at[pl.ds(low - 2, high - low)], dst.at[pl.ds(low, high - low)])
        if t == 0:
            go(edge.at[0], dst.at[pl.ds(0, 2)])
        if t == quads - 1:
            go(edge.at[1], dst.at[pl.ds(na - 2, 2)])

    fetch(0, a2i, a2e, a2, 2)
    fetch(0, g1i, g1e, g1, 1)
    for t in range(quads):
        if t > 0:
            fetch(t, a2i, a2e, a2, 2)
            fetch(t, g1i, g1e, g1, 1)
        here = pl.ds(4 * t, 4)
        if t not in middle_quads(na):
            go(si.at[here], st.at[here])
            go(fxi.at[pl.ds(2 + 4 * t, 4)], fm.at[here])
            go(loi.at[here], lo.at[here])
        if t == 0:
            stage_three = len(jobs)
    cm[...] = column_mask(meta, nj)
    loads = len(jobs)
    rest_of = [t for t in range(quads) if t not in middle_quads(na)]

    def arrive(first, last):
        for c in jobs[first:last]:
            c.wait()

    for t in rest_of:
        r = 2 + 4 * t
        if t == 0:
            arrive(0, stage_three)
        elif t == rest_of[1]:
            arrive(stage_three, loads)
        acc2 = conv_pairs(lambda row, q: a2[row, 32 * q : 32 * q + m0], [r, r + 1], 2, wc2[...])
        acc1 = conv_pairs(lambda row, q: g1[row, 16 * q : 16 * q + m0], [r, r + 2], 1, wb1[...])
        finish_quad(
            meta, cm, r, acc2, acc1, lambda row: st[row - 2], lambda row: g1[row, 16 : 16 + m0],
            lambda row: lo[row - 2], lambda row: fm[row - 2], ot, ft, 16 * t,
        )
        here, there = pl.ds(16 * t, 16), pl.ds(16 * t + 8, 16)
        go(ot.at[here], out.at[there])
        go(ft.at[here], fg.at[there])
    arrive(loads, len(jobs))


def mask_kernel(meta, cm, *, nj):
    cm[...] = column_mask(meta, nj)


def last_kernel(
    meta, cm, fxi, gxi, a1i, upa, dna, upb, dnb, wc2, wb1, wci, wbi, a2i, a2e, g1i, g1e, si, loi, _out, _fg, out, fg,
    own, near, a1, a2, g1, st, lo, ah, a2h, es, g1h, ot, ft, wc, wb, sem, *, na, nj,
):
    m0, m1, m2, w = 16 * nj, 16 * (nj + 2), 16 * (nj + 4), 16 * (nj + 6)
    jobs = []
    go = copier(sem, jobs)
    go(a1i, a1)
    go(wci, wc)
    go(gxi, near)
    go(wbi, wb)
    early = len(jobs)
    go(a2e.at[0], a2.at[0, pl.ds(0, 2)])
    go(a2i.at[pl.ds(0, 4)], a2.at[0, pl.ds(2, 4)])
    go(a2i.at[pl.ds(na - 8, 4)], a2.at[1, pl.ds(0, 4)])
    go(a2e.at[1], a2.at[1, pl.ds(4, 2)])
    go(g1e.at[0], g1.at[0, pl.ds(0, 2)])
    go(g1i.at[pl.ds(0, 1)], g1.at[0, pl.ds(2, 1)])
    go(g1i.at[pl.ds(na - 5, 1)], g1.at[1, pl.ds(0, 1)])
    go(g1e.at[1], g1.at[1, pl.ds(1, 2)])
    go(si, st)
    go(loi, lo)
    for s in range(2):
        go(fxi.at[pl.ds((na - 2) * s, 2)], own.at[s])
    feats = {-3: upb.at[0], -2: upb.at[1], -1: upa.at[0], na: dna.at[0], na + 1: dnb.at[0], na + 2: dnb.at[1]}
    grads = {-3: upb.at[2], -1: upa.at[2], na: dna.at[1], na + 2: dnb.at[2]}
    order = list(feats)
    for i, row in enumerate(order):
        v, _e = elu_parts(feats[row][...].astype(F32))
        ah[i] = (v * live(meta, cm, row, 0, w)).astype(BF16)

    def act_one(row, start):
        part = slice(start, start + m2)
        return ah[order.index(row), part] if row in feats else a1[0 if row == 0 else 1, part]

    def grad_two(row, start):
        part = slice(start, start + m1)
        return grads[row][part] if row in grads else near[(1, 3, na - 4, na - 2).index(row), part]

    def act_two(row, start):
        part = slice(start, start + m0)
        if row < 0 or row >= na:
            return a2h[row + 2 if row < 0 else row - na + 2, part]
        return a2[0, row, part] if row < 6 else a2[1, row - (na - 6), part]

    def grad_one(row, start):
        part = slice(start, start + m0)
        if row < 0 or row >= na:
            return g1h[0 if row < 0 else 1, part]
        return g1[0, row, part] if row < 3 else g1[1, row - (na - 3), part]

    for c in jobs[:early]:
        c.wait()
    acc = conv_pairs(lambda row, q: act_one(row, 16 * q), [-2, na], 1, wc[...])
    for s in range(2):
        for b in range(2):
            row = b - 2 if s == 0 else na + b
            v = feats[row][16 : 16 + m2].astype(F32) + acc[s * m2 : (s + 1) * m2, b * C : (b + 1) * C]
            act, e = elu_parts(v)
            a2h[2 * s + b] = (act * live(meta, cm, row, 16, m2)).astype(BF16)
            if b != s:
                es[s] = e[16 : 16 + m1]
    acc = conv_pairs(lambda row, q: grad_two(row, 32 * q), [-1, na - 2], 2, wb[...])
    for s in range(2):
        row = -1 if s == 0 else na
        back = acc[s * m1 : (s + 1) * m1, s * C : (s + 1) * C]
        full = grads[row][32 : 32 + m1].astype(F32) + live(meta, cm, row, 32, m1) * es[s] * back
        g1h[s] = full.astype(BF16)
    for c in jobs[early:]:
        c.wait()
    acc2 = conv_pairs(lambda row, q: act_two(row, 32 * q), [0, 1, na - 4, na - 3], 2, wc2[...])
    acc1 = conv_pairs(lambda row, q: grad_one(row, 16 * q), [0, na - 2], 1, wb1[...])
    for s in range(2):
        for b in range(2):
            row = (na - 2) * s + b
            k = 2 * s + b
            product = acc2[k * m0 : (k + 1) * m0, s * C : (s + 1) * C]
            for i, x in enumerate(finish_state(meta, cm, row, st[s, b], product)):
                ot[s, 4 * b + i] = x.astype(BF16)
            product = acc1[s * m0 : (s + 1) * m0, b * C : (b + 1) * C]
            rounded = g1[s, s + b, 16 : 16 + m0]
            for i, x in enumerate(finish_gradient(meta, cm, row, rounded, lo[s, b], own[s, b], product)):
                ft[s, 4 * b + i] = x.astype(BF16)
    done = len(jobs)
    for s in range(2):
        go(ot.at[s], out.at[pl.ds(4 * (na - 2) * s, 8)])
        go(ft.at[s], fg.at[pl.ds(4 * (na - 2) * s, 8)])
    for c in jobs[done:]:
        c.wait()


def sum_kernel(meta, x_ref, _out, o_ref):
    total = jnp.sum(x_ref[...].astype(F32), axis=0) / meta[2].astype(F32)
    o_ref[...] = jnp.broadcast_to(total.astype(BF16)[None], o_ref.shape)


def add_kernel(x_ref, y_ref, o_ref):
    o_ref[...] = (x_ref[...] + y_ref[...].astype(F32)).astype(BF16)


def hold_kernel(x_ref, o_ref):
    del x_ref, o_ref


def after_kernel(x_ref, _out, o_ref):
    o_ref[...] = x_ref[...]


def join_kernel(meta, mine_ref, other_ref, o_ref):
    mine = meta[3]
    o_ref[mine] = mine_ref[...].astype(F32)
    o_ref[1 - mine] = other_ref[...].astype(F32)


def in_hbm(*arrays):
    return [pltpu.with_memory_space_constraint(x, pltpu.HBM) for x in arrays]


def in_vmem(*arrays):
    return [pltpu.with_memory_space_constraint(x, pltpu.VMEM) for x in arrays]


def shift(x, axis, step):
    n = lax.axis_size(axis)
    return lax.ppermute(x, axis, [(i, i + step) for i in range(n) if 0 <= i + step < n])


def body(features, kernels, length, cotangent):
    rows, cols, _ = features.shape
    na, nj = rows // 4, cols // 4
    m0, m1, m2, w = 16 * nj, 16 * (nj + 2), 16 * (nj + 4), 16 * (nj + 6)
    ni = na - 4
    odd = lax.rem(lax.axis_index("col"), 2)
    meta = jnp.stack([lax.axis_index("row") * rows, lax.axis_index("col") * cols, length[0], odd]).astype(jnp.int32)
    sds = jax.ShapeDtypeStruct

    def columns(near):
        return pl.pallas_call(
            functools.partial(columns_kernel, cols=cols, na=na, near=near),
            in_specs=[SMEM] + [ANY] * 2,
            out_specs=VMEM,
            out_shape=pltpu.VMEM((2, na, 16 * H, C), BF16),
            scratch_shapes=[pltpu.VMEM((2, rows, 16, C), BF16), pltpu.SemaphoreType.DMA((2,))],
            compiler_params=params(10),
            cost_estimate=cost(0, 2 << 20),
        )(meta, *in_hbm(features, cotangent))

    n = lax.axis_size("col")
    inner = [(i, i ^ 1) for i in range(n)]
    outer_pairs = [(i, i + 1) for i in range(1, n - 1, 2)]
    od = lax.ppermute(columns(False), "col", outer_pairs + [(j, i) for i, j in outer_pairs])
    ev = lax.ppermute(columns(True), "col", inner)

    def pack(conv_layer, back_layer):
        return pl.pallas_call(
            functools.partial(pack_kernel, conv_layer=conv_layer, back_layer=back_layer),
            in_specs=[VMEM],
            out_specs=[VMEM] * 2,
            out_shape=[pltpu.VMEM((12 * C, 2 * C), BF16)] * 2,
            compiler_params=params(12),
            cost_estimate=cost(0, 8 << 20),
        )(kernels)

    w_one, w_two_back = pack(0, 1)
    w_two, w_one_back = pack(1, 0)
    cm = pl.pallas_call(
        functools.partial(mask_kernel, nj=nj),
        in_specs=[SMEM],
        out_specs=VMEM,
        out_shape=sds((w, C), F32),
        compiler_params=params(8),
        cost_estimate=cost(0, 1 << 20),
    )(meta)
    vm, hbm = pltpu.VMEM, pltpu.HBM
    fx, gx, a1 = pl.pallas_call(
        functools.partial(layout_kernel, nj=nj, na=na),
        in_specs=[SMEM] + [ANY] * 2,
        out_specs=[VMEM] * 3,
        out_shape=[vm((na, m0, C), BF16)] * 3,
        scratch_shapes=[vm(features.shape, BF16), vm(features.shape, BF16), pltpu.SemaphoreType.DMA((8,))],
        compiler_params=params(16),
        cost_estimate=cost(0, 12 << 20),
    )(meta, *in_hbm(features, cotangent))
    fx, gx, a1, ua, da, ub, db = pl.pallas_call(
        functools.partial(halo_kernel, nj=nj, na=na),
        in_specs=[SMEM] + [VMEM] * 5 + [ANY] * 2,
        out_specs=[VMEM] * 5 + [ANY] * 2,
        out_shape=[vm((na, w, C), BF16)] * 3 + [vm((3, w, C), BF16)] * 2 + [hbm((3, w, C), BF16)] * 2,
        scratch_shapes=[pltpu.SemaphoreType.DMA((4,))],
        compiler_params=params(12),
        cost_estimate=cost(0, 4 << 20),
    )(meta, ev, od, *in_vmem(fx, gx, a1), w_two, cm)
    dna = shift(ua, "row", -1)
    upa = shift(da, "row", 1)

    conv_flops = 2 * rows * cols * 9 * C * C
    acc, w_one_far, w_two_back_far, fxo, gxo, a1o, a2, st, g1, lo, ub, db, out, fg = pl.pallas_call(
        functools.partial(inner_kernel, na=na, nj=nj),
        in_specs=[SMEM] + [VMEM] * 7 + [ANY] * 2,
        out_specs=[VMEM] + [ANY] * 13,
        out_shape=[
            vm((2, 3 * C, 3 * C), F32),
            hbm((12 * C, 2 * C), BF16),
            hbm((12 * C, 2 * C), BF16),
            hbm((na, m0, C), BF16),
            hbm((4, w, C), BF16),
            hbm((2, w, C), BF16),
            hbm((ni, m2, C), BF16),
            hbm((ni, m0, C), F32),
            hbm((ni, m1, C), BF16),
            hbm((ni, m0, C), BF16),
            hbm((3, w, C), BF16),
            hbm((3, w, C), BF16),
            hbm(features.shape, BF16),
            hbm(features.shape, BF16),
        ],
        scratch_shapes=[
            vm((na + 4, m2, C), BF16),
            vm((ni, m0, C), F32),
            vm((na + 2, m1, C), BF16),
            vm((ni, m0, C), BF16),
            vm((ni, m1, C), F32),
            vm((w, C), F32),
            vm((16 * max(1, len(middle_quads(na))), cols, C), BF16),
            vm((16 * max(1, len(middle_quads(na))), cols, C), BF16),
            pltpu.SemaphoreType.DMA((13 + 2 * len(middle_quads(na)),)),
        ],
        input_output_aliases={8: 10, 9: 11},
        compiler_params=params(30),
        cost_estimate=cost(0, 1 << 20),
    )(meta, *in_vmem(fx, gx, a1, w_one, w_two_back, w_two, w_one_back), *in_hbm(ub, db))
    dnb = shift(ub, "row", -1)
    upb = shift(db, "row", 1)

    a2e, ste, g1e, loe, keep, send = pl.pallas_call(
        functools.partial(edge_kernel, na=na, nj=nj),
        in_specs=[SMEM] + [VMEM] * 8,
        out_specs=[ANY] * 4 + [VMEM] * 2,
        out_shape=[
            hbm((2, 2, m2, C), BF16),
            hbm((2, 2, m0, C), F32),
            hbm((2, 2, m1, C), BF16),
            hbm((2, 2, m0, C), BF16),
            sds((9, C, C), F32),
            sds((9, C, C), BF16),
        ],
        scratch_shapes=[
            vm((2, 2, m2, C), BF16),
            vm((2, 2, m0, C), F32),
            vm((2, 2, m1, C), BF16),
            vm((2, 2, m0, C), BF16),
            vm((2, w, C), BF16),
            vm((2, 2, m1, C), F32),
            vm((w, C), F32),
            vm((2, 3 * C, 3 * C), F32),
            vm((2, 9, C, C), F32),
            pltpu.SemaphoreType.DMA((4,)),
        ],
        compiler_params=params(20),
        cost_estimate=cost(0, 1 << 20),
    )(meta, *in_vmem(fx, gx, a1), upa, dna, *in_vmem(w_one, w_two_back, acc))

    out, fg = pl.pallas_call(
        functools.partial(middle_kernel, na=na, nj=nj),
        in_specs=[SMEM] + [VMEM] * 2 + [ANY] * 9,
        out_specs=[ANY] * 2,
        out_shape=[hbm(features.shape, BF16)] * 2,
        scratch_shapes=[
            vm((ni, m0, C), BF16),
            vm((na, m2, C), BF16),
            vm((ni, m0, C), F32),
            vm((na, m1, C), BF16),
            vm((ni, m0, C), BF16),
            vm((w, C), F32),
            vm((4 * ni, cols, C), BF16),
            vm((4 * ni, cols, C), BF16),
            pltpu.SemaphoreType.DMA((4 + 7 * (ni // 4),)),
        ],
        input_output_aliases={10: 0, 11: 1},
        compiler_params=params(28),
        cost_estimate=cost(20 * conv_flops, 24 << 20),
    )(meta, *in_vmem(w_two, w_one_back), *in_hbm(fxo, a2, a2e, st, g1, g1e, lo, out, fg))

    received = lax.ppermute(send, "col", inner)
    axes = ("row", "col")
    groups = [
        [r * n + c for r in range(lax.axis_size("row")) for c in range(side, n, 2)] for side in range(2)
    ]
    keep = pl.pallas_call(
        hold_kernel,
        in_specs=[ANY],
        out_specs=ANY,
        out_shape=sds((9, C, C), F32),
        input_output_aliases={0: 0},
        compiler_params=params(10),
        cost_estimate=cost(20 * conv_flops, 1 << 20),
    )(keep)
    share = pl.pallas_call(
        add_kernel,
        in_specs=[VMEM] * 2,
        out_specs=VMEM,
        out_shape=sds((9, C, C), BF16),
        compiler_params=params(10),
        cost_estimate=cost(0, 1 << 20),
    )(keep, received).reshape(len(groups[0]), -1, C)
    shares = lax.all_to_all(share, axes, 0, 0, axis_index_groups=groups, tiled=True)
    spread = pl.pallas_call(
        sum_kernel,
        in_specs=[SMEM, VMEM, ANY],
        out_specs=VMEM,
        out_shape=sds(shares.shape, BF16),
        compiler_params=params(10),
        cost_estimate=cost(0, 2 << 20),
    )(meta, shares, *in_hbm(out))
    mine = lax.all_to_all(spread, axes, 0, 0, axis_index_groups=groups, tiled=True).reshape(9, C, C)
    out, fg = pl.pallas_call(
        functools.partial(last_kernel, na=na, nj=nj),
        in_specs=[SMEM, VMEM] + [ANY] * 3 + [VMEM] * 6 + [ANY] * 10,
        out_specs=[ANY] * 2,
        out_shape=[hbm(features.shape, BF16)] * 2,
        scratch_shapes=[
            vm((2, 2, m0, C), BF16),
            vm((4, w, C), BF16),
            vm((2, w, C), BF16),
            vm((2, 6, m2, C), BF16),
            vm((2, 3, m1, C), BF16),
            vm((2, 2, m0, C), F32),
            vm((2, 2, m0, C), BF16),
            vm((6, w, C), BF16),
            vm((4, m2, C), BF16),
            vm((2, m1, C), F32),
            vm((2, m1, C), BF16),
            vm((2, 8, cols, C), BF16),
            vm((2, 8, cols, C), BF16),
            vm((12 * C, 2 * C), BF16),
            vm((12 * C, 2 * C), BF16),
            pltpu.SemaphoreType.DMA((24,)),
        ],
        input_output_aliases={19: 0, 20: 1},
        compiler_params=params(24),
        cost_estimate=cost(20 * conv_flops, 24 << 20),
    )(
        meta, cm, *in_hbm(fxo, gxo, a1o), upa, dna, upb, dnb, *in_vmem(w_two, w_one_back),
        *in_hbm(w_one_far, w_two_back_far, a2, a2e, g1, g1e, ste, loe, out, fg),
    )
    mine = pl.pallas_call(
        after_kernel,
        in_specs=[VMEM, ANY],
        out_specs=VMEM,
        out_shape=sds((9, C, C), BF16),
        compiler_params=params(10),
        cost_estimate=cost(0, 1 << 20),
    )(mine, *in_hbm(out))
    other = lax.ppermute(mine, "col", inner)
    kernel_gradient = pl.pallas_call(
        join_kernel,
        in_specs=[SMEM, VMEM, VMEM],
        out_specs=VMEM,
        out_shape=sds((2, 9, C, C), F32),
        compiler_params=params(10),
        cost_estimate=cost(0, 2 << 20),
    )(meta, mine, other).reshape(kernels.shape)

    return out, fg, kernel_gradient


def solution(mesh):
    spec = P("row", "col", None)
    return jax.shard_map(
        body, mesh=mesh, in_specs=(spec, P(), P(), spec), out_specs=(spec, spec, P()), check_vma=False
    )
```
